512 devices in a mesh: seq: 64 (over x, y, core), tp: 8 (over z).
Axes of the slice: x: 4, y: 8, z: 8, core: 2. Of those that a mesh axis runs over, the one named last changes fastest.
Arguments:
- queries: bfloat16 [10240, 8192], P('seq', 'tp'), may hold values from -6 to 6
- key_vectors: bfloat16 [10240, 8192], P('seq', 'tp'), may hold values from -6 to 6
- values: bfloat16 [10240, 8192], P('seq', 'tp'), may hold values from -6 to 6
- decay_log: float32 [10240, 64], P('seq', 'tp'), may hold values from -1 to 0, as said below
- norm_gain: float32 [8192], P('tp'), may hold values from 0.1 to 1.9
- grad_out: bfloat16 [10240, 8192], P('seq', 'tp'), may hold values from -6 to 6
Outputs:
- normed: bfloat16 [10240, 8192], P('seq', 'tp')
- grad_query: bfloat16 [10240, 8192], P('seq', 'tp')
- grad_key: bfloat16 [10240, 8192], P('seq', 'tp')
- grad_value: bfloat16 [10240, 8192], P('seq', 'tp')
The draws below stay inside these ranges and needn't reach their ends.
Inputs may be any that keep to these rules, and one draw needn't show every extreme that they name: `decay_log`: every entry is negative.
All inputs are finite; a program needn't handle non-finite values.
Results may differ from the reference program's by a relative error of at most 0.0062.
Values sent between devices are 32-bit elements; how exact they have to be, the bound alone decides.
No kernel may reach another device: no remote copies, remote signals or barrier semaphores. Data moves between devices by JAX's collectives and lax.ppermute only.
A program may use at most 128 MiB of HBM per device.

```python
import math
import jax
import jax.numpy as jnp
from jax import lax

HEAD_COUNT = 64
HEAD = 128
TOK_DEV = 160
TOKEN_COUNT = 10240
FEATURES = 8192
N_SEQ = 64


def draw_decay_log(key, part):
    key = jax.random.fold_in(key, 7)
    random_subkeys = jax.random.split(key, 7)
    fast_share = 0.5
    fast_heads = jax.random.uniform(random_subkeys[0], (HEAD_COUNT,)) < fast_share
    fast_rate = jnp.exp(jax.random.uniform(random_subkeys[1], (HEAD_COUNT,), minval=math.log(1.0 / 50.0), maxval=math.log(1.0 / 25.0)))
    slow_rate = jax.random.uniform(random_subkeys[2], (HEAD_COUNT,), minval=0.1, maxval=0.5) / TOKEN_COUNT
    head_rate = jnp.where(fast_heads, fast_rate, slow_rate)
    block_count = TOKEN_COUNT // TOK_DEV
    block_factor = jnp.exp(jax.random.uniform(random_subkeys[3], (block_count, HEAD_COUNT), minval=math.log(0.6), maxval=math.log(1.5)))
    block_factor = jnp.repeat(block_factor, TOK_DEV, axis=0)
    roughness = jax.random.uniform(random_subkeys[4], (TOKEN_COUNT, HEAD_COUNT), minval=0.5, maxval=1.5)
    final_output = -head_rate[None, :] * block_factor * roughness
    spike_locations = jax.random.randint(random_subkeys[5], (2, HEAD_COUNT), 0, TOKEN_COUNT)
    spike_retained = jax.random.uniform(random_subkeys[6], (2, HEAD_COUNT), minval=0.5, maxval=0.8)
    token_offset = jnp.arange(TOKEN_COUNT)[:, None]
    for spike_index in range(2):
        final_output = final_output + jnp.where(token_offset == spike_locations[spike_index][None, :], jnp.log(spike_retained[spike_index])[None, :], 0.0)
    return final_output.astype(jnp.float32)


def steps_of(key, extent, shards, low, high):
    factor_of, own = 1.0, jax.random.fold_in(key, 6)
    for dim, parts in shards:
        draws = jnp.exp(jax.random.uniform(jax.random.fold_in(own, dim), (parts,), jnp.float32, low / len(shards), high / len(shards)))
        factor_of = factor_of * jnp.repeat(draws, extent[dim] // parts).reshape([-1 if axis == dim else 1 for axis in range(len(extent))])
    return factor_of


def centred(own_key, extent, deviation, most, cuts=(), kind=jnp.bfloat16):
    values = deviation * jax.random.normal(own_key, extent, jnp.float32)
    if cuts:
        values = values * steps_of(own_key, extent, cuts, -0.22, 0.18)
    return jnp.clip(values, -most, most).astype(kind)


def setup_inputs(seed: int = 0) -> dict:
    arg_keys = jax.random.split(jax.random.key(seed), 7)
    return {
        "queries": centred(arg_keys[0], (TOKEN_COUNT, FEATURES), 1.0, 6.0, ((0, 64), (1, 8))),
        "key_vectors": centred(arg_keys[1], (TOKEN_COUNT, FEATURES), 1.0, 6.0, ((0, 64), (1, 8))),
        "values": centred(arg_keys[2], (TOKEN_COUNT, FEATURES), 1.0, 6.0, ((0, 64), (1, 8))),
        "decay_log": draw_decay_log(jax.random.fold_in(arg_keys[6], 71), 0),
        "norm_gain": jnp.clip(1.0 + 0.18 * jax.random.normal(arg_keys[4], (FEATURES,), jnp.float32), 0.1, 1.9),
        "grad_out": centred(arg_keys[5], (TOKEN_COUNT, FEATURES), 1.0, 6.0, ((0, 64), (1, 8))),
    }


EPSILON = 1e-06
HIGH = lax.Precision.HIGHEST

def decay_tables(decay_part):
    inside = jnp.cumsum(decay_part, axis=0)
    totals = inside[-1]
    length = decay_part.shape[0]
    across = inside.T
    spread = across[:, :, None] - across[:, None, :]
    causal = jnp.tril(jnp.ones((length, length), jnp.bool_))[None]
    weights = jnp.where(causal, jnp.exp(jnp.where(causal, spread, 0.0)), 0.0)
    return (inside, totals, weights)

def reference(queries, key_vectors, values, decay_log, norm_gain, grad_out):

    def split_rows(array):
        return array.reshape(N_SEQ, TOK_DEV, HEAD_COUNT, HEAD)
    decay_blocks = decay_log.reshape(N_SEQ, TOK_DEV, HEAD_COUNT)
    total_width = HEAD_COUNT * HEAD

    def forward_step(state, inputs):
        query3, key3, value3, decay_part, grad_part = inputs
        inside, totals, weights = decay_tables(decay_part)
        query_decayed = (query3.astype(jnp.float32) * jnp.exp(inside)[:, :, None]).astype(jnp.bfloat16)
        key_decayed = (key3.astype(jnp.float32) * jnp.exp(totals[None] - inside)[:, :, None]).astype(jnp.bfloat16)
        scores = jnp.einsum('thd,uhd->htu', query3.astype(jnp.float32), key3.astype(jnp.float32), precision=HIGH)
        mixing = (scores * weights).astype(jnp.bfloat16)
        attended = jnp.einsum('htu,uhe->the', mixing.astype(jnp.float32), value3.astype(jnp.float32), precision=HIGH)
        attended = attended + jnp.einsum('thd,hde->the', query_decayed.astype(jnp.float32), state, precision=HIGH)
        flat = attended.reshape(TOK_DEV, total_width)
        inverse = lax.rsqrt(lax.optimization_barrier(jnp.sum(flat * flat, axis=-1)) / total_width + EPSILON)
        normed = (flat * inverse[:, None] * norm_gain[None]).astype(jnp.bfloat16)
        scaled_grad = grad_part.reshape(TOK_DEV, total_width).astype(jnp.float32) * norm_gain[None]
        cross_mean = lax.optimization_barrier(jnp.sum(scaled_grad * flat, axis=-1)) / total_width
        grad_flat = (inverse[:, None] * scaled_grad - flat * (inverse ** 3 * cross_mean)[:, None]).astype(jnp.bfloat16)
        grad3 = grad_flat.reshape(TOK_DEV, HEAD_COUNT, HEAD)
        grad_scores = jnp.einsum('thd,uhd->htu', grad3.astype(jnp.float32), value3.astype(jnp.float32), precision=HIGH)
        grad_mix = (grad_scores * weights).astype(jnp.bfloat16)
        grad_query = jnp.einsum('htu,uhd->thd', grad_mix.astype(jnp.float32), key3.astype(jnp.float32), precision=HIGH)
        grad_query = grad_query + jnp.exp(inside)[:, :, None] * jnp.einsum('the,hde->thd', grad3.astype(jnp.float32), state, precision=HIGH)
        local_state = jnp.einsum('thd,the->hde', key_decayed.astype(jnp.float32), value3.astype(jnp.float32), precision=HIGH)
        new_state = jnp.exp(totals)[:, None, None] * state + local_state
        return (new_state, (normed, grad_query.astype(jnp.bfloat16), grad3))
    zero_state = jnp.zeros((HEAD_COUNT, HEAD, HEAD), jnp.float32)
    forward_inputs = (split_rows(queries), split_rows(key_vectors), split_rows(values), decay_blocks, split_rows(grad_out))
    unused_state, (normed, grad_query, grad_blocks) = lax.scan(forward_step, zero_state, forward_inputs)

    def backward_step(arriving, inputs):
        query3, key3, value3, decay_part, grad3 = inputs
        inside, totals, weights = decay_tables(decay_part)
        query_decayed = (query3.astype(jnp.float32) * jnp.exp(inside)[:, :, None]).astype(jnp.bfloat16)
        key_decayed = (key3.astype(jnp.float32) * jnp.exp(totals[None] - inside)[:, :, None]).astype(jnp.bfloat16)
        scores = jnp.einsum('thd,uhd->htu', query3.astype(jnp.float32), key3.astype(jnp.float32), precision=HIGH)
        mixing = (scores * weights).astype(jnp.bfloat16)
        grad_scores = jnp.einsum('thd,uhd->htu', grad3.astype(jnp.float32), value3.astype(jnp.float32), precision=HIGH)
        grad_mix = (grad_scores * weights).astype(jnp.bfloat16)
        grad_key = jnp.einsum('htu,thd->uhd', grad_mix.astype(jnp.float32), query3.astype(jnp.float32), precision=HIGH)
        grad_key = grad_key + jnp.exp(totals[None] - inside)[:, :, None] * jnp.einsum('uhe,hde->uhd', value3.astype(jnp.float32), arriving, precision=HIGH)
        grad_value = jnp.einsum('htu,the->uhe', mixing.astype(jnp.float32), grad3.astype(jnp.float32), precision=HIGH)
        grad_value = grad_value + jnp.einsum('uhd,hde->uhe', key_decayed.astype(jnp.float32), arriving, precision=HIGH)
        grad_local = jnp.einsum('thd,the->hde', query_decayed.astype(jnp.float32), grad3.astype(jnp.float32), precision=HIGH)
        new_arriving = grad_local + jnp.exp(totals)[:, None, None] * arriving
        return (new_arriving, (grad_key.astype(jnp.bfloat16), grad_value.astype(jnp.bfloat16)))
    backward_inputs = (split_rows(queries), split_rows(key_vectors), split_rows(values), decay_blocks, grad_blocks)
    unused_grad, (grad_key, grad_value) = lax.scan(backward_step, zero_state, backward_inputs, reverse=True)
    shape_out = (TOKEN_COUNT, HEAD_COUNT * HEAD)
    return (normed.reshape(shape_out), grad_query.reshape(shape_out), grad_key.reshape(shape_out), grad_value.reshape(shape_out))
```

```python
import functools

import jax
import jax.numpy as jnp
from jax import lax
from jax.experimental import pallas as pl
from jax.experimental.pallas import tpu as pltpu
from jax.sharding import PartitionSpec as P

HEAD_COUNT = 64
HEAD = 128
EPSILON = 1e-06
HIGH = lax.Precision.HIGHEST
F32 = jnp.float32
BF16 = jnp.bfloat16
VMEM_LIMIT = 48 * 1024 * 1024


def dot_nn(a, b):
    return lax.dot_general(a, b, (((1,), (0,)), ((), ())), preferred_element_type=F32)


def dot_nt(a, b):
    return lax.dot_general(a, b, (((1,), (1,)), ((), ())), preferred_element_type=F32)


def dot_tn(a, b):
    return lax.dot_general(a, b, (((0,), (0,)), ((), ())), preferred_element_type=F32)


def call(kernel, outs, args, flops, bytes_accessed, smem=0):
    specs = [pl.BlockSpec(memory_space=pltpu.SMEM)] * smem
    specs += [pl.BlockSpec(memory_space=pltpu.VMEM)] * (len(args) - smem)
    return pl.pallas_call(
        kernel,
        out_shape=[jax.ShapeDtypeStruct(s, d) for s, d in outs],
        in_specs=specs,
        out_specs=[pl.BlockSpec(memory_space=pltpu.VMEM)] * len(outs),
        compiler_params=pltpu.CompilerParams(vmem_limit_bytes=VMEM_LIMIT),
        cost_estimate=pl.CostEstimate(
            flops=flops, bytes_accessed=bytes_accessed, transcendentals=0
        ),
    )(*args)


def head_cols(h):
    return slice(h * HEAD, (h + 1) * HEAD)


def local_kernel(k_ref, v_ref, decay_ref, pay_ref, inside_ref, across_ref):
    rows, heads = decay_ref.shape
    per_head = pay_ref.shape[0] // heads
    slab = HEAD // per_head
    decay = decay_ref[...]
    first = lax.broadcasted_iota(jnp.int32, (rows, rows), 0)
    second = lax.broadcasted_iota(jnp.int32, (rows, rows), 1)
    inside = lax.dot_general(
        (first >= second).astype(F32), decay, (((1,), (0,)), ((), ())),
        precision=HIGH, preferred_element_type=F32,
    )
    inside_ref[...] = inside
    across_ref[...] = lax.dot_general(
        decay, (first <= second).astype(F32), (((0,), (0,)), ((), ())),
        precision=HIGH, preferred_element_type=F32,
    )
    totals = inside[rows - 1 : rows, :]
    shares = jnp.exp(totals - inside)
    kept = jnp.exp(totals)
    for h in range(heads):
        key_decayed = (k_ref[:, head_cols(h)].astype(F32) * shares[:, h : h + 1]).astype(BF16)
        state = dot_tn(key_decayed, v_ref[:, head_cols(h)])
        here = slice(h * per_head, (h + 1) * per_head)
        pay_ref[here, 0:slab, :] = state.reshape(per_head, slab, HEAD)
        pay_ref[here, slab : slab + 8, :] = jnp.broadcast_to(
            kept[:, h : h + 1].reshape(1, 1, 1), (per_head, 8, HEAD)
        )


def weights_of(inside_ref, across_ref, h):
    rows = inside_ref.shape[0]
    first = lax.broadcasted_iota(jnp.int32, (rows, rows), 0)
    second = lax.broadcasted_iota(jnp.int32, (rows, rows), 1)
    spread = inside_ref[:, h : h + 1] - across_ref[h : h + 1, :]
    return jnp.exp(jnp.where(first >= second, spread, -1e30))


def mixing_kernel(q_ref, k_ref, v_ref, inside_ref, across_ref, mix_ref, near_ref):
    for h in range(inside_ref.shape[1]):
        cols = head_cols(h)
        scores = dot_nt(q_ref[:, cols], k_ref[:, cols])
        mixing = (scores * weights_of(inside_ref, across_ref, h)).astype(BF16)
        mix_ref[h] = mixing
        near_ref[:, cols] = dot_nn(mixing, v_ref[:, cols])


def forward_scan_kernel(core_ref, own_ref, other_ref, out_ref, kept_ref):
    count, slab = out_ref.shape[0], out_ref.shape[1]

    def run(first_ref, second_ref, second_core):
        state = jnp.zeros((slab // 8, 8, HEAD), F32)
        for j in range(count):
            kept0, kept1 = first_ref[j, slab:, :], second_ref[j, slab:, :]
            kept_ref[j, 0:8, :] = kept0
            kept_ref[j, 8:16, :] = kept1
            middle = kept0 * state + first_ref[j, 0:slab, :].reshape(state.shape)
            out_ref[j] = (middle if second_core else state).reshape(slab, HEAD)
            state = kept1 * middle + second_ref[j, 0:slab, :].reshape(state.shape)

    @pl.when(core_ref[0] == 0)
    def _():
        run(own_ref, other_ref, False)

    @pl.when(core_ref[0] == 1)
    def _():
        run(other_ref, own_ref, True)


def reverse_scan_kernel(core_ref, own_ref, other_ref, kept_ref, out_ref):
    count, slab = out_ref.shape[0], out_ref.shape[1]

    def run(first_ref, second_ref, second_core):
        state = jnp.zeros((slab // 8, 8, HEAD), F32)
        for j in reversed(range(count)):
            middle = kept_ref[j, 8:16, :] * state + second_ref[j].reshape(state.shape)
            out_ref[j] = (state if second_core else middle).reshape(slab, HEAD)
            state = kept_ref[j, 0:8, :] * middle + first_ref[j].reshape(state.shape)

    @pl.when(core_ref[0] == 0)
    def _():
        run(own_ref, other_ref, False)

    @pl.when(core_ref[0] == 1)
    def _():
        run(other_ref, own_ref, True)


def attend_kernel(q_ref, near_ref, state_ref, inside_ref, g_ref, gain_ref, att_ref, sums_ref):
    rows, heads = inside_ref.shape
    grown = jnp.exp(inside_ref[...])
    squares = jnp.zeros((rows, HEAD), F32)
    crossed = jnp.zeros((rows, HEAD), F32)
    for h in range(heads):
        cols = head_cols(h)
        query_decayed = (q_ref[:, cols].astype(F32) * grown[:, h : h + 1]).astype(BF16)
        attended = near_ref[:, cols] + dot_nn(query_decayed, state_ref[h].astype(BF16))
        att_ref[:, cols] = attended
        squares += attended * attended
        crossed += g_ref[:, cols].astype(F32) * gain_ref[:, cols] * attended
    ones = jnp.ones((8, HEAD), F32)
    dims = (((1,), (1,)), ((), ()))
    square_rows = lax.dot_general(ones, squares, dims, precision=HIGH, preferred_element_type=F32)
    cross_rows = lax.dot_general(ones, crossed, dims, precision=HIGH, preferred_element_type=F32)
    which = lax.broadcasted_iota(jnp.int32, (8, rows), 0)
    both = jnp.where(which == 0, square_rows, cross_rows)
    for peer in range(sums_ref.shape[0]):
        sums_ref[peer] = both


def norm_columns(sums_ref, rows):
    whole = jnp.sum(sums_ref[...], axis=0)
    first = lax.broadcasted_iota(jnp.int32, (rows, rows), 0)
    second = lax.broadcasted_iota(jnp.int32, (rows, rows), 1)
    same = first == second
    square_sum = jnp.sum(jnp.where(same, whole[0:1, :], 0.0), axis=1, keepdims=True)
    cross_sum = jnp.sum(jnp.where(same, whole[1:2, :], 0.0), axis=1, keepdims=True)
    width = HEAD_COUNT * HEAD
    inverse = lax.rsqrt(square_sum / width + EPSILON)
    return inverse, inverse * inverse * inverse * (cross_sum / width)


def norm_grad_kernel(sums_ref, att_ref, g_ref, gain_ref, q_ref, inside_ref, gf_ref, pay_ref):
    rows, heads = inside_ref.shape
    per_head = pay_ref.shape[0] // heads
    slab = HEAD // per_head
    inverse, factor = norm_columns(sums_ref, rows)
    grown = jnp.exp(inside_ref[...])
    for h in range(heads):
        cols = head_cols(h)
        scaled = g_ref[:, cols].astype(F32) * gain_ref[:, cols]
        grad_flat = (inverse * scaled - att_ref[:, cols] * factor).astype(BF16)
        gf_ref[:, cols] = grad_flat
        query_decayed = (q_ref[:, cols].astype(F32) * grown[:, h : h + 1]).astype(BF16)
        state = dot_tn(query_decayed, grad_flat)
        pay_ref[h * per_head : (h + 1) * per_head] = state.reshape(per_head, slab, HEAD)


def near_grad_kernel(
    sums_ref, att_ref, gain_ref, gf_ref, q_ref, k_ref, v_ref, mix_ref, state_ref, inside_ref, across_ref,
    normed_ref, gq_ref, gk_ref, gv_ref,
):
    rows, heads = inside_ref.shape
    inverse, _ = norm_columns(sums_ref, rows)
    grown = jnp.exp(inside_ref[...])
    for h in range(heads):
        cols = head_cols(h)
        normed_ref[:, cols] = (att_ref[:, cols] * inverse * gain_ref[:, cols]).astype(BF16)
        grad_flat = gf_ref[:, cols]
        grad_scores = dot_nt(grad_flat, v_ref[:, cols])
        grad_mix = (grad_scores * weights_of(inside_ref, across_ref, h)).astype(BF16)
        far = dot_nt(grad_flat, state_ref[h].astype(BF16))
        gq_ref[:, cols] = (dot_nn(grad_mix, k_ref[:, cols]) + grown[:, h : h + 1] * far).astype(BF16)
        gk_ref[:, cols] = dot_tn(grad_mix, q_ref[:, cols])
        gv_ref[:, cols] = dot_tn(mix_ref[h], grad_flat)


def far_grad_kernel(gk_near_ref, gv_near_ref, k_ref, v_ref, state_ref, inside_ref, gk_ref, gv_ref):
    rows, heads = inside_ref.shape
    inside = inside_ref[...]
    shares = jnp.exp(inside[rows - 1 : rows, :] - inside)
    for h in range(heads):
        cols = head_cols(h)
        share = shares[:, h : h + 1]
        arriving = state_ref[h].astype(BF16)
        far = dot_nt(v_ref[:, cols], arriving)
        gk_ref[:, cols] = (gk_near_ref[:, cols] + share * far).astype(BF16)
        key_decayed = (k_ref[:, cols].astype(F32) * share).astype(BF16)
        gv_ref[:, cols] = (gv_near_ref[:, cols] + dot_nn(key_decayed, arriving)).astype(BF16)


def body(chips, tp_size, queries, key_vectors, values, decay_log, norm_gain, grad_out):
    rows, width = queries.shape
    heads = decay_log.shape[1]
    slab = heads * HEAD // chips
    groups = [[2 * chip + core for chip in range(chips)] for core in range(2)]
    swap = [(i, i ^ 1) for i in range(2 * chips)]
    core = (lax.axis_index("seq") % 2).astype(jnp.int32).reshape(1)
    gain = norm_gain.reshape(1, width)
    wide, tile = (rows, width), (chips, slab, HEAD)
    whole = rows * width

    def across_chips(array):
        return lax.all_to_all(array, "seq", 0, 0, axis_index_groups=groups)

    pay, inside, across = call(
        local_kernel,
        [((chips, slab + 8, HEAD), F32), ((rows, heads), F32), ((heads, rows), F32)],
        [key_vectors, values, decay_log],
        2 * whole * HEAD, 8 * whole,
    )
    mixing, near = call(
        mixing_kernel,
        [((heads, rows, rows), BF16), (wide, F32)],
        [queries, key_vectors, values, inside, across],
        4 * whole * rows, 12 * whole,
    )
    own = across_chips(pay)
    other = lax.ppermute(own, "seq", swap)
    entering_tiles, kept = call(
        forward_scan_kernel,
        [(tile, F32), ((chips, 16, HEAD), F32)],
        [core, own, other],
        4 * heads * HEAD * HEAD, 12 * heads * HEAD * HEAD, smem=1,
    )
    entering = across_chips(entering_tiles).reshape(heads, HEAD, HEAD)
    attended, sums = call(
        attend_kernel,
        [(wide, F32), ((tp_size, 8, rows), F32)],
        [queries, near, entering, inside, grad_out, gain],
        2 * whole * HEAD, 12 * whole,
    )
    sums = lax.all_to_all(sums, "tp", 0, 0)
    grad_flat, pay_back = call(
        norm_grad_kernel,
        [(wide, BF16), (tile, F32)],
        [sums, attended, grad_out, gain, queries, inside],
        2 * whole * HEAD, 12 * whole,
    )
    normed, grad_query, grad_key_near, grad_value_near = call(
        near_grad_kernel,
        [(wide, BF16), (wide, BF16), (wide, F32), (wide, F32)],
        [sums, attended, gain, grad_flat, queries, key_vectors, values, mixing, entering, inside, across],
        10 * whole * rows, 24 * whole,
    )
    own_back = across_chips(pay_back)
    other_back = lax.ppermute(own_back, "seq", swap)
    (arriving_tiles,) = call(
        reverse_scan_kernel,
        [(tile, F32)],
        [core, own_back, other_back, kept],
        4 * heads * HEAD * HEAD, 12 * heads * HEAD * HEAD, smem=1,
    )
    arriving = across_chips(arriving_tiles).reshape(heads, HEAD, HEAD)
    grad_key, grad_value = call(
        far_grad_kernel,
        [(wide, BF16), (wide, BF16)],
        [grad_key_near, grad_value_near, key_vectors, values, arriving, inside],
        4 * whole * HEAD, 16 * whole,
    )
    return normed, grad_query, grad_key, grad_value


def solution(mesh):
    spec = P("seq", "tp")
    return jax.shard_map(
        functools.partial(body, mesh.shape["seq"] // 2, mesh.shape["tp"]),
        mesh=mesh,
        in_specs=(spec, spec, spec, spec, P("tp"), spec),
        out_specs=(spec, spec, spec, spec),
        check_vma=False,
    )
```

```python
import functools

import jax
import jax.numpy as jnp
from jax import lax
from jax.experimental import pallas as pl
from jax.experimental.pallas import tpu as pltpu
from jax.sharding import Mesh
from jax.sharding import PartitionSpec as P

HEAD_COUNT = 64
HEAD = 128
EPSILON = 1e-06
HIGH = lax.Precision.HIGHEST
F32 = jnp.float32
BF16 = jnp.bfloat16
VMEM_LIMIT = 16 * 1024 * 1024
NN = (((1,), (0,)), ((), ()))
NT = (((1,), (1,)), ((), ()))
TN = (((0,), (0,)), ((), ()))


def dot(a, b, dims, precision=None):
    return lax.dot_general(a, b, dims, precision=precision, preferred_element_type=F32)


def call(kernel, outs, args, flops, bytes_accessed, smem=0, hbm=0, scratch=()):
    specs = [pl.BlockSpec(memory_space=pltpu.SMEM)] * smem
    specs += [pl.BlockSpec(memory_space=pltpu.HBM)] * hbm
    specs += [pl.BlockSpec(memory_space=pltpu.VMEM)] * (len(args) - smem - hbm)
    return pl.pallas_call(
        kernel,
        out_shape=[jax.ShapeDtypeStruct(s, d) for s, d in outs],
        in_specs=specs,
        out_specs=[pl.BlockSpec(memory_space=pltpu.VMEM)] * len(outs),
        scratch_shapes=list(scratch),
        compiler_params=pltpu.CompilerParams(vmem_limit_bytes=VMEM_LIMIT),
        cost_estimate=pl.CostEstimate(
            flops=flops, bytes_accessed=bytes_accessed, transcendentals=0
        ),
    )(*args)


def head_cols(h):
    return slice(h * HEAD, (h + 1) * HEAD)


def head_rows(h):
    return slice(h * HEAD, (h + 1) * HEAD)


def local_kernel(k_hbm, v_hbm, decay_ref, pay_ref, kept_ref, inside_ref, across_ref, k_ref, v_ref, sems):
    heads, rows = decay_ref.shape
    copies = [
        pltpu.make_async_copy(k_hbm, k_ref, sems.at[0]),
        pltpu.make_async_copy(v_hbm, v_ref, sems.at[1]),
    ]
    for copy in copies:
        copy.start()
    decay = decay_ref[...]
    first = lax.broadcasted_iota(jnp.int32, (rows, rows), 0)
    second = lax.broadcasted_iota(jnp.int32, (rows, rows), 1)
    inside = dot((first >= second).astype(F32), decay, NT, HIGH)
    across = dot(decay, (first <= second).astype(F32), NN, HIGH)
    inside_ref[...] = inside
    across_ref[...] = across
    shares = jnp.exp(inside[rows - 1 : rows, :] - inside)
    kept = jnp.broadcast_to(jnp.exp(across[:, rows - 1 : rows]), (heads, HEAD))
    kept_ref[...] = kept
    pay_ref[heads * HEAD :, :] = kept
    for copy in copies:
        copy.wait()
    for h in range(heads):
        key_decayed = (k_ref[:, head_cols(h)].astype(F32) * shares[:, h : h + 1]).astype(BF16)
        pay_ref[head_rows(h), :] = dot(key_decayed, v_ref[:, head_cols(h)], TN)


def forward_join_kernel(core_ref, own_ref, other_ref, pay_ref):
    half = pay_ref.shape[0] // 17 * 16 // HEAD
    core = core_ref[0]
    base = pl.multiple_of(core * half * HEAD, half * HEAD)
    kept_own = own_ref[2 * half * HEAD :, :]
    kept_other = other_ref[2 * half * HEAD :, :]
    kept_both = kept_own * kept_other
    kept_second = jnp.where(core == 0, kept_other, kept_own)

    def half_of(rows, i):
        return jnp.where(core == 0, rows[i : i + 1], rows[half + i : half + i + 1])

    for i in range(half):
        here = pl.ds(base + i * HEAD, HEAD)
        own, other = own_ref[here, :], other_ref[here, :]
        first = jnp.where(core == 0, own, other)
        second = jnp.where(core == 0, other, own)
        joined = half_of(kept_second, i) * first + second
        kept = half_of(kept_both, i)
        for part in range(8):
            at = 17 * (8 * i + part)
            pay_ref[at : at + 16, :] = joined[16 * part : 16 * part + 16]
            pay_ref[at + 16 : at + 17, :] = kept


def forward_scan_kernel(got_ref, out_ref, kept_ref):
    count = out_ref.shape[0]
    state = jnp.zeros(out_ref.shape[1:], F32)
    for j in range(count):
        out_ref[j] = state
        kept = got_ref[17 * j + 16 : 17 * j + 17, :]
        kept_ref[j : j + 1, :] = kept
        state = kept * state + got_ref[17 * j : 17 * j + 16, :]


def reverse_join_kernel(core_ref, own_ref, other_ref, kept_own_ref, got_ref, out_ref):
    half = own_ref.shape[0] // HEAD // 2
    core = core_ref[0]
    base = pl.multiple_of(core * half * HEAD, half * HEAD)
    kept_first = jnp.where(core == 0, kept_own_ref[...], got_ref[2 * half * HEAD :, :])
    for i in range(half):
        here = pl.ds(base + i * HEAD, HEAD)
        own, other = own_ref[here, :], other_ref[here, :]
        first = jnp.where(core == 0, own, other)
        second = jnp.where(core == 0, other, own)
        kept = jnp.where(core == 0, kept_first[i : i + 1], kept_first[half + i : half + i + 1])
        out_ref[head_rows(i), :] = first + kept * second


def reverse_scan_kernel(got_ref, kept_ref, out_ref):
    count = out_ref.shape[0]
    state = jnp.zeros(out_ref.shape[1:], F32)
    for j in reversed(range(count)):
        out_ref[j] = state
        state = kept_ref[j : j + 1, :] * state + got_ref[j]


def weights_of(inside_ref, across_ref, h):
    rows = inside_ref.shape[0]
    first = lax.broadcasted_iota(jnp.int32, (rows, rows), 0)
    second = lax.broadcasted_iota(jnp.int32, (rows, rows), 1)
    spread = inside_ref[:, h : h + 1] - across_ref[h : h + 1, :]
    return jnp.exp(jnp.where(first >= second, spread, -1e30))


def mixing_kernel(q_ref, k_ref, inside_ref, across_ref, mix_ref):
    for h in range(inside_ref.shape[1]):
        cols = head_cols(h)
        scores = dot(q_ref[:, cols], k_ref[:, cols], NT)
        mix_ref[h] = (scores * weights_of(inside_ref, across_ref, h)).astype(BF16)


def attend_kernel(
    core_ref, q_ref, v_ref, mix_ref, half_ref, half_other_ref, got_ref, inside_ref, g_ref, gain_ref,
    att_ref, sums_ref, state_ref,
):
    rows, heads = inside_ref.shape
    half = heads // 2
    core = core_ref[0]
    state_ref[pl.ds(core * half, half)] = half_ref[...]
    state_ref[pl.ds((1 - core) * half, half)] = half_other_ref[...]

    @pl.when(core == 1)
    def _():
        for h in range(heads):
            kept = got_ref[heads * HEAD + h : heads * HEAD + h + 1, :]
            state_ref[h] = kept * state_ref[h] + got_ref[head_rows(h), :]

    grown = jnp.exp(inside_ref[...])
    squares = jnp.zeros((rows, HEAD), F32)
    crossed = jnp.zeros((rows, HEAD), F32)
    for h in range(heads):
        cols = head_cols(h)
        query_decayed = (q_ref[:, cols].astype(F32) * grown[:, h : h + 1]).astype(BF16)
        attended = dot(mix_ref[h], v_ref[:, cols], NN) + dot(query_decayed, state_ref[h].astype(BF16), NN)
        att_ref[:, cols] = attended
        squares += attended * attended
        crossed += g_ref[:, cols].astype(F32) * gain_ref[:, cols] * attended
    ones = jnp.ones((8, HEAD), F32)
    square_rows = dot(ones, squares, NT, HIGH)
    cross_rows = dot(ones, crossed, NT, HIGH)
    which = lax.broadcasted_iota(jnp.int32, (8, rows), 0)
    both = jnp.where(which == 0, square_rows, cross_rows)
    for peer in range(sums_ref.shape[0]):
        sums_ref[peer] = both


def norm_columns(sums_ref, rows):
    whole = jnp.sum(sums_ref[...], axis=0)
    first = lax.broadcasted_iota(jnp.int32, (rows, rows), 0)
    second = lax.broadcasted_iota(jnp.int32, (rows, rows), 1)
    same = first == second
    square_sum = jnp.sum(jnp.where(same, whole[0:1, :], 0.0), axis=1, keepdims=True)
    cross_sum = jnp.sum(jnp.where(same, whole[1:2, :], 0.0), axis=1, keepdims=True)
    width = HEAD_COUNT * HEAD
    inverse = lax.rsqrt(square_sum / width + EPSILON)
    return inverse, inverse * inverse * inverse * (cross_sum / width)


def grad_flat_of(inverse, factor, att_ref, g_ref, gain_ref, cols):
    scaled = g_ref[:, cols].astype(F32) * gain_ref[:, cols]
    return (inverse * scaled - att_ref[:, cols] * factor).astype(BF16)


def norm_grad_kernel(sums_ref, att_ref, g_ref, gain_ref, q_ref, inside_ref, pay_ref):
    rows, heads = inside_ref.shape
    inverse, factor = norm_columns(sums_ref, rows)
    grown = jnp.exp(inside_ref[...])
    for h in range(heads):
        cols = head_cols(h)
        grad_flat = grad_flat_of(inverse, factor, att_ref, g_ref, gain_ref, cols)
        query_decayed = (q_ref[:, cols].astype(F32) * grown[:, h : h + 1]).astype(BF16)
        pay_ref[head_rows(h), :] = dot(query_decayed, grad_flat, TN)


def near_grad_kernel(
    sums_ref, att_ref, g_ref, gain_ref, q_ref, k_ref, v_ref, mix_ref, state_ref, inside_ref, across_ref,
    normed_ref, gq_ref, gk_ref, gv_ref,
):
    rows, heads = inside_ref.shape
    inverse, factor = norm_columns(sums_ref, rows)
    grown = jnp.exp(inside_ref[...])
    for h in range(heads):
        cols = head_cols(h)
        normed_ref[:, cols] = (att_ref[:, cols] * inverse * gain_ref[:, cols]).astype(BF16)
        grad_flat = grad_flat_of(inverse, factor, att_ref, g_ref, gain_ref, cols)
        grad_scores = dot(grad_flat, v_ref[:, cols], NT)
        grad_mix = (grad_scores * weights_of(inside_ref, across_ref, h)).astype(BF16)
        far = dot(grad_flat, state_ref[h].astype(BF16), NT)
        gq_ref[:, cols] = (dot(grad_mix, k_ref[:, cols], NN) + grown[:, h : h + 1] * far).astype(BF16)
        gk_ref[:, cols] = dot(grad_mix, q_ref[:, cols], TN)
        gv_ref[:, cols] = dot(mix_ref[h], grad_flat, TN)


def far_grad_kernel(
    core_ref, gk_near_ref, gv_near_ref, k_ref, v_ref, half_ref, half_other_ref, other_ref, kept_got_ref,
    inside_ref, gk_ref, gv_ref, state_ref,
):
    rows, heads = inside_ref.shape
    half = heads // 2
    core = core_ref[0]
    state_ref[pl.ds(core * half, half)] = half_ref[...]
    state_ref[pl.ds((1 - core) * half, half)] = half_other_ref[...]

    @pl.when(core == 0)
    def _():
        for h in range(heads):
            kept = kept_got_ref[heads * HEAD + h : heads * HEAD + h + 1, :]
            state_ref[h] = kept * state_ref[h] + other_ref[head_rows(h), :]

    inside = inside_ref[...]
    shares = jnp.exp(inside[rows - 1 : rows, :] - inside)
    for h in range(heads):
        cols = head_cols(h)
        share = shares[:, h : h + 1]
        arriving = state_ref[h].astype(BF16)
        far = dot(v_ref[:, cols], arriving, NT)
        gk_ref[:, cols] = (gk_near_ref[:, cols] + share * far).astype(BF16)
        key_decayed = (k_ref[:, cols].astype(F32) * share).astype(BF16)
        gv_ref[:, cols] = (gv_near_ref[:, cols] + dot(key_decayed, arriving, NN)).astype(BF16)


def body(chips, tp_size, queries, key_vectors, values, decay_log, norm_gain, grad_out):
    rows, width = queries.shape
    heads = decay_log.shape[1]
    half = heads // 2
    slab = half * HEAD // chips
    core = lax.axis_index("core").astype(jnp.int32).reshape(1)
    gain = norm_gain.reshape(1, width)
    wide, tile = (rows, width), (chips, slab, HEAD)
    state_rows, half_state = (heads * HEAD, HEAD), (half, HEAD, HEAD)
    whole, size = rows * width, heads * HEAD * HEAD

    def across_chips(array):
        return lax.all_to_all(array, ("x", "y"), 0, 0)

    def swap(array):
        return lax.ppermute(array, "core", [(0, 1), (1, 0)])

    own, kept_own, inside, across = call(
        local_kernel,
        [((heads * HEAD + heads, HEAD), F32), ((heads, HEAD), F32), ((rows, heads), F32), ((heads, rows), F32)],
        [key_vectors, values, decay_log.T],
        2 * whole * HEAD, 8 * whole, hbm=2,
        scratch=[pltpu.VMEM(wide, BF16), pltpu.VMEM(wide, BF16), pltpu.SemaphoreType.DMA((2,))],
    )
    (mixing,) = call(
        mixing_kernel,
        [((heads, rows, rows), BF16)],
        [queries, key_vectors, inside, across],
        2 * whole * rows, 12 * whole,
    )
    got = swap(own)
    (pay,) = call(
        forward_join_kernel,
        [((chips * (slab + 1), HEAD), F32)],
        [core, own, got],
        2 * size, 12 * size, smem=1,
    )
    pay = across_chips(pay.reshape(chips, 1, (slab + 1) * HEAD)).reshape(chips * (slab + 1), HEAD)
    tiles, kept_chips = call(
        forward_scan_kernel,
        [(tile, F32), ((chips, HEAD), F32)],
        [pay],
        size, 4 * size,
    )
    half_in = across_chips(tiles).reshape(half_state)
    half_other = swap(half_in)
    attended, sums, entering = call(
        attend_kernel,
        [(wide, F32), ((tp_size, 8, rows), F32), ((heads, HEAD, HEAD), F32)],
        [core, queries, values, mixing, half_in, half_other, got, inside, grad_out, gain],
        2 * whole * (HEAD + rows), 12 * whole, smem=1,
    )
    sums = lax.all_to_all(sums, "tp", 0, 0)
    (back,) = call(
        norm_grad_kernel,
        [(state_rows, F32)],
        [sums, attended, grad_out, gain, queries, inside],
        2 * whole * HEAD, 12 * whole,
    )
    back_other = swap(back)
    normed, grad_query, grad_key_near, grad_value_near = call(
        near_grad_kernel,
        [(wide, BF16), (wide, BF16), (wide, F32), (wide, F32)],
        [sums, attended, grad_out, gain, queries, key_vectors, values, mixing, entering, inside, across],
        10 * whole * rows, 24 * whole,
    )
    (pay_back,) = call(
        reverse_join_kernel,
        [((half * HEAD, HEAD), F32)],
        [core, back, back_other, kept_own, got],
        2 * size, 12 * size, smem=1,
    )
    (tiles_back,) = call(
        reverse_scan_kernel,
        [(tile, F32)],
        [across_chips(pay_back.reshape(tile)), kept_chips],
        size, 4 * size,
    )
    half_back = across_chips(tiles_back).reshape(half_state)
    half_back_other = swap(half_back)
    grad_key, grad_value = call(
        far_grad_kernel,
        [(wide, BF16), (wide, BF16)],
        [
            core, grad_key_near, grad_value_near, key_vectors, values,
            half_back, half_back_other, back_other, got, inside,
        ],
        4 * whole * HEAD, 16 * whole, smem=1,
        scratch=[pltpu.VMEM((heads, HEAD, HEAD), F32)],
    )
    return normed, grad_query, grad_key, grad_value


def solution(mesh):
    seq, tp = mesh.shape["seq"], mesh.shape["tp"]
    fine = Mesh(mesh.devices.reshape(seq // 16, 8, 2, tp), ("x", "y", "core", "tp"))
    spec = P(("x", "y", "core"), "tp")
    return jax.shard_map(
        functools.partial(body, seq // 2, tp),
        mesh=fine,
        in_specs=(spec, spec, spec, spec, P("tp"), spec),
        out_specs=(spec, spec, spec, spec),
        check_vma=False,
    )
```

```python
import functools

import jax
import jax.numpy as jnp
from jax import lax
from jax.experimental import pallas as pl
from jax.experimental.pallas import tpu as pltpu
from jax.sharding import Mesh
from jax.sharding import PartitionSpec as P

HEAD_COUNT = 64
HEAD = 128
EPSILON = 1e-06
HIGH = lax.Precision.HIGHEST
F32 = jnp.float32
BF16 = jnp.bfloat16
VMEM_LIMIT = 20 * 1024 * 1024
NN = (((1,), (0,)), ((), ()))
NT = (((1,), (1,)), ((), ()))
TN = (((0,), (0,)), ((), ()))


def dot(a, b, dims, precision=None):
    return lax.dot_general(a, b, dims, precision=precision, preferred_element_type=F32)


SPACES = {"s": pltpu.SMEM, "h": pltpu.HBM, "v": pltpu.VMEM, "a": pl.ANY}


def call(kernel, outs, args, flops, bytes_accessed, scratch=()):
    return pl.pallas_call(
        kernel,
        out_shape=[SPACES[m](s, d) for m, s, d in outs],
        in_specs=[pl.BlockSpec(memory_space=SPACES[m]) for m, _ in args],
        out_specs=[pl.BlockSpec(memory_space=SPACES[m]) for m, _, _ in outs],
        scratch_shapes=list(scratch),
        compiler_params=pltpu.CompilerParams(vmem_limit_bytes=VMEM_LIMIT),
        cost_estimate=pl.CostEstimate(
            flops=flops, bytes_accessed=bytes_accessed, transcendentals=0
        ),
    )(*[pltpu.with_memory_space_constraint(a, SPACES[m]) if m in "hv" else a for m, a in args])


def head_cols(h):
    return slice(h * HEAD, (h + 1) * HEAD)


def head_rows(h):
    return slice(h * HEAD, (h + 1) * HEAD)


def local_kernel(
    q_hbm, k_hbm, v_hbm, g_hbm, decay_hbm, gain_hbm,
    pay_ref, kept_ref, inside_ref, across_ref, key_ref, q_ref, k_ref, v_ref, g_ref, gain_ref, decay_ref, sems,
):
    heads, rows = decay_ref.shape
    halves = [slice(0, heads // 2 * HEAD), slice(heads // 2 * HEAD, heads * HEAD)]
    pieces = [(decay_hbm, decay_ref)]
    for cols in halves:
        pieces += [(k_hbm.at[:, cols], k_ref.at[:, cols]), (v_hbm.at[:, cols], v_ref.at[:, cols])]
    pieces += [(q_hbm, q_ref), (g_hbm, g_ref), (gain_hbm, gain_ref)]
    copies = [pltpu.make_async_copy(*piece, sems.at[i]) for i, piece in enumerate(pieces)]
    for copy in copies:
        copy.start()
    first = lax.broadcasted_iota(jnp.int32, (rows, rows), 0)
    second = lax.broadcasted_iota(jnp.int32, (rows, rows), 1)
    copies[0].wait()
    decay = decay_ref[...]
    inside = dot((first >= second).astype(F32), decay, NT, HIGH)
    across = dot(decay, (first <= second).astype(F32), NN, HIGH)
    inside_ref[...] = inside
    across_ref[...] = across
    shares = jnp.exp(inside[rows - 1 : rows, :] - inside)
    kept = jnp.broadcast_to(jnp.exp(across[:, rows - 1 : rows]), (heads, HEAD))
    kept_ref[...] = kept
    pay_ref[heads * HEAD :, :] = kept
    for h in range(heads):
        if h == 0 or h == heads // 2:
            at = 1 if h == 0 else 3
            copies[at].wait()
            copies[at + 1].wait()
        cols = head_cols(h)
        key_decayed = (k_ref[:, cols].astype(F32) * shares[:, h : h + 1]).astype(BF16)
        key_ref[:, cols] = key_decayed
        pay_ref[head_rows(h), :] = dot(key_decayed, v_ref[:, cols], TN)
    for copy in copies[5:]:
        copy.wait()


def forward_join_kernel(core_ref, after_ref, own_ref, other_ref, pay_ref):
    half = pay_ref.shape[0] // 17 * 16 // HEAD
    core = core_ref[0]
    base = pl.multiple_of(core * half * HEAD, half * HEAD)
    kept_own = own_ref[2 * half * HEAD :, :]
    kept_other = other_ref[2 * half * HEAD :, :]
    kept_both = kept_own * kept_other
    kept_second = jnp.where(core == 0, kept_other, kept_own)

    def half_of(rows, i):
        return jnp.where(core == 0, rows[i : i + 1], rows[half + i : half + i + 1])

    for i in range(half):
        here = pl.ds(base + i * HEAD, HEAD)
        own, other = own_ref[here, :], other_ref[here, :]
        first = jnp.where(core == 0, own, other)
        second = jnp.where(core == 0, other, own)
        joined = half_of(kept_second, i) * first + second
        kept = half_of(kept_both, i)
        for part in range(8):
            at = 17 * (8 * i + part)
            pay_ref[at : at + 16, :] = joined[16 * part : 16 * part + 16]
            pay_ref[at + 16 : at + 17, :] = kept


def forward_scan_kernel(got_ref, out_ref, kept_ref):
    count = out_ref.shape[0]
    state = jnp.zeros(out_ref.shape[1:], F32)
    for j in range(count):
        out_ref[j] = state
        kept = got_ref[17 * j + 16 : 17 * j + 17, :]
        kept_ref[j : j + 1, :] = kept
        state = kept * state + got_ref[17 * j : 17 * j + 16, :]


def reverse_join_kernel(core_ref, after_hbm, own_ref, other_ref, kept_own_ref, got_ref, out_ref):
    half = own_ref.shape[0] // HEAD // 2
    core = core_ref[0]
    base = pl.multiple_of(core * half * HEAD, half * HEAD)
    kept_first = jnp.where(core == 0, kept_own_ref[...], got_ref[2 * half * HEAD :, :])
    for i in range(half):
        here = pl.ds(base + i * HEAD, HEAD)
        own, other = own_ref[here, :], other_ref[here, :]
        first = jnp.where(core == 0, own, other)
        second = jnp.where(core == 0, other, own)
        kept = jnp.where(core == 0, kept_first[i : i + 1], kept_first[half + i : half + i + 1])
        out_ref[head_rows(i), :] = first + kept * second


def reverse_scan_kernel(got_ref, kept_ref, out_ref):
    count = out_ref.shape[0]
    state = jnp.zeros(out_ref.shape[1:], F32)
    for j in reversed(range(count)):
        out_ref[j] = state
        state = kept_ref[j : j + 1, :] * state + got_ref[j]


def weights_of(inside_ref, across_ref, h, transposed=False):
    rows = inside_ref.shape[0]
    first = lax.broadcasted_iota(jnp.int32, (rows, rows), 0)
    second = lax.broadcasted_iota(jnp.int32, (rows, rows), 1)
    if transposed:
        spread = across_ref[h : h + 1, :] - inside_ref[:, h : h + 1]
        return jnp.exp(jnp.where(second >= first, spread, -1e30))
    spread = inside_ref[:, h : h + 1] - across_ref[h : h + 1, :]
    return jnp.exp(jnp.where(first >= second, spread, -1e30))


def mixing_kernel(
    q_ref, k_ref, v_ref, g_ref, gain_ref, inside_ref, across_ref,
    near_ref, mix_turned_ref, query_ref, query_turned_ref, weights_ref, weights_turned_ref, scaled_ref,
):
    grown = jnp.exp(inside_ref[...])
    for h in range(inside_ref.shape[1]):
        cols = head_cols(h)
        queries, keys = q_ref[:, cols], k_ref[:, cols]
        weights = weights_of(inside_ref, across_ref, h)
        weights_ref[h] = weights
        mixing = (dot(queries, keys, NT) * weights).astype(BF16)
        near_ref[:, cols] = dot(mixing, v_ref[:, cols], NN)
        weights_turned = weights_of(inside_ref, across_ref, h, True)
        weights_turned_ref[h] = weights_turned
        mix_turned_ref[h] = (dot(keys, queries, NT) * weights_turned).astype(BF16)
        decayed = queries.astype(F32) * grown[:, h : h + 1]
        query_ref[:, cols] = decayed.astype(BF16)
        query_turned_ref[h] = decayed.T.astype(BF16)
        scaled_ref[:, cols] = g_ref[:, cols].astype(F32) * gain_ref[:, cols]


def attend_kernel(
    core_ref, near_ref, query_ref, half_ref, half_other_ref, got_ref, scaled_ref,
    att_ref, sums_ref, state_bf_ref, state_ref,
):
    rows, width = near_ref.shape
    heads = width // HEAD
    half = heads // 2
    core = core_ref[0]
    state_ref[pl.ds(core * half, half)] = half_ref[...]
    state_ref[pl.ds((1 - core) * half, half)] = half_other_ref[...]

    @pl.when(core == 1)
    def _():
        for h in range(heads):
            kept = got_ref[heads * HEAD + h : heads * HEAD + h + 1, :]
            state_ref[h] = kept * state_ref[h] + got_ref[head_rows(h), :]

    squares = jnp.zeros((rows, HEAD), F32)
    crossed = jnp.zeros((rows, HEAD), F32)
    for h in range(heads):
        cols = head_cols(h)
        state = state_ref[h].astype(BF16)
        state_bf_ref[h] = state
        attended = near_ref[:, cols] + dot(query_ref[:, cols], state, NN)
        att_ref[:, cols] = attended
        squares += attended * attended
        crossed += scaled_ref[:, cols] * attended
    ones = jnp.ones((8, HEAD), F32)
    square_rows = dot(ones, squares, NT, HIGH)
    cross_rows = dot(ones, crossed, NT, HIGH)
    for peer in range(sums_ref.shape[0]):
        sums_ref[peer, 0:1, :] = square_rows[0:1]
        sums_ref[peer, 1:2, :] = cross_rows[0:1]


def norm_columns(sums_ref, rows):
    whole = jnp.sum(sums_ref[...], axis=0)
    first = lax.broadcasted_iota(jnp.int32, (rows, rows), 0)
    second = lax.broadcasted_iota(jnp.int32, (rows, rows), 1)
    same = first == second
    square_sum = jnp.sum(jnp.where(same, whole[0:1, :], 0.0), axis=1, keepdims=True)
    cross_sum = jnp.sum(jnp.where(same, whole[1:2, :], 0.0), axis=1, keepdims=True)
    width = HEAD_COUNT * HEAD
    inverse = lax.rsqrt(square_sum / width + EPSILON)
    return inverse, inverse * inverse * inverse * (cross_sum / width)


def norm_grad_kernel(sums_ref, att_ref, scaled_ref, query_turned_ref, pay_ref, gf_ref):
    rows, width = att_ref.shape
    inverse, factor = norm_columns(sums_ref, rows)
    for h in range(width // HEAD):
        cols = head_cols(h)
        grad_flat = (inverse * scaled_ref[:, cols] - att_ref[:, cols] * factor).astype(BF16)
        gf_ref[:, cols] = grad_flat
        pay_ref[head_rows(h), :] = dot(query_turned_ref[h], grad_flat, NN)


def send_out(copies, source, target, sems, i, cols):
    copy = pltpu.make_async_copy(source.at[:, cols], target.at[:, cols], sems.at[i])
    copy.start()
    copies.append(copy)


def near_query_kernel(
    sums_ref, att_ref, gain_ref, gf_ref, k_ref, v_ref, state_ref, inside_ref, weights_ref,
    normed_hbm, gq_hbm, normed_ref, gq_ref, sems,
):
    rows, heads = inside_ref.shape
    inverse, _ = norm_columns(sums_ref, rows)
    grown = jnp.exp(inside_ref[...])
    copies = []
    for h in range(heads):
        cols = head_cols(h)
        normed_ref[:, cols] = (att_ref[:, cols] * inverse * gain_ref[:, cols]).astype(BF16)
        grad_flat = gf_ref[:, cols]
        grad_mix = (dot(grad_flat, v_ref[:, cols], NT) * weights_ref[h]).astype(BF16)
        far = dot(grad_flat, state_ref[h], NT)
        gq_ref[:, cols] = (dot(grad_mix, k_ref[:, cols], NN) + grown[:, h : h + 1] * far).astype(BF16)
        if h % 2:
            pair = slice((h - 1) * HEAD, (h + 1) * HEAD)
            send_out(copies, normed_ref, normed_hbm, sems, h - 1, pair)
            send_out(copies, gq_ref, gq_hbm, sems, h, pair)
    for copy in copies:
        copy.wait()


def near_key_kernel(gf_ref, q_ref, v_ref, mix_turned_ref, weights_turned_ref, gk_ref, gv_ref):
    for h in range(mix_turned_ref.shape[0]):
        cols = head_cols(h)
        grad_flat = gf_ref[:, cols]
        turned = (dot(v_ref[:, cols], grad_flat, NT) * weights_turned_ref[h]).astype(BF16)
        gk_ref[:, cols] = dot(turned, q_ref[:, cols], NN)
        gv_ref[:, cols] = dot(mix_turned_ref[h], grad_flat, NN)


def far_grad_kernel(
    core_ref, gk_near_ref, gv_near_ref, key_ref, v_ref, half_ref, half_other_ref, other_ref, kept_got_ref,
    inside_ref, gk_hbm, gv_hbm, state_ref, gk_ref, gv_ref, sems,
):
    rows, heads = inside_ref.shape
    half = heads // 2
    core = core_ref[0]
    state_ref[pl.ds(core * half, half)] = half_ref[...]
    state_ref[pl.ds((1 - core) * half, half)] = half_other_ref[...]

    @pl.when(core == 0)
    def _():
        for h in range(heads):
            kept = kept_got_ref[heads * HEAD + h : heads * HEAD + h + 1, :]
            state_ref[h] = kept * state_ref[h] + other_ref[head_rows(h), :]

    inside = inside_ref[...]
    shares = jnp.exp(inside[rows - 1 : rows, :] - inside)
    copies = []
    for h in range(heads):
        cols = head_cols(h)
        arriving = state_ref[h].astype(BF16)
        far = dot(v_ref[:, cols], arriving, NT)
        gk_ref[:, cols] = (gk_near_ref[:, cols] + shares[:, h : h + 1] * far).astype(BF16)
        gv_ref[:, cols] = (gv_near_ref[:, cols] + dot(key_ref[:, cols], arriving, NN)).astype(BF16)
        if h % 2:
            pair = slice((h - 1) * HEAD, (h + 1) * HEAD)
            send_out(copies, gk_ref, gk_hbm, sems, h - 1, pair)
            send_out(copies, gv_ref, gv_hbm, sems, h, pair)
    for copy in copies:
        copy.wait()


def body(chips, tp_size, queries, key_vectors, values, decay_log, norm_gain, grad_out):
    rows, width = queries.shape
    heads = decay_log.shape[1]
    half = heads // 2
    slab = half * HEAD // chips
    core = lax.axis_index("core").astype(jnp.int32).reshape(1)
    gain = norm_gain.reshape(1, width)
    wide, tile = (rows, width), (chips, slab, HEAD)
    state_rows, half_state = (heads * HEAD, HEAD), (half, HEAD, HEAD)
    whole, size = rows * width, heads * HEAD * HEAD

    def across_chips(array):
        return lax.all_to_all(array, ("x", "y"), 0, 0)

    def swap(array):
        return lax.ppermute(array, "core", [(0, 1), (1, 0)])

    wide_bf, wide_f32 = ("v", wide, BF16), ("v", wide, F32)
    square, per_token = (heads, rows, rows), ("v", (rows, heads), F32)
    inputs = [queries, key_vectors, values, grad_out, decay_log.T, gain]
    own, kept_own, inside, across, key_decayed, q, k, v, g, gain = call(
        local_kernel,
        [
            ("v", (heads * HEAD + heads, HEAD), F32), ("v", (heads, HEAD), F32), per_token,
            ("v", (heads, rows), F32), wide_bf, wide_bf, wide_bf, wide_bf, wide_bf, ("v", (1, width), F32),
        ],
        [("h", a) for a in inputs],
        2 * whole * HEAD, 8 * whole,
        scratch=[pltpu.VMEM((heads, rows), F32), pltpu.SemaphoreType.DMA((8,))],
    )
    got = swap(own)
    near, mixing_turned, query_decayed, query_turned, weights, weights_turned, scaled = call(
        mixing_kernel,
        [
            wide_f32, ("v", square, BF16), wide_bf, ("v", (heads, HEAD, rows), BF16), ("v", square, F32),
            ("v", square, F32), wide_f32,
        ],
        [("v", a) for a in (q, k, v, g, gain, inside, across)],
        6 * whole * rows, 12 * whole,
    )
    (pay,) = call(
        forward_join_kernel,
        [("v", (chips * (slab + 1), HEAD), F32)],
        [("s", core), ("a", query_decayed), ("v", own), ("v", got)],
        2 * size, 12 * size,
    )
    pay = across_chips(pay.reshape(chips, 1, (slab + 1) * HEAD)).reshape(chips * (slab + 1), HEAD)
    tiles, kept_chips = call(
        forward_scan_kernel,
        [("v", tile, F32), ("v", (chips, HEAD), F32)],
        [("v", pay)],
        size, 4 * size,
    )
    half_in = across_chips(tiles).reshape(half_state)
    half_other = swap(half_in)
    attended, sums, entering = call(
        attend_kernel,
        [wide_f32, ("v", (tp_size, 2, rows), F32), ("v", (heads, HEAD, HEAD), BF16)],
        [("s", core)] + [("v", a) for a in (near, query_decayed, half_in, half_other, got, scaled)],
        2 * whole * HEAD, 12 * whole,
        scratch=[pltpu.VMEM((heads, HEAD, HEAD), F32)],
    )
    sums = lax.all_to_all(sums, "tp", 0, 0)
    back, grad_flat = call(
        norm_grad_kernel,
        [("v", state_rows, F32), wide_bf],
        [("v", a) for a in (sums, attended, scaled, query_turned)],
        2 * whole * HEAD, 12 * whole,
    )
    back_other = swap(back)
    outputs = [pltpu.VMEM(wide, BF16), pltpu.VMEM(wide, BF16), pltpu.SemaphoreType.DMA((heads,))]
    normed, grad_query = call(
        near_query_kernel,
        [("h", wide, BF16), ("h", wide, BF16)],
        [("v", a) for a in (sums, attended, gain, grad_flat, k, v, entering, inside, weights)],
        6 * whole * rows, 16 * whole, scratch=outputs,
    )
    (pay_back,) = call(
        reverse_join_kernel,
        [("v", (half * HEAD, HEAD), F32)],
        [("s", core), ("h", grad_query)] + [("v", a) for a in (back, back_other, kept_own, got)],
        2 * size, 12 * size,
    )
    grad_key_near, grad_value_near = call(
        near_key_kernel,
        [wide_f32, wide_f32],
        [("v", a) for a in (grad_flat, q, v, mixing_turned, weights_turned)],
        6 * whole * rows, 16 * whole,
    )
    (tiles_back,) = call(
        reverse_scan_kernel,
        [("v", tile, F32)],
        [("v", across_chips(pay_back.reshape(tile))), ("v", kept_chips)],
        size, 4 * size,
    )
    half_back = across_chips(tiles_back).reshape(half_state)
    half_back_other = swap(half_back)
    far_args = (
        grad_key_near, grad_value_near, key_decayed, v, half_back, half_back_other, back_other, got, inside
    )
    grad_key, grad_value = call(
        far_grad_kernel,
        [("h", wide, BF16), ("h", wide, BF16)],
        [("s", core)] + [("v", a) for a in far_args],
        4 * whole * HEAD, 16 * whole,
        scratch=[pltpu.VMEM((heads, HEAD, HEAD), F32), *outputs],
    )
    return normed, grad_query, grad_key, grad_value


def solution(mesh):
    seq, tp = mesh.shape["seq"], mesh.shape["tp"]
    fine = Mesh(mesh.devices.reshape(seq // 16, 8, 2, tp), ("x", "y", "core", "tp"))
    spec = P(("x", "y", "core"), "tp")
    return jax.shard_map(
        functools.partial(body, seq // 2, tp),
        mesh=fine,
        in_specs=(spec, spec, spec, spec, P("tp"), spec),
        out_specs=(spec, spec, spec, spec),
        check_vma=False,
    )
```

```python
import functools

import jax
import jax.numpy as jnp
from jax import lax
from jax.experimental import pallas as pl
from jax.experimental.pallas import tpu as pltpu
from jax.sharding import Mesh
from jax.sharding import PartitionSpec as P

HEAD_COUNT = 64
HEAD = 128
EPSILON = 1e-06
HIGH = lax.Precision.HIGHEST
F32 = jnp.float32
BF16 = jnp.bfloat16
VMEM_LIMIT = 20 * 1024 * 1024
NN = (((1,), (0,)), ((), ()))
NT = (((1,), (1,)), ((), ()))
TN = (((0,), (0,)), ((), ()))


def dot(a, b, dims, precision=None):
    return lax.dot_general(a, b, dims, precision=precision, preferred_element_type=F32)


SPACES = {"s": pltpu.SMEM, "h": pltpu.HBM, "v": pltpu.VMEM, "a": pl.ANY}


def call(kernel, outs, args, flops, bytes_accessed, scratch=(), aliases=()):
    return pl.pallas_call(
        kernel,
        out_shape=[SPACES[m](s, d) for m, s, d in outs],
        in_specs=[pl.BlockSpec(memory_space=SPACES[m]) for m, _ in args],
        out_specs=[pl.BlockSpec(memory_space=SPACES[m]) for m, _, _ in outs],
        scratch_shapes=list(scratch),
        input_output_aliases=dict(aliases),
        compiler_params=pltpu.CompilerParams(vmem_limit_bytes=VMEM_LIMIT),
        cost_estimate=pl.CostEstimate(
            flops=flops, bytes_accessed=bytes_accessed, transcendentals=0
        ),
    )(*[pltpu.with_memory_space_constraint(a, SPACES[m]) if m in "hv" else a for m, a in args])


def head_cols(h):
    return slice(h * HEAD, (h + 1) * HEAD)


def head_rows(h):
    return slice(h * HEAD, (h + 1) * HEAD)


def local_kernel(
    q_hbm, k_hbm, v_hbm, g_hbm, decay_hbm, gain_hbm,
    pay_ref, kept_ref, inside_ref, across_ref, key_ref, q_ref, k_ref, v_ref, g_ref, gain_ref, decay_ref, sems,
):
    heads, rows = decay_ref.shape
    pieces = [
        (decay_hbm, decay_ref), (k_hbm, k_ref), (v_hbm, v_ref), (q_hbm, q_ref), (g_hbm, g_ref), (gain_hbm, gain_ref)
    ]
    copies = [pltpu.make_async_copy(*piece, sems.at[i]) for i, piece in enumerate(pieces)]
    for copy in copies:
        copy.start()
    first = lax.broadcasted_iota(jnp.int32, (rows, rows), 0)
    second = lax.broadcasted_iota(jnp.int32, (rows, rows), 1)
    copies[0].wait()
    decay = decay_ref[...]
    high = decay.astype(BF16)
    rest = decay - high.astype(F32)
    middle = rest.astype(BF16)
    low = (rest - middle.astype(F32)).astype(BF16)
    terms = jnp.concatenate([high, middle, low], axis=0)
    sums = dot(terms, (first <= second).astype(BF16), NN)
    across = sums[:heads] + (sums[heads : 2 * heads] + sums[2 * heads :])
    sums = dot((first >= second).astype(BF16), terms, NT)
    inside = sums[:, :heads] + (sums[:, heads : 2 * heads] + sums[:, 2 * heads :])
    inside_ref[...] = inside
    across_ref[...] = across
    shares = jnp.exp(inside[rows - 1 : rows, :] - inside)
    kept = jnp.broadcast_to(jnp.exp(across[:, rows - 1 : rows]), (heads, HEAD))
    kept_ref[...] = kept
    pay_ref[heads * HEAD :, :] = kept
    for h in range(heads):
        if h == 0:
            copies[1].wait()
            copies[2].wait()
        cols = head_cols(h)
        key_decayed = (k_ref[:, cols].astype(F32) * shares[:, h : h + 1]).astype(BF16)
        key_ref[:, cols] = key_decayed
        pay_ref[head_rows(h), :] = dot(key_decayed, v_ref[:, cols], TN)
    for copy in copies[3:]:
        copy.wait()


def forward_join_kernel(core_ref, after_ref, own_ref, other_ref, pay_ref):
    half = pay_ref.shape[0] // 17 * 16 // HEAD
    core = core_ref[0]
    base = pl.multiple_of(core * half * HEAD, half * HEAD)
    kept_own = own_ref[2 * half * HEAD :, :]
    kept_other = other_ref[2 * half * HEAD :, :]
    kept_both = kept_own * kept_other
    kept_second = jnp.where(core == 0, kept_other, kept_own)

    def half_of(rows, i):
        return jnp.where(core == 0, rows[i : i + 1], rows[half + i : half + i + 1])

    for i in range(half):
        here = pl.ds(base + i * HEAD, HEAD)
        own, other = own_ref[here, :], other_ref[here, :]
        first = jnp.where(core == 0, own, other)
        second = jnp.where(core == 0, other, own)
        joined = half_of(kept_second, i) * first + second
        kept = half_of(kept_both, i)
        for part in range(8):
            at = 17 * (8 * i + part)
            pay_ref[at : at + 16, :] = joined[16 * part : 16 * part + 16]
            pay_ref[at + 16 : at + 17, :] = kept


def forward_scan_kernel(got_ref, out_ref, kept_ref):
    count = out_ref.shape[0]
    state = jnp.zeros(out_ref.shape[1:], F32)
    for j in range(count):
        out_ref[j] = state
        kept = got_ref[17 * j + 16 : 17 * j + 17, :]
        kept_ref[j : j + 1, :] = kept
        state = kept * state + got_ref[17 * j : 17 * j + 16, :]


def reverse_join_kernel(core_ref, after_hbm, own_ref, other_ref, kept_own_ref, got_ref, out_ref):
    half = own_ref.shape[0] // HEAD // 2
    core = core_ref[0]
    base = pl.multiple_of(core * half * HEAD, half * HEAD)
    kept_first = jnp.where(core == 0, kept_own_ref[...], got_ref[2 * half * HEAD :, :])
    for i in range(half):
        here = pl.ds(base + i * HEAD, HEAD)
        own, other = own_ref[here, :], other_ref[here, :]
        first = jnp.where(core == 0, own, other)
        second = jnp.where(core == 0, other, own)
        kept = jnp.where(core == 0, kept_first[i : i + 1], kept_first[half + i : half + i + 1])
        out_ref[head_rows(i), :] = first + kept * second


def reverse_scan_kernel(got_ref, kept_ref, out_ref):
    count = out_ref.shape[0]
    state = jnp.zeros(out_ref.shape[1:], F32)
    for j in reversed(range(count)):
        out_ref[j] = state
        state = kept_ref[j : j + 1, :] * state + got_ref[j]


def weights_of(inside_ref, across_ref, h, transposed=False):
    rows = inside_ref.shape[0]
    first = lax.broadcasted_iota(jnp.int32, (rows, rows), 0)
    second = lax.broadcasted_iota(jnp.int32, (rows, rows), 1)
    if transposed:
        spread = across_ref[h : h + 1, :] - inside_ref[:, h : h + 1]
        return jnp.exp(jnp.where(second >= first, spread, -1e30))
    spread = inside_ref[:, h : h + 1] - across_ref[h : h + 1, :]
    return jnp.exp(jnp.where(first >= second, spread, -1e30))


def mixing_kernel(
    q_ref, k_ref, v_ref, g_ref, gain_ref, inside_ref, across_ref,
    near_ref, mix_turned_ref, query_ref, query_turned_ref, weights_ref, weights_turned_ref, scaled_ref,
):
    grown = jnp.exp(inside_ref[...])
    for h in range(inside_ref.shape[1]):
        cols = head_cols(h)
        queries, keys = q_ref[:, cols], k_ref[:, cols]
        weights = weights_of(inside_ref, across_ref, h)
        weights_ref[h] = weights
        mixing = (dot(queries, keys, NT) * weights).astype(BF16)
        near_ref[:, cols] = dot(mixing, v_ref[:, cols], NN)
        weights_turned = weights_of(inside_ref, across_ref, h, True)
        weights_turned_ref[h] = weights_turned
        mix_turned_ref[h] = (dot(keys, queries, NT) * weights_turned).astype(BF16)
        decayed = queries.astype(F32) * grown[:, h : h + 1]
        query_ref[:, cols] = decayed.astype(BF16)
        query_turned_ref[h] = decayed.T.astype(BF16)
        scaled_ref[:, cols] = g_ref[:, cols].astype(F32) * gain_ref[:, cols]


def attend_half(
    base, core, near_ref, query_ref, half_ref, got_ref, scaled_ref, att_ref, entering_ref, squares, crossed
):
    heads = entering_ref.shape[0]
    for i in range(heads // 2):
        h = base + i
        cols = pl.ds(pl.multiple_of(h * HEAD, HEAD), HEAD)
        kept = got_ref[pl.ds(heads * HEAD + h, 1), :]
        state = half_ref[i]
        state = jnp.where(core == 0, state, kept * state + got_ref[cols, :]).astype(BF16)
        entering_ref[h] = state
        attended = near_ref[:, cols] + dot(query_ref[:, cols], state, NN)
        att_ref[:, cols] = attended
        squares += attended * attended
        crossed += scaled_ref[:, cols] * attended
    return squares, crossed


def attend_own_kernel(
    core_ref, near_ref, query_ref, half_ref, got_ref, scaled_ref, att_ref, entering_ref, squares_ref, crossed_ref
):
    core = core_ref[0]
    zero = jnp.zeros(squares_ref.shape, F32)
    squares_ref[...], crossed_ref[...] = attend_half(
        core * (entering_ref.shape[0] // 2), core, near_ref, query_ref, half_ref, got_ref, scaled_ref,
        att_ref, entering_ref, zero, zero,
    )


def attend_other_kernel(
    core_ref, near_ref, query_ref, half_ref, got_ref, scaled_ref, squares_ref, crossed_ref,
    att_in_ref, entering_in_ref, att_ref, entering_ref, sums_ref,
):
    core = core_ref[0]
    squares, crossed = attend_half(
        (1 - core) * (entering_ref.shape[0] // 2), core, near_ref, query_ref, half_ref, got_ref, scaled_ref,
        att_ref, entering_ref, squares_ref[...], crossed_ref[...],
    )
    sums = jnp.concatenate(
        [jnp.sum(squares, axis=1, keepdims=True), jnp.sum(crossed, axis=1, keepdims=True)], axis=1
    ).T
    for peer in range(sums_ref.shape[0]):
        sums_ref[peer] = sums


def norm_columns(sums_ref, rows):
    whole = jnp.sum(sums_ref[...], axis=0)
    first = lax.broadcasted_iota(jnp.int32, (rows, rows), 0)
    second = lax.broadcasted_iota(jnp.int32, (rows, rows), 1)
    same = first == second
    square_sum = jnp.sum(jnp.where(same, whole[0:1, :], 0.0), axis=1, keepdims=True)
    cross_sum = jnp.sum(jnp.where(same, whole[1:2, :], 0.0), axis=1, keepdims=True)
    width = HEAD_COUNT * HEAD
    inverse = lax.rsqrt(square_sum / width + EPSILON)
    return inverse, inverse * inverse * inverse * (cross_sum / width)


def norm_grad_kernel(sums_ref, att_ref, scaled_ref, query_turned_ref, pay_ref, gf_ref):
    rows, width = att_ref.shape
    inverse, factor = norm_columns(sums_ref, rows)
    for h in range(width // HEAD):
        cols = head_cols(h)
        grad_flat = (inverse * scaled_ref[:, cols] - att_ref[:, cols] * factor).astype(BF16)
        gf_ref[:, cols] = grad_flat
        pay_ref[head_rows(h), :] = dot(query_turned_ref[h], grad_flat, NN)


def send_out(copies, source, target, sems, i, cols):
    copy = pltpu.make_async_copy(source.at[:, cols], target.at[:, cols], sems.at[i])
    copy.start()
    copies.append(copy)


def near_query_kernel(
    sums_ref, att_ref, gain_ref, gf_ref, k_ref, v_ref, state_ref, inside_ref, weights_ref,
    normed_hbm, gq_hbm, normed_ref, gq_ref, sems,
):
    rows, heads = inside_ref.shape
    inverse, _ = norm_columns(sums_ref, rows)
    grown = jnp.exp(inside_ref[...])
    copies = []
    for h in range(heads):
        cols = head_cols(h)
        normed_ref[:, cols] = (att_ref[:, cols] * inverse * gain_ref[:, cols]).astype(BF16)
        grad_flat = gf_ref[:, cols]
        grad_mix = (dot(grad_flat, v_ref[:, cols], NT) * weights_ref[h]).astype(BF16)
        far = dot(grad_flat, state_ref[h], NT)
        gq_ref[:, cols] = (dot(grad_mix, k_ref[:, cols], NN) + grown[:, h : h + 1] * far).astype(BF16)
        if h % 2:
            pair = slice((h - 1) * HEAD, (h + 1) * HEAD)
            send_out(copies, normed_ref, normed_hbm, sems, h - 1, pair)
            send_out(copies, gq_ref, gq_hbm, sems, h, pair)
    for copy in copies:
        copy.wait()


def near_key_kernel(gf_ref, q_ref, v_ref, mix_turned_ref, weights_turned_ref, gk_ref, gv_ref):
    for h in range(mix_turned_ref.shape[0]):
        cols = head_cols(h)
        grad_flat = gf_ref[:, cols]
        turned = (dot(v_ref[:, cols], grad_flat, NT) * weights_turned_ref[h]).astype(BF16)
        gk_ref[:, cols] = dot(turned, q_ref[:, cols], NN)
        gv_ref[:, cols] = dot(mix_turned_ref[h], grad_flat, NN)


def far_grad_kernel(
    core_ref, gk_near_ref, gv_near_ref, key_ref, v_ref, half_ref, half_other_ref, other_ref, kept_got_ref,
    inside_ref, gk_hbm, gv_hbm, state_ref, gk_ref, gv_ref, sems,
):
    rows, heads = inside_ref.shape
    half = heads // 2
    core = core_ref[0]
    state_ref[pl.ds(core * half, half)] = half_ref[...]
    state_ref[pl.ds((1 - core) * half, half)] = half_other_ref[...]

    @pl.when(core == 0)
    def _():
        for h in range(heads):
            kept = kept_got_ref[heads * HEAD + h : heads * HEAD + h + 1, :]
            state_ref[h] = kept * state_ref[h] + other_ref[head_rows(h), :]

    inside = inside_ref[...]
    shares = jnp.exp(inside[rows - 1 : rows, :] - inside)
    copies = []
    for h in range(heads):
        cols = head_cols(h)
        arriving = state_ref[h].astype(BF16)
        far = dot(v_ref[:, cols], arriving, NT)
        gk_ref[:, cols] = (gk_near_ref[:, cols] + shares[:, h : h + 1] * far).astype(BF16)
        gv_ref[:, cols] = (gv_near_ref[:, cols] + dot(key_ref[:, cols], arriving, NN)).astype(BF16)
        if h % 2:
            pair = slice((h - 1) * HEAD, (h + 1) * HEAD)
            send_out(copies, gk_ref, gk_hbm, sems, h - 1, pair)
            send_out(copies, gv_ref, gv_hbm, sems, h, pair)
    for copy in copies:
        copy.wait()


def body(chips, tp_size, queries, key_vectors, values, decay_log, norm_gain, grad_out):
    rows, width = queries.shape
    heads = decay_log.shape[1]
    half = heads // 2
    slab = half * HEAD // chips
    core = lax.axis_index("core").astype(jnp.int32).reshape(1)
    gain = norm_gain.reshape(1, width)
    wide, tile = (rows, width), (chips, slab, HEAD)
    state_rows, half_state = (heads * HEAD, HEAD), (half, HEAD, HEAD)
    whole, size = rows * width, heads * HEAD * HEAD

    def across_chips(array):
        return lax.all_to_all(array, ("x", "y"), 0, 0)

    def swap(array):
        return lax.ppermute(array, "core", [(0, 1), (1, 0)])

    wide_bf, wide_f32 = ("v", wide, BF16), ("v", wide, F32)
    square, per_token = (heads, rows, rows), ("v", (rows, heads), F32)
    inputs = [queries, key_vectors, values, grad_out, decay_log.T, gain]
    own, kept_own, inside, across, key_decayed, q, k, v, g, gain = call(
        local_kernel,
        [
            ("v", (heads * HEAD + heads, HEAD), F32), ("v", (heads, HEAD), F32), per_token,
            ("v", (heads, rows), F32), wide_bf, wide_bf, wide_bf, wide_bf, wide_bf, ("v", (1, width), F32),
        ],
        [("h", a) for a in inputs],
        2 * whole * HEAD, 8 * whole,
        scratch=[pltpu.VMEM((heads, rows), F32), pltpu.SemaphoreType.DMA((6,))],
    )
    got = swap(own)
    near, mixing_turned, query_decayed, query_turned, weights, weights_turned, scaled = call(
        mixing_kernel,
        [
            wide_f32, ("v", square, BF16), wide_bf, ("v", (heads, HEAD, rows), BF16), ("v", square, F32),
            ("v", square, F32), wide_f32,
        ],
        [("v", a) for a in (q, k, v, g, gain, inside, across)],
        6 * whole * rows, 12 * whole,
    )
    (pay,) = call(
        forward_join_kernel,
        [("v", (chips * (slab + 1), HEAD), F32)],
        [("s", core), ("a", query_decayed), ("v", own), ("v", got)],
        2 * size, 12 * size,
    )
    pay = across_chips(pay.reshape(chips, 1, (slab + 1) * HEAD)).reshape(chips * (slab + 1), HEAD)
    tiles, kept_chips = call(
        forward_scan_kernel,
        [("v", tile, F32), ("v", (chips, HEAD), F32)],
        [("v", pay)],
        size, 4 * size,
    )
    half_in = across_chips(tiles).reshape(half_state)
    half_other = swap(half_in)
    entering_bf, column = ("v", (heads, HEAD, HEAD), BF16), ("v", (rows, HEAD), F32)
    attended, entering, squares, crossed = call(
        attend_own_kernel,
        [wide_f32, entering_bf, column, column],
        [("s", core)] + [("v", a) for a in (near, query_decayed, half_in, got, scaled)],
        whole * HEAD, 6 * whole,
    )
    other_args = (near, query_decayed, half_other, got, scaled, squares, crossed, attended, entering)
    attended, entering, sums = call(
        attend_other_kernel,
        [wide_f32, entering_bf, ("v", (tp_size, 2, rows), F32)],
        [("s", core)] + [("v", a) for a in other_args],
        whole * HEAD, 6 * whole, aliases={8: 0, 9: 1},
    )
    sums = lax.all_to_all(sums, "tp", 0, 0)
    back, grad_flat = call(
        norm_grad_kernel,
        [("v", state_rows, F32), wide_bf],
        [("v", a) for a in (sums, attended, scaled, query_turned)],
        2 * whole * HEAD, 12 * whole,
    )
    back_other = swap(back)
    outputs = [pltpu.VMEM(wide, BF16), pltpu.VMEM(wide, BF16), pltpu.SemaphoreType.DMA((heads,))]
    normed, grad_query = call(
        near_query_kernel,
        [("h", wide, BF16), ("h", wide, BF16)],
        [("v", a) for a in (sums, attended, gain, grad_flat, k, v, entering, inside, weights)],
        6 * whole * rows, 16 * whole, scratch=outputs,
    )
    (pay_back,) = call(
        reverse_join_kernel,
        [("v", (half * HEAD, HEAD), F32)],
        [("s", core), ("h", grad_query)] + [("v", a) for a in (back, back_other, kept_own, got)],
        2 * size, 12 * size,
    )
    grad_key_near, grad_value_near = call(
        near_key_kernel,
        [wide_f32, wide_f32],
        [("v", a) for a in (grad_flat, q, v, mixing_turned, weights_turned)],
        6 * whole * rows, 16 * whole,
    )
    (tiles_back,) = call(
        reverse_scan_kernel,
        [("v", tile, F32)],
        [("v", across_chips(pay_back.reshape(tile))), ("v", kept_chips)],
        size, 4 * size,
    )
    half_back = across_chips(tiles_back).reshape(half_state)
    half_back_other = swap(half_back)
    far_args = (
        grad_key_near, grad_value_near, key_decayed, v, half_back, half_back_other, back_other, got, inside
    )
    grad_key, grad_value = call(
        far_grad_kernel,
        [("h", wide, BF16), ("h", wide, BF16)],
        [("s", core)] + [("v", a) for a in far_args],
        4 * whole * HEAD, 16 * whole,
        scratch=[pltpu.VMEM((heads, HEAD, HEAD), F32), *outputs],
    )
    return normed, grad_query, grad_key, grad_value


def solution(mesh):
    seq, tp = mesh.shape["seq"], mesh.shape["tp"]
    fine = Mesh(mesh.devices.reshape(seq // 16, 8, 2, tp), ("x", "y", "core", "tp"))
    spec = P(("x", "y", "core"), "tp")
    return jax.shard_map(
        functools.partial(body, seq // 2, tp),
        mesh=fine,
        in_specs=(spec, spec, spec, spec, P("tp"), spec),
        out_specs=(spec, spec, spec, spec),
        check_vma=False,
    )
```

```python
import functools

import jax
import jax.numpy as jnp
from jax import lax
from jax.experimental import pallas as pl
from jax.experimental.pallas import tpu as pltpu
from jax.sharding import Mesh
from jax.sharding import PartitionSpec as P

HEAD_COUNT = 64
HEAD = 128
EPSILON = 1e-06
HIGH = lax.Precision.HIGHEST
F32 = jnp.float32
BF16 = jnp.bfloat16
VMEM_LIMIT = 20 * 1024 * 1024
NN = (((1,), (0,)), ((), ()))
NT = (((1,), (1,)), ((), ()))
TN = (((0,), (0,)), ((), ()))


def dot(a, b, dims, precision=None):
    return lax.dot_general(a, b, dims, precision=precision, preferred_element_type=F32)


SPACES = {"s": pltpu.SMEM, "h": pltpu.HBM, "v": pltpu.VMEM, "a": pl.ANY}


def call(kernel, outs, args, flops, bytes_accessed, scratch=(), aliases=()):
    return pl.pallas_call(
        kernel,
        out_shape=[SPACES[m](s, d) for m, s, d in outs],
        in_specs=[pl.BlockSpec(memory_space=SPACES[m]) for m, _ in args],
        out_specs=[pl.BlockSpec(memory_space=SPACES[m]) for m, _, _ in outs],
        scratch_shapes=list(scratch),
        input_output_aliases=dict(aliases),
        compiler_params=pltpu.CompilerParams(vmem_limit_bytes=VMEM_LIMIT),
        cost_estimate=pl.CostEstimate(
            flops=flops, bytes_accessed=bytes_accessed, transcendentals=0
        ),
    )(*[pltpu.with_memory_space_constraint(a, SPACES[m]) if m in "hv" else a for m, a in args])


def head_cols(h):
    return slice(h * HEAD, (h + 1) * HEAD)


def head_rows(h):
    return slice(h * HEAD, (h + 1) * HEAD)


def deal_halves(core, state_of, half, keep_ref, send_ref):
    for i in range(half):
        low, high = state_of(i), state_of(half + i)
        keep_ref[head_rows(i), :] = jnp.where(core == 0, low, high)
        send_ref[head_rows(i), :] = jnp.where(core == 0, high, low)


def local_kernel(
    core_ref, q_hbm, k_hbm, v_hbm, g_hbm, decay_hbm, gain_hbm,
    keep_ref, send_ref, kept_ref, inside_ref, across_ref, key_ref, q_ref, k_ref, v_ref, g_ref, gain_ref, decay_ref, sems,
):
    heads, rows = decay_ref.shape
    pieces = [
        (decay_hbm, decay_ref), (k_hbm, k_ref), (v_hbm, v_ref), (q_hbm, q_ref), (g_hbm, g_ref), (gain_hbm, gain_ref)
    ]
    copies = [pltpu.make_async_copy(*piece, sems.at[i]) for i, piece in enumerate(pieces)]
    for copy in copies:
        copy.start()
    first = lax.broadcasted_iota(jnp.int32, (rows, rows), 0)
    second = lax.broadcasted_iota(jnp.int32, (rows, rows), 1)
    copies[0].wait()
    decay = decay_ref[...]
    high = decay.astype(BF16)
    rest = decay - high.astype(F32)
    middle = rest.astype(BF16)
    low = (rest - middle.astype(F32)).astype(BF16)
    terms = jnp.concatenate([high, middle, low], axis=0)
    sums = dot(terms, (first <= second).astype(BF16), NN)
    across = sums[:heads] + (sums[heads : 2 * heads] + sums[2 * heads :])
    sums = dot((first >= second).astype(BF16), terms, NT)
    inside = sums[:, :heads] + (sums[:, heads : 2 * heads] + sums[:, 2 * heads :])
    inside_ref[...] = inside
    across_ref[...] = across
    shares = jnp.exp(inside[rows - 1 : rows, :] - inside)
    kept = jnp.broadcast_to(jnp.exp(across[:, rows - 1 : rows]), (heads, HEAD))
    kept_ref[...] = kept
    send_ref[heads // 2 * HEAD :, :] = kept
    copies[1].wait()
    copies[2].wait()

    def state_of(h):
        cols = head_cols(h)
        key_decayed = (k_ref[:, cols].astype(F32) * shares[:, h : h + 1]).astype(BF16)
        key_ref[:, cols] = key_decayed
        return dot(key_decayed, v_ref[:, cols], TN)

    deal_halves(core_ref[0], state_of, heads // 2, keep_ref, send_ref)
    for copy in copies[3:]:
        copy.wait()


def kept_rows(core, own_ref, got_ref, i):
    half = got_ref.shape[0] // (HEAD + 2)
    at = got_ref.shape[0] - 2 * half
    own = jnp.where(core == 0, own_ref[i : i + 1, :], own_ref[half + i : half + i + 1, :])
    got = jnp.where(core == 0, got_ref[at + i : at + i + 1, :], got_ref[at + half + i : at + half + i + 1, :])
    return jnp.where(core == 0, own, got), jnp.where(core == 0, got, own)


def in_order(core, own, got):
    return jnp.where(core == 0, own, got), jnp.where(core == 0, got, own)


def forward_join_kernel(core_ref, after_ref, keep_ref, got_ref, kept_ref, pay_ref):
    core = core_ref[0]
    for i in range(keep_ref.shape[0] // HEAD):
        first, second = in_order(core, keep_ref[head_rows(i), :], got_ref[head_rows(i), :])
        kept_first, kept_second = kept_rows(core, kept_ref, got_ref, i)
        joined = kept_second * first + second
        for part in range(8):
            at = 17 * (8 * i + part)
            pay_ref[at : at + 16, :] = joined[16 * part : 16 * part + 16]
            pay_ref[at + 16 : at + 17, :] = kept_first * kept_second


def forward_scan_kernel(got_ref, out_ref, kept_ref):
    count = out_ref.shape[0]
    state = jnp.zeros(out_ref.shape[1:], F32)
    for j in range(count):
        out_ref[j] = state
        kept = got_ref[17 * j + 16 : 17 * j + 17, :]
        kept_ref[j : j + 1, :] = kept
        state = kept * state + got_ref[17 * j : 17 * j + 16, :]


def reverse_join_kernel(core_ref, after_ref, keep_ref, got_ref, kept_ref, got_kept_ref, out_ref):
    core = core_ref[0]
    for i in range(keep_ref.shape[0] // HEAD):
        first, second = in_order(core, keep_ref[head_rows(i), :], got_ref[head_rows(i), :])
        kept_first, _ = kept_rows(core, kept_ref, got_kept_ref, i)
        out_ref[head_rows(i), :] = first + kept_first * second


def reverse_scan_kernel(got_ref, kept_ref, out_ref):
    count = out_ref.shape[0]
    state = jnp.zeros(out_ref.shape[1:], F32)
    for j in reversed(range(count)):
        out_ref[j] = state
        state = kept_ref[j : j + 1, :] * state + got_ref[j]


def weights_of(inside_ref, across_ref, h, transposed=False):
    rows = inside_ref.shape[0]
    first = lax.broadcasted_iota(jnp.int32, (rows, rows), 0)
    second = lax.broadcasted_iota(jnp.int32, (rows, rows), 1)
    if transposed:
        spread = across_ref[h : h + 1, :] - inside_ref[:, h : h + 1]
        return jnp.exp(jnp.where(second >= first, spread, -1e30))
    spread = inside_ref[:, h : h + 1] - across_ref[h : h + 1, :]
    return jnp.exp(jnp.where(first >= second, spread, -1e30))


def mixing_of(
    q_ref, k_ref, v_ref, g_ref, gain_ref, inside_ref, across_ref,
    near_ref, mix_turned_ref, query_ref, query_turned_ref, weights_ref, weights_turned_ref, scaled_ref,
):
    grown = jnp.exp(inside_ref[...])
    for h in range(inside_ref.shape[1]):
        cols = head_cols(h)
        queries, keys = q_ref[:, cols], k_ref[:, cols]
        weights = weights_of(inside_ref, across_ref, h)
        weights_ref[h] = weights
        mixing = (dot(queries, keys, NT) * weights).astype(BF16)
        near_ref[:, cols] = dot(mixing, v_ref[:, cols], NN)
        weights_turned = weights_of(inside_ref, across_ref, h, True)
        weights_turned_ref[h] = weights_turned
        mix_turned_ref[h] = (dot(keys, queries, NT) * weights_turned).astype(BF16)
        decayed = queries.astype(F32) * grown[:, h : h + 1]
        query_ref[:, cols] = decayed.astype(BF16)
        query_turned_ref[h] = decayed.T.astype(BF16)
        scaled_ref[:, cols] = g_ref[:, cols].astype(F32) * gain_ref[:, cols]


def mixing_first_kernel(core_ref, *refs):
    @pl.when(core_ref[0] == 0)
    def _():
        mixing_of(*refs)


def enter_kernel(core_ref, half_ref, keep_ref, got_ref, kept_ref, *refs):
    inputs, (own_ref, send_ref, *outputs) = refs[:7], refs[14:]
    core = core_ref[0]
    for i in range(half_ref.shape[0]):
        kept_first, _ = kept_rows(core, kept_ref, got_ref, i)
        first, _ = in_order(core, keep_ref[head_rows(i), :], got_ref[head_rows(i), :])
        state = half_ref[i]
        later = kept_first * state + first
        own_ref[i] = jnp.where(core == 0, state, later)
        send_ref[i] = jnp.where(core == 0, later, state)

    @pl.when(core == 1)
    def _():
        mixing_of(*inputs, *outputs)


def attend_half(base, near_ref, query_ref, half_ref, scaled_ref, att_ref, entering_ref, squares, crossed):
    for i in range(half_ref.shape[0]):
        h = base + i
        cols = pl.ds(pl.multiple_of(h * HEAD, HEAD), HEAD)
        state = half_ref[i].astype(BF16)
        entering_ref[h] = state
        attended = near_ref[:, cols] + dot(query_ref[:, cols], state, NN)
        att_ref[:, cols] = attended
        squares += attended * attended
        crossed += scaled_ref[:, cols] * attended
    return squares, crossed


def attend_own_kernel(
    core_ref, near_ref, query_ref, half_ref, scaled_ref, att_ref, entering_ref, squares_ref, crossed_ref
):
    zero = jnp.zeros(squares_ref.shape, F32)
    squares_ref[...], crossed_ref[...] = attend_half(
        core_ref[0] * half_ref.shape[0], near_ref, query_ref, half_ref, scaled_ref, att_ref, entering_ref, zero, zero
    )


def attend_other_kernel(
    core_ref, near_ref, query_ref, half_ref, scaled_ref, squares_ref, crossed_ref,
    att_in_ref, entering_in_ref, att_ref, entering_ref, sums_ref,
):
    squares, crossed = attend_half(
        (1 - core_ref[0]) * half_ref.shape[0], near_ref, query_ref, half_ref, scaled_ref, att_ref, entering_ref,
        squares_ref[...], crossed_ref[...],
    )
    sums = jnp.concatenate(
        [jnp.sum(squares, axis=1, keepdims=True), jnp.sum(crossed, axis=1, keepdims=True)], axis=1
    ).T
    for peer in range(sums_ref.shape[0]):
        sums_ref[peer] = sums


def norm_columns(sums_ref, rows):
    whole = jnp.sum(sums_ref[...], axis=0)
    first = lax.broadcasted_iota(jnp.int32, (rows, rows), 0)
    second = lax.broadcasted_iota(jnp.int32, (rows, rows), 1)
    same = first == second
    square_sum = jnp.sum(jnp.where(same, whole[0:1, :], 0.0), axis=1, keepdims=True)
    cross_sum = jnp.sum(jnp.where(same, whole[1:2, :], 0.0), axis=1, keepdims=True)
    width = HEAD_COUNT * HEAD
    inverse = lax.rsqrt(square_sum / width + EPSILON)
    return inverse, inverse * inverse * inverse * (cross_sum / width)


def norm_grad_kernel(core_ref, sums_ref, att_ref, scaled_ref, query_turned_ref, keep_ref, send_ref, gf_ref):
    rows, width = att_ref.shape
    inverse, factor = norm_columns(sums_ref, rows)

    def state_of(h):
        cols = head_cols(h)
        grad_flat = (inverse * scaled_ref[:, cols] - att_ref[:, cols] * factor).astype(BF16)
        gf_ref[:, cols] = grad_flat
        return dot(query_turned_ref[h], grad_flat, NN)

    deal_halves(core_ref[0], state_of, width // HEAD // 2, keep_ref, send_ref)


def send_out(copies, source, target, sems, i, cols):
    copy = pltpu.make_async_copy(source.at[:, cols], target.at[:, cols], sems.at[i])
    copy.start()
    copies.append(copy)


def near_grad(
    sums_ref, att_ref, gain_ref, gf_ref, q_ref, k_ref, v_ref, state_ref, inside_ref, weights_ref,
    weights_turned_ref, mix_turned_ref, normed_hbm, gq_hbm, gk_ref, gv_ref, normed_ref, gq_ref, sems,
):
    rows, heads = inside_ref.shape
    inverse, _ = norm_columns(sums_ref, rows)
    grown = jnp.exp(inside_ref[...])
    copies = []
    for h in range(heads):
        cols = head_cols(h)
        normed_ref[:, cols] = (att_ref[:, cols] * inverse * gain_ref[:, cols]).astype(BF16)
        grad_flat = gf_ref[:, cols]
        grad_mix = (dot(grad_flat, v_ref[:, cols], NT) * weights_ref[h]).astype(BF16)
        far = dot(grad_flat, state_ref[h], NT)
        gq_ref[:, cols] = (dot(grad_mix, k_ref[:, cols], NN) + grown[:, h : h + 1] * far).astype(BF16)
        if h % 2:
            pair = slice((h - 1) * HEAD, (h + 1) * HEAD)
            send_out(copies, normed_ref, normed_hbm, sems, h - 1, pair)
            send_out(copies, gq_ref, gq_hbm, sems, h, pair)
    for h in range(heads):
        cols = head_cols(h)
        grad_flat = gf_ref[:, cols]
        turned = (dot(v_ref[:, cols], grad_flat, NT) * weights_turned_ref[h]).astype(BF16)
        gk_ref[:, cols] = dot(turned, q_ref[:, cols], NN)
        gv_ref[:, cols] = dot(mix_turned_ref[h], grad_flat, NN)
    for copy in copies:
        copy.wait()


def near_first_kernel(core_ref, *refs):
    @pl.when(core_ref[0] == 0)
    def _():
        near_grad(*refs)


def leave_kernel(core_ref, half_ref, keep_ref, got_ref, kept_ref, got_kept_ref, *refs):
    inputs, (own_ref, send_ref, *outputs) = refs[:12], refs[16:]
    core = core_ref[0]
    for i in range(half_ref.shape[0]):
        _, kept_second = kept_rows(core, kept_ref, got_kept_ref, i)
        _, second = in_order(core, keep_ref[head_rows(i), :], got_ref[head_rows(i), :])
        state = half_ref[i]
        earlier = second + kept_second * state
        own_ref[i] = jnp.where(core == 0, earlier, state)
        send_ref[i] = jnp.where(core == 0, state, earlier)

    @pl.when(core == 1)
    def _():
        near_grad(*inputs, *outputs)


def far_half(
    base, gk_near_ref, gv_near_ref, key_ref, v_ref, half_ref, inside_ref, gk_hbm, gv_hbm, gk_ref, gv_ref, sems
):
    rows, heads = inside_ref.shape
    inside = inside_ref[...]
    shares = jnp.exp(inside[rows - 1 : rows, :] - inside)
    head = lax.broadcasted_iota(jnp.int32, (rows, heads), 1)
    copies = []
    for i in range(half_ref.shape[0]):
        cols = pl.ds(pl.multiple_of((base + i) * HEAD, HEAD), HEAD)
        share = jnp.sum(jnp.where(head == base + i, shares, 0.0), axis=1, keepdims=True)
        arriving = half_ref[i].astype(BF16)
        far = dot(v_ref[:, cols], arriving, NT)
        gk_ref[:, cols] = (gk_near_ref[:, cols] + share * far).astype(BF16)
        gv_ref[:, cols] = (gv_near_ref[:, cols] + dot(key_ref[:, cols], arriving, NN)).astype(BF16)
        if i % 2:
            pair = pl.ds(pl.multiple_of((base + i - 1) * HEAD, 2 * HEAD), 2 * HEAD)
            send_out(copies, gk_ref, gk_hbm, sems, i - 1, pair)
            send_out(copies, gv_ref, gv_hbm, sems, i, pair)
    for copy in copies:
        copy.wait()


def far_own_kernel(core_ref, gk_near_ref, gv_near_ref, key_ref, v_ref, half_ref, inside_ref, *refs):
    base = core_ref[0] * half_ref.shape[0]
    far_half(base, gk_near_ref, gv_near_ref, key_ref, v_ref, half_ref, inside_ref, *refs)


def far_other_kernel(core_ref, gk_near_ref, gv_near_ref, key_ref, v_ref, half_ref, inside_ref, gk_in, gv_in, *refs):
    base = (1 - core_ref[0]) * half_ref.shape[0]
    far_half(base, gk_near_ref, gv_near_ref, key_ref, v_ref, half_ref, inside_ref, *refs)


def body(chips, tp_size, queries, key_vectors, values, decay_log, norm_gain, grad_out):
    rows, width = queries.shape
    heads = decay_log.shape[1]
    half = heads // 2
    slab = half * HEAD // chips
    core = lax.axis_index("core").astype(jnp.int32).reshape(1)
    gain = norm_gain.reshape(1, width)
    wide, tile, half_state = (rows, width), (chips, slab, HEAD), (half, HEAD, HEAD)
    whole, size = rows * width, heads * HEAD * HEAD

    def across_chips(array):
        return lax.all_to_all(array, ("x", "y"), 0, 0)

    def swap(array):
        return lax.ppermute(array, "core", [(0, 1), (1, 0)])

    wide_bf, wide_f32 = ("v", wide, BF16), ("v", wide, F32)
    square, per_token = (heads, rows, rows), ("v", (rows, heads), F32)
    half_rows, half_tile = ("v", (half * HEAD, HEAD), F32), ("v", half_state, F32)
    on_core = ("s", core)

    def vmem(*arrays):
        return [("v", a) for a in arrays]

    def like(outs, arrays):
        return [(m, a) for (m, _, _), a in zip(outs, arrays)]

    inputs = [queries, key_vectors, values, grad_out, decay_log.T, gain]
    keep, send, kept, inside, across, key_decayed, q, k, v, g, gain = call(
        local_kernel,
        [
            half_rows, ("v", (half * HEAD + heads, HEAD), F32), ("v", (heads, HEAD), F32), per_token,
            ("v", (heads, rows), F32), wide_bf, wide_bf, wide_bf, wide_bf, wide_bf, ("v", (1, width), F32),
        ],
        [on_core] + [("h", a) for a in inputs],
        2 * whole * HEAD, 8 * whole,
        scratch=[pltpu.VMEM((heads, rows), F32), pltpu.SemaphoreType.DMA((6,))],
    )
    got = swap(send)
    mixing_args = vmem(q, k, v, g, gain, inside, across)
    mixing_outs = [
        wide_f32, ("v", square, BF16), wide_bf, ("v", (heads, HEAD, rows), BF16), ("v", square, F32),
        ("v", square, F32), wide_f32,
    ]
    mixing_done = call(mixing_first_kernel, mixing_outs, [on_core] + mixing_args, 6 * whole * rows, 12 * whole)
    (pay,) = call(
        forward_join_kernel,
        [("v", (chips * (slab + 1), HEAD), F32)],
        [on_core, ("a", mixing_done[0])] + vmem(keep, got, kept),
        2 * size, 12 * size,
    )
    pay = across_chips(pay.reshape(chips, 1, (slab + 1) * HEAD)).reshape(chips * (slab + 1), HEAD)
    tiles, kept_chips = call(
        forward_scan_kernel,
        [("v", tile, F32), ("v", (chips, HEAD), F32)],
        vmem(pay),
        size, 4 * size,
    )
    half_in = across_chips(tiles).reshape(half_state)
    half_own, half_send, near, mixing_turned, query_decayed, query_turned, weights, weights_turned, scaled = call(
        enter_kernel,
        [half_tile, half_tile] + mixing_outs,
        [on_core] + vmem(half_in, keep, got, kept) + mixing_args + like(mixing_outs, mixing_done),
        6 * whole * rows, 12 * whole, aliases={12 + i: 2 + i for i in range(7)},
    )
    half_other = swap(half_send)
    entering_bf, column = ("v", (heads, HEAD, HEAD), BF16), ("v", (rows, HEAD), F32)
    attended, entering, squares, crossed = call(
        attend_own_kernel,
        [wide_f32, entering_bf, column, column],
        [on_core] + vmem(near, query_decayed, half_own, scaled),
        whole * HEAD, 6 * whole,
    )
    attended, entering, sums = call(
        attend_other_kernel,
        [wide_f32, entering_bf, ("v", (tp_size, 2, rows), F32)],
        [on_core] + vmem(near, query_decayed, half_other, scaled, squares, crossed, attended, entering),
        whole * HEAD, 6 * whole, aliases={7: 0, 8: 1},
    )
    sums = lax.all_to_all(sums, "tp", 0, 0)
    back_keep, back_send, grad_flat = call(
        norm_grad_kernel,
        [half_rows, half_rows, wide_bf],
        [on_core] + vmem(sums, attended, scaled, query_turned),
        2 * whole * HEAD, 12 * whole,
    )
    back_got = swap(back_send)
    near_args = vmem(
        sums, attended, gain, grad_flat, q, k, v, entering, inside, weights, weights_turned, mixing_turned
    )
    near_outs = [("h", wide, BF16), ("h", wide, BF16), wide_f32, wide_f32]
    outputs = [pltpu.VMEM(wide, BF16), pltpu.VMEM(wide, BF16), pltpu.SemaphoreType.DMA((heads,))]
    near_done = call(
        near_first_kernel, near_outs, [on_core] + near_args, 12 * whole * rows, 16 * whole, scratch=outputs
    )
    (pay_back,) = call(
        reverse_join_kernel,
        [half_rows],
        [on_core, ("a", near_done[2])] + vmem(back_keep, back_got, kept, got),
        2 * size, 12 * size,
    )
    (tiles_back,) = call(
        reverse_scan_kernel,
        [("v", tile, F32)],
        vmem(across_chips(pay_back.reshape(tile)), kept_chips),
        size, 4 * size,
    )
    half_back = across_chips(tiles_back).reshape(half_state)
    arriving_own, arriving_send, normed, grad_query, grad_key_near, grad_value_near = call(
        leave_kernel,
        [half_tile, half_tile] + near_outs,
        [on_core] + vmem(half_back, back_keep, back_got, kept, got) + near_args + like(near_outs, near_done),
        12 * whole * rows, 16 * whole, scratch=outputs, aliases={18 + i: 2 + i for i in range(4)},
    )
    arriving_other = swap(arriving_send)
    far_outs = [("h", wide, BF16), ("h", wide, BF16)]
    far_args = vmem(grad_key_near, grad_value_near, key_decayed, v)
    far_done = call(
        far_own_kernel, far_outs, [on_core] + far_args + vmem(arriving_own, inside),
        2 * whole * HEAD, 8 * whole, scratch=outputs,
    )
    grad_key, grad_value = call(
        far_other_kernel, far_outs,
        [on_core] + far_args + vmem(arriving_other, inside) + like(far_outs, far_done),
        2 * whole * HEAD, 8 * whole, scratch=outputs, aliases={7: 0, 8: 1},
    )
    return normed, grad_query, grad_key, grad_value


def solution(mesh):
    seq, tp = mesh.shape["seq"], mesh.shape["tp"]
    fine = Mesh(mesh.devices.reshape(seq // 16, 8, 2, tp), ("x", "y", "core", "tp"))
    spec = P(("x", "y", "core"), "tp")
    return jax.shard_map(
        functools.partial(body, seq // 2, tp),
        mesh=fine,
        in_specs=(spec, spec, spec, spec, P("tp"), spec),
        out_specs=(spec, spec, spec, spec),
        check_vma=False,
    )
```

```python
import functools

import jax
import jax.numpy as jnp
from jax import lax
from jax.experimental import pallas as pl
from jax.experimental.pallas import tpu as pltpu
from jax.sharding import Mesh
from jax.sharding import PartitionSpec as P

HEAD_COUNT = 64
HEAD = 128
EPSILON = 1e-06
HIGH = lax.Precision.HIGHEST
F32 = jnp.float32
BF16 = jnp.bfloat16
VMEM_LIMIT = 20 * 1024 * 1024
NN = (((1,), (0,)), ((), ()))
NT = (((1,), (1,)), ((), ()))
TN = (((0,), (0,)), ((), ()))


def dot(a, b, dims, precision=None):
    return lax.dot_general(a, b, dims, precision=precision, preferred_element_type=F32)


SPACES = {"s": pltpu.SMEM, "h": pltpu.HBM, "v": pltpu.VMEM, "a": pl.ANY}


def call(kernel, outs, args, flops, bytes_accessed, scratch=(), aliases=()):
    return pl.pallas_call(
        kernel,
        out_shape=[SPACES[m](s, d) for m, s, d in outs],
        in_specs=[pl.BlockSpec(memory_space=SPACES[m]) for m, _ in args],
        out_specs=[pl.BlockSpec(memory_space=SPACES[m]) for m, _, _ in outs],
        scratch_shapes=list(scratch),
        input_output_aliases=dict(aliases),
        compiler_params=pltpu.CompilerParams(vmem_limit_bytes=VMEM_LIMIT),
        cost_estimate=pl.CostEstimate(
            flops=flops, bytes_accessed=bytes_accessed, transcendentals=0
        ),
    )(*[pltpu.with_memory_space_constraint(a, SPACES[m]) if m in "hv" else a for m, a in args])


def head_cols(h):
    return slice(h * HEAD, (h + 1) * HEAD)


def head_rows(h):
    return slice(h * HEAD, (h + 1) * HEAD)


def deal_halves(core, state_of, half, keep_ref, send_ref):
    for i in range(half):
        low, high = state_of(i), state_of(half + i)
        keep_ref[head_rows(i), :] = jnp.where(core == 0, low, high)
        send_ref[head_rows(i), :] = jnp.where(core == 0, high, low)


def local_kernel(
    core_ref, q_hbm, k_hbm, v_hbm, g_hbm, decay_hbm, gain_hbm,
    keep_ref, send_ref, kept_ref, inside_ref, across_ref, key_ref, q_ref, k_ref, v_ref, g_ref, gain_ref, decay_ref, sems,
):
    heads, rows = decay_ref.shape
    pieces = [
        (decay_hbm, decay_ref), (k_hbm, k_ref), (v_hbm, v_ref), (q_hbm, q_ref), (g_hbm, g_ref), (gain_hbm, gain_ref)
    ]
    copies = [pltpu.make_async_copy(*piece, sems.at[i]) for i, piece in enumerate(pieces)]
    for copy in copies:
        copy.start()
    first = lax.broadcasted_iota(jnp.int32, (rows, rows), 0)
    second = lax.broadcasted_iota(jnp.int32, (rows, rows), 1)
    copies[0].wait()
    decay = decay_ref[...]
    high = decay.astype(BF16)
    rest = decay - high.astype(F32)
    middle = rest.astype(BF16)
    low = (rest - middle.astype(F32)).astype(BF16)
    terms = jnp.concatenate([high, middle, low], axis=0)
    sums = dot(terms, (first <= second).astype(BF16), NN)
    across = sums[:heads] + (sums[heads : 2 * heads] + sums[2 * heads :])
    sums = dot((first >= second).astype(BF16), terms, NT)
    inside = sums[:, :heads] + (sums[:, heads : 2 * heads] + sums[:, 2 * heads :])
    inside_ref[...] = inside
    across_ref[...] = across
    shares = jnp.exp(inside[rows - 1 : rows, :] - inside)
    kept = jnp.broadcast_to(jnp.exp(across[:, rows - 1 : rows]), (heads, HEAD))
    kept_ref[...] = kept
    send_ref[heads // 2 * HEAD :, :] = kept
    copies[1].wait()
    copies[2].wait()

    def state_of(h):
        cols = head_cols(h)
        key_decayed = (k_ref[:, cols].astype(F32) * shares[:, h : h + 1]).astype(BF16)
        key_ref[:, cols] = key_decayed
        return dot(key_decayed, v_ref[:, cols], TN)

    deal_halves(core_ref[0], state_of, heads // 2, keep_ref, send_ref)
    for copy in copies[3:]:
        copy.wait()


def kept_rows(core, own_ref, got_ref, i):
    half = got_ref.shape[0] // (HEAD + 2)
    at = got_ref.shape[0] - 2 * half
    own = jnp.where(core == 0, own_ref[i : i + 1, :], own_ref[half + i : half + i + 1, :])
    got = jnp.where(core == 0, got_ref[at + i : at + i + 1, :], got_ref[at + half + i : at + half + i + 1, :])
    return jnp.where(core == 0, own, got), jnp.where(core == 0, got, own)


def in_order(core, own, got):
    return jnp.where(core == 0, own, got), jnp.where(core == 0, got, own)


def forward_join_kernel(core_ref, after_ref, keep_ref, got_ref, kept_ref, pay_ref):
    core = core_ref[0]
    for i in range(keep_ref.shape[0] // HEAD):
        first, second = in_order(core, keep_ref[head_rows(i), :], got_ref[head_rows(i), :])
        kept_first, kept_second = kept_rows(core, kept_ref, got_ref, i)
        joined = kept_second * first + second
        for part in range(8):
            at = 17 * (8 * i + part)
            pay_ref[at : at + 16, :] = joined[16 * part : 16 * part + 16]
            pay_ref[at + 16 : at + 17, :] = kept_first * kept_second


def forward_scan_kernel(got_ref, out_ref, kept_ref):
    count = out_ref.shape[0]
    state = jnp.zeros(out_ref.shape[1:], F32)
    for j in range(count):
        out_ref[j] = state
        kept = got_ref[17 * j + 16 : 17 * j + 17, :]
        kept_ref[j : j + 1, :] = kept
        state = kept * state + got_ref[17 * j : 17 * j + 16, :]


def reverse_join_kernel(core_ref, after_ref, keep_ref, got_ref, kept_ref, got_kept_ref, out_ref):
    core = core_ref[0]
    for i in range(keep_ref.shape[0] // HEAD):
        first, second = in_order(core, keep_ref[head_rows(i), :], got_ref[head_rows(i), :])
        kept_first, _ = kept_rows(core, kept_ref, got_kept_ref, i)
        out_ref[head_rows(i), :] = first + kept_first * second


def reverse_scan_kernel(got_ref, kept_ref, out_ref):
    count = out_ref.shape[0]
    state = jnp.zeros(out_ref.shape[1:], F32)
    for j in reversed(range(count)):
        out_ref[j] = state
        state = kept_ref[j : j + 1, :] * state + got_ref[j]


def weights_of(inside_ref, across_ref, h, transposed=False):
    rows = inside_ref.shape[0]
    first = lax.broadcasted_iota(jnp.int32, (rows, rows), 0)
    second = lax.broadcasted_iota(jnp.int32, (rows, rows), 1)
    if transposed:
        spread = across_ref[h : h + 1, :] - inside_ref[:, h : h + 1]
        return jnp.exp(jnp.where(second >= first, spread, -1e30))
    spread = inside_ref[:, h : h + 1] - across_ref[h : h + 1, :]
    return jnp.exp(jnp.where(first >= second, spread, -1e30))


def mixing_of(
    q_ref, k_ref, v_ref, g_ref, gain_ref, inside_ref, across_ref,
    near_ref, mix_turned_ref, query_ref, query_turned_ref, weights_ref, weights_turned_ref, scaled_ref,
):
    grown = jnp.exp(inside_ref[...])
    for h in range(inside_ref.shape[1]):
        cols = head_cols(h)
        queries, keys = q_ref[:, cols], k_ref[:, cols]
        weights = weights_of(inside_ref, across_ref, h)
        weights_ref[h] = weights
        mixing = (dot(queries, keys, NT) * weights).astype(BF16)
        near_ref[:, cols] = dot(mixing, v_ref[:, cols], NN)
        weights_turned = weights_of(inside_ref, across_ref, h, True)
        weights_turned_ref[h] = weights_turned
        mix_turned_ref[h] = (dot(keys, queries, NT) * weights_turned).astype(BF16)
        decayed = queries.astype(F32) * grown[:, h : h + 1]
        query_ref[:, cols] = decayed.astype(BF16)
        query_turned_ref[h] = decayed.T.astype(BF16)
        scaled_ref[:, cols] = g_ref[:, cols].astype(F32) * gain_ref[:, cols]


def mixing_first_kernel(core_ref, after_ref, *refs):
    @pl.when(core_ref[0] == 0)
    def _():
        mixing_of(*refs)


def enter_kernel(core_ref, half_ref, keep_ref, got_ref, kept_ref, *refs):
    inputs, (own_ref, send_ref, *outputs) = refs[:7], refs[14:]
    core = core_ref[0]
    for i in range(half_ref.shape[0]):
        kept_first, _ = kept_rows(core, kept_ref, got_ref, i)
        first, _ = in_order(core, keep_ref[head_rows(i), :], got_ref[head_rows(i), :])
        state = half_ref[i]
        later = kept_first * state + first
        own_ref[i] = jnp.where(core == 0, state, later)
        send_ref[i] = jnp.where(core == 0, later, state)

    @pl.when(core == 1)
    def _():
        mixing_of(*inputs, *outputs)


def attend_half(base, near_ref, query_ref, half_ref, scaled_ref, att_ref, entering_ref, squares, crossed):
    for i in range(half_ref.shape[0]):
        h = base + i
        cols = pl.ds(pl.multiple_of(h * HEAD, HEAD), HEAD)
        state = half_ref[i].astype(BF16)
        entering_ref[h] = state
        attended = near_ref[:, cols] + dot(query_ref[:, cols], state, NN)
        att_ref[:, cols] = attended
        squares += attended * attended
        crossed += scaled_ref[:, cols] * attended
    return squares, crossed


def attend_own_kernel(
    core_ref, near_ref, query_ref, half_ref, scaled_ref, att_ref, entering_ref, squares_ref, crossed_ref
):
    zero = jnp.zeros(squares_ref.shape, F32)
    squares_ref[...], crossed_ref[...] = attend_half(
        core_ref[0] * half_ref.shape[0], near_ref, query_ref, half_ref, scaled_ref, att_ref, entering_ref, zero, zero
    )


def attend_other_kernel(
    core_ref, near_ref, query_ref, half_ref, scaled_ref, squares_ref, crossed_ref,
    att_in_ref, entering_in_ref, att_ref, entering_ref, sums_ref,
):
    squares, crossed = attend_half(
        (1 - core_ref[0]) * half_ref.shape[0], near_ref, query_ref, half_ref, scaled_ref, att_ref, entering_ref,
        squares_ref[...], crossed_ref[...],
    )
    sums = jnp.concatenate(
        [jnp.sum(squares, axis=1, keepdims=True), jnp.sum(crossed, axis=1, keepdims=True)], axis=1
    ).T
    for peer in range(sums_ref.shape[0]):
        sums_ref[peer] = sums


def norm_columns(sums_ref, rows):
    whole = jnp.sum(sums_ref[...], axis=0)
    first = lax.broadcasted_iota(jnp.int32, (rows, rows), 0)
    second = lax.broadcasted_iota(jnp.int32, (rows, rows), 1)
    same = first == second
    square_sum = jnp.sum(jnp.where(same, whole[0:1, :], 0.0), axis=1, keepdims=True)
    cross_sum = jnp.sum(jnp.where(same, whole[1:2, :], 0.0), axis=1, keepdims=True)
    width = HEAD_COUNT * HEAD
    inverse = lax.rsqrt(square_sum / width + EPSILON)
    return inverse, inverse * inverse * inverse * (cross_sum / width)


def norm_grad_kernel(core_ref, sums_ref, att_ref, scaled_ref, query_turned_ref, keep_ref, send_ref, gf_ref):
    rows, width = att_ref.shape
    inverse, factor = norm_columns(sums_ref, rows)

    def state_of(h):
        cols = head_cols(h)
        grad_flat = (inverse * scaled_ref[:, cols] - att_ref[:, cols] * factor).astype(BF16)
        gf_ref[:, cols] = grad_flat
        return dot(query_turned_ref[h], grad_flat, NN)

    deal_halves(core_ref[0], state_of, width // HEAD // 2, keep_ref, send_ref)


def send_out(copies, source, target, sems, i, cols):
    copy = pltpu.make_async_copy(source.at[:, cols], target.at[:, cols], sems.at[i])
    copy.start()
    copies.append(copy)


def near_grad(
    sums_ref, att_ref, gain_ref, gf_ref, q_ref, k_ref, v_ref, state_ref, inside_ref, weights_ref,
    weights_turned_ref, mix_turned_ref, normed_hbm, gq_hbm, gk_ref, gv_ref, normed_ref, gq_ref, sems,
):
    rows, heads = inside_ref.shape
    inverse, _ = norm_columns(sums_ref, rows)
    grown = jnp.exp(inside_ref[...])
    copies = []
    for h in range(heads):
        cols = head_cols(h)
        normed_ref[:, cols] = (att_ref[:, cols] * inverse * gain_ref[:, cols]).astype(BF16)
        grad_flat = gf_ref[:, cols]
        grad_mix = (dot(grad_flat, v_ref[:, cols], NT) * weights_ref[h]).astype(BF16)
        far = dot(grad_flat, state_ref[h], NT)
        gq_ref[:, cols] = (dot(grad_mix, k_ref[:, cols], NN) + grown[:, h : h + 1] * far).astype(BF16)
        if h % 2:
            pair = slice((h - 1) * HEAD, (h + 1) * HEAD)
            send_out(copies, normed_ref, normed_hbm, sems, h - 1, pair)
            send_out(copies, gq_ref, gq_hbm, sems, h, pair)
    for h in range(heads):
        cols = head_cols(h)
        grad_flat = gf_ref[:, cols]
        turned = (dot(v_ref[:, cols], grad_flat, NT) * weights_turned_ref[h]).astype(BF16)
        gk_ref[:, cols] = dot(turned, q_ref[:, cols], NN)
        gv_ref[:, cols] = dot(mix_turned_ref[h], grad_flat, NN)
    for copy in copies:
        copy.wait()


def near_first_kernel(core_ref, *refs):
    @pl.when(core_ref[0] == 0)
    def _():
        near_grad(*refs)


def leave_kernel(core_ref, half_ref, keep_ref, got_ref, kept_ref, got_kept_ref, *refs):
    inputs, (own_ref, send_ref, *outputs) = refs[:12], refs[16:]
    core = core_ref[0]
    for i in range(half_ref.shape[0]):
        _, kept_second = kept_rows(core, kept_ref, got_kept_ref, i)
        _, second = in_order(core, keep_ref[head_rows(i), :], got_ref[head_rows(i), :])
        state = half_ref[i]
        earlier = second + kept_second * state
        own_ref[i] = jnp.where(core == 0, earlier, state)
        send_ref[i] = jnp.where(core == 0, state, earlier)

    @pl.when(core == 1)
    def _():
        near_grad(*inputs, *outputs)


def far_half(
    base, gk_near_ref, gv_near_ref, key_ref, v_ref, half_ref, inside_ref, gk_hbm, gv_hbm, gk_ref, gv_ref, sems
):
    rows, heads = inside_ref.shape
    inside = inside_ref[...]
    shares = jnp.exp(inside[rows - 1 : rows, :] - inside)
    head = lax.broadcasted_iota(jnp.int32, (rows, heads), 1)
    copies = []
    for i in range(half_ref.shape[0]):
        cols = pl.ds(pl.multiple_of((base + i) * HEAD, HEAD), HEAD)
        share = jnp.sum(jnp.where(head == base + i, shares, 0.0), axis=1, keepdims=True)
        arriving = half_ref[i].astype(BF16)
        far = dot(v_ref[:, cols], arriving, NT)
        gk_ref[:, cols] = (gk_near_ref[:, cols] + share * far).astype(BF16)
        gv_ref[:, cols] = (gv_near_ref[:, cols] + dot(key_ref[:, cols], arriving, NN)).astype(BF16)
        if i % 2:
            pair = pl.ds(pl.multiple_of((base + i - 1) * HEAD, 2 * HEAD), 2 * HEAD)
            send_out(copies, gk_ref, gk_hbm, sems, i - 1, pair)
            send_out(copies, gv_ref, gv_hbm, sems, i, pair)
    for copy in copies:
        copy.wait()


def far_own_kernel(core_ref, gk_near_ref, gv_near_ref, key_ref, v_ref, half_ref, inside_ref, *refs):
    base = core_ref[0] * half_ref.shape[0]
    far_half(base, gk_near_ref, gv_near_ref, key_ref, v_ref, half_ref, inside_ref, *refs)


def far_other_kernel(core_ref, gk_near_ref, gv_near_ref, key_ref, v_ref, half_ref, inside_ref, gk_in, gv_in, *refs):
    base = (1 - core_ref[0]) * half_ref.shape[0]
    far_half(base, gk_near_ref, gv_near_ref, key_ref, v_ref, half_ref, inside_ref, *refs)


def body(chips, tp_size, queries, key_vectors, values, decay_log, norm_gain, grad_out):
    rows, width = queries.shape
    heads = decay_log.shape[1]
    half = heads // 2
    slab = half * HEAD // chips
    core = lax.axis_index("core").astype(jnp.int32).reshape(1)
    gain = norm_gain.reshape(1, width)
    wide, tile, half_state = (rows, width), (chips, slab, HEAD), (half, HEAD, HEAD)
    whole, size = rows * width, heads * HEAD * HEAD

    def across_chips(array):
        return lax.all_to_all(array, ("x", "y"), 0, 0)

    def swap(array):
        return lax.ppermute(array, "core", [(0, 1), (1, 0)])

    wide_bf, wide_f32 = ("v", wide, BF16), ("v", wide, F32)
    square, per_token = (heads, rows, rows), ("v", (rows, heads), F32)
    half_rows, half_tile = ("v", (half * HEAD, HEAD), F32), ("v", half_state, F32)
    on_core = ("s", core)

    def vmem(*arrays):
        return [("v", a) for a in arrays]

    def like(outs, arrays):
        return [(m, a) for (m, _, _), a in zip(outs, arrays)]

    inputs = [queries, key_vectors, values, grad_out, decay_log.T, gain]
    keep, send, kept, inside, across, key_decayed, q, k, v, g, gain = call(
        local_kernel,
        [
            half_rows, ("v", (half * HEAD + heads, HEAD), F32), ("v", (heads, HEAD), F32), per_token,
            ("v", (heads, rows), F32), wide_bf, wide_bf, wide_bf, wide_bf, wide_bf, ("v", (1, width), F32),
        ],
        [on_core] + [("h", a) for a in inputs],
        2 * whole * HEAD, 8 * whole,
        scratch=[pltpu.VMEM((heads, rows), F32), pltpu.SemaphoreType.DMA((6,))],
    )
    got = swap(send)
    mixing_args = vmem(q, k, v, g, gain, inside, across)
    mixing_outs = [
        wide_f32, ("v", square, BF16), wide_bf, ("v", (heads, HEAD, rows), BF16), ("v", square, F32),
        ("v", square, F32), wide_f32,
    ]
    mixing_done = call(mixing_first_kernel, mixing_outs, [on_core, ("a", got)] + mixing_args, 6 * whole * rows, 12 * whole)
    (pay,) = call(
        forward_join_kernel,
        [("v", (chips * (slab + 1), HEAD), F32)],
        [on_core, ("a", mixing_done[0])] + vmem(keep, got, kept),
        2 * size, 12 * size,
    )
    pay = across_chips(pay.reshape(chips, 1, (slab + 1) * HEAD)).reshape(chips * (slab + 1), HEAD)
    tiles, kept_chips = call(
        forward_scan_kernel,
        [("v", tile, F32), ("v", (chips, HEAD), F32)],
        vmem(pay),
        size, 4 * size,
    )
    half_in = across_chips(tiles).reshape(half_state)
    half_own, half_send, near, mixing_turned, query_decayed, query_turned, weights, weights_turned, scaled = call(
        enter_kernel,
        [half_tile, half_tile] + mixing_outs,
        [on_core] + vmem(half_in, keep, got, kept) + mixing_args + like(mixing_outs, mixing_done),
        6 * whole * rows, 12 * whole, aliases={12 + i: 2 + i for i in range(7)},
    )
    half_other = swap(half_send)
    entering_bf, column = ("v", (heads, HEAD, HEAD), BF16), ("v", (rows, HEAD), F32)
    attended, entering, squares, crossed = call(
        attend_own_kernel,
        [wide_f32, entering_bf, column, column],
        [on_core] + vmem(near, query_decayed, half_own, scaled),
        whole * HEAD, 6 * whole,
    )
    attended, entering, sums = call(
        attend_other_kernel,
        [wide_f32, entering_bf, ("v", (tp_size, 2, rows), F32)],
        [on_core] + vmem(near, query_decayed, half_other, scaled, squares, crossed, attended, entering),
        whole * HEAD, 6 * whole, aliases={7: 0, 8: 1},
    )
    sums = lax.all_to_all(sums, "tp", 0, 0)
    back_keep, back_send, grad_flat = call(
        norm_grad_kernel,
        [half_rows, half_rows, wide_bf],
        [on_core] + vmem(sums, attended, scaled, query_turned),
        2 * whole * HEAD, 12 * whole,
    )
    back_got = swap(back_send)
    near_args = vmem(
        sums, attended, gain, grad_flat, q, k, v, entering, inside, weights, weights_turned, mixing_turned
    )
    near_outs = [("h", wide, BF16), ("h", wide, BF16), wide_f32, wide_f32]
    outputs = [pltpu.VMEM(wide, BF16), pltpu.VMEM(wide, BF16), pltpu.SemaphoreType.DMA((heads,))]
    near_done = call(
        near_first_kernel, near_outs, [on_core] + near_args, 12 * whole * rows, 16 * whole, scratch=outputs
    )
    (pay_back,) = call(
        reverse_join_kernel,
        [half_rows],
        [on_core, ("a", near_done[2])] + vmem(back_keep, back_got, kept, got),
        2 * size, 12 * size,
    )
    (tiles_back,) = call(
        reverse_scan_kernel,
        [("v", tile, F32)],
        vmem(across_chips(pay_back.reshape(tile)), kept_chips),
        size, 4 * size,
    )
    half_back = across_chips(tiles_back).reshape(half_state)
    arriving_own, arriving_send, normed, grad_query, grad_key_near, grad_value_near = call(
        leave_kernel,
        [half_tile, half_tile] + near_outs,
        [on_core] + vmem(half_back, back_keep, back_got, kept, got) + near_args + like(near_outs, near_done),
        12 * whole * rows, 16 * whole, scratch=outputs, aliases={18 + i: 2 + i for i in range(4)},
    )
    arriving_other = swap(arriving_send)
    far_outs = [("h", wide, BF16), ("h", wide, BF16)]
    far_args = vmem(grad_key_near, grad_value_near, key_decayed, v)
    far_done = call(
        far_own_kernel, far_outs, [on_core] + far_args + vmem(arriving_own, inside),
        2 * whole * HEAD, 8 * whole, scratch=outputs,
    )
    grad_key, grad_value = call(
        far_other_kernel, far_outs,
        [on_core] + far_args + vmem(arriving_other, inside) + like(far_outs, far_done),
        2 * whole * HEAD, 8 * whole, scratch=outputs, aliases={7: 0, 8: 1},
    )
    return normed, grad_query, grad_key, grad_value


def solution(mesh):
    seq, tp = mesh.shape["seq"], mesh.shape["tp"]
    fine = Mesh(mesh.devices.reshape(seq // 16, 8, 2, tp), ("x", "y", "core", "tp"))
    spec = P(("x", "y", "core"), "tp")
    return jax.shard_map(
        functools.partial(body, seq // 2, tp),
        mesh=fine,
        in_specs=(spec, spec, spec, spec, P("tp"), spec),
        out_specs=(spec, spec, spec, spec),
        check_vma=False,
    )
```

```python
import functools

import jax
import jax.numpy as jnp
from jax import lax
from jax.experimental import pallas as pl
from jax.experimental.pallas import tpu as pltpu
from jax.sharding import Mesh
from jax.sharding import PartitionSpec as P

HEAD_COUNT = 64
HEAD = 128
EPSILON = 1e-06
HIGH = lax.Precision.HIGHEST
F32 = jnp.float32
BF16 = jnp.bfloat16
VMEM_LIMIT = 20 * 1024 * 1024
NN = (((1,), (0,)), ((), ()))
NT = (((1,), (1,)), ((), ()))
TN = (((0,), (0,)), ((), ()))


def dot(a, b, dims, precision=None):
    return lax.dot_general(a, b, dims, precision=precision, preferred_element_type=F32)


SPACES = {"s": pltpu.SMEM, "h": pltpu.HBM, "v": pltpu.VMEM, "a": pl.ANY}


def call(kernel, outs, args, flops, bytes_accessed, scratch=(), aliases=()):
    return pl.pallas_call(
        kernel,
        out_shape=[SPACES[m](s, d) for m, s, d in outs],
        in_specs=[pl.BlockSpec(memory_space=SPACES[m]) for m, _ in args],
        out_specs=[pl.BlockSpec(memory_space=SPACES[m]) for m, _, _ in outs],
        scratch_shapes=list(scratch),
        input_output_aliases=dict(aliases),
        compiler_params=pltpu.CompilerParams(vmem_limit_bytes=VMEM_LIMIT),
        cost_estimate=pl.CostEstimate(
            flops=flops, bytes_accessed=bytes_accessed, transcendentals=0
        ),
    )(*[pltpu.with_memory_space_constraint(a, SPACES[m]) if m in "hv" else a for m, a in args])


def head_cols(h):
    return slice(h * HEAD, (h + 1) * HEAD)


def head_rows(h):
    return slice(h * HEAD, (h + 1) * HEAD)


def half_of_heads(core, half, sent, state_of, out_ref):
    for place in range(2):

        @pl.when(core == place)
        def _(first=(place ^ sent) * half):
            for i in range(half):
                out_ref[head_rows(i), :] = state_of(first + i)


def local_kernel(
    core_ref, q_hbm, k_hbm, v_hbm, g_hbm, decay_hbm, gain_hbm,
    send_ref, kept_ref, inside_ref, across_ref, q_ref, k_ref, v_ref, g_ref, gain_ref, decay_ref, sems,
):
    heads, rows = decay_ref.shape
    pieces = [
        (decay_hbm, decay_ref), (k_hbm, k_ref), (v_hbm, v_ref), (q_hbm, q_ref), (g_hbm, g_ref), (gain_hbm, gain_ref)
    ]
    copies = [pltpu.make_async_copy(*piece, sems.at[i]) for i, piece in enumerate(pieces)]
    for copy in copies:
        copy.start()
    first = lax.broadcasted_iota(jnp.int32, (rows, rows), 0)
    second = lax.broadcasted_iota(jnp.int32, (rows, rows), 1)
    copies[0].wait()
    decay = decay_ref[...]
    high = decay.astype(BF16)
    rest = decay - high.astype(F32)
    middle = rest.astype(BF16)
    low = (rest - middle.astype(F32)).astype(BF16)
    terms = jnp.concatenate([high, middle, low], axis=0)
    sums = dot(terms, (first <= second).astype(BF16), NN)
    across = sums[:heads] + (sums[heads : 2 * heads] + sums[2 * heads :])
    sums = dot((first >= second).astype(BF16), terms, NT)
    inside = sums[:, :heads] + (sums[:, heads : 2 * heads] + sums[:, 2 * heads :])
    inside_ref[...] = inside
    across_ref[...] = across
    shares = jnp.exp(inside[rows - 1 : rows, :] - inside)
    kept = jnp.broadcast_to(jnp.exp(across[:, rows - 1 : rows]), (heads, HEAD))
    kept_ref[...] = kept
    send_ref[heads // 2 * HEAD :, :] = kept
    copies[1].wait()
    copies[2].wait()

    def state_of(h):
        cols = head_cols(h)
        key_decayed = (k_ref[:, cols].astype(F32) * shares[:, h : h + 1]).astype(BF16)
        return dot(key_decayed, v_ref[:, cols], TN)

    half_of_heads(core_ref[0], heads // 2, 1, state_of, send_ref)
    for copy in copies[3:]:
        copy.wait()


def local_keep_kernel(core_ref, k_ref, v_ref, inside_ref, keep_ref, key_ref):
    rows, heads = inside_ref.shape
    inside = inside_ref[...]
    shares = jnp.exp(inside[rows - 1 : rows, :] - inside)
    for h in range(heads):
        cols = head_cols(h)
        key_ref[:, cols] = (k_ref[:, cols].astype(F32) * shares[:, h : h + 1]).astype(BF16)

    def state_of(h):
        return dot(key_ref[:, head_cols(h)], v_ref[:, head_cols(h)], TN)

    half_of_heads(core_ref[0], heads // 2, 0, state_of, keep_ref)


def kept_rows(core, own_ref, got_ref, i):
    half = got_ref.shape[0] // (HEAD + 2)
    at = got_ref.shape[0] - 2 * half
    own = jnp.where(core == 0, own_ref[i : i + 1, :], own_ref[half + i : half + i + 1, :])
    got = jnp.where(core == 0, got_ref[at + i : at + i + 1, :], got_ref[at + half + i : at + half + i + 1, :])
    return jnp.where(core == 0, own, got), jnp.where(core == 0, got, own)


def in_order(core, own, got):
    return jnp.where(core == 0, own, got), jnp.where(core == 0, got, own)


def forward_join_kernel(core_ref, after_ref, keep_ref, got_ref, kept_ref, pay_ref):
    core = core_ref[0]
    for i in range(keep_ref.shape[0] // HEAD):
        first, second = in_order(core, keep_ref[head_rows(i), :], got_ref[head_rows(i), :])
        kept_first, kept_second = kept_rows(core, kept_ref, got_ref, i)
        joined = kept_second * first + second
        for part in range(8):
            at = 17 * (8 * i + part)
            pay_ref[at : at + 16, :] = joined[16 * part : 16 * part + 16]
            pay_ref[at + 16 : at + 17, :] = kept_first * kept_second


def forward_scan_kernel(got_ref, out_ref, kept_ref):
    count = out_ref.shape[0]
    state = jnp.zeros(out_ref.shape[1:], F32)
    for j in range(count):
        out_ref[j] = state
        kept = got_ref[17 * j + 16 : 17 * j + 17, :]
        kept_ref[j : j + 1, :] = kept
        state = kept * state + got_ref[17 * j : 17 * j + 16, :]


def reverse_join_kernel(core_ref, after_ref, keep_ref, got_ref, kept_ref, got_kept_ref, out_ref):
    core = core_ref[0]
    for i in range(keep_ref.shape[0] // HEAD):
        first, second = in_order(core, keep_ref[head_rows(i), :], got_ref[head_rows(i), :])
        kept_first, _ = kept_rows(core, kept_ref, got_kept_ref, i)
        out_ref[head_rows(i), :] = first + kept_first * second


def reverse_scan_kernel(got_ref, kept_ref, out_ref):
    count = out_ref.shape[0]
    state = jnp.zeros(out_ref.shape[1:], F32)
    for j in reversed(range(count)):
        out_ref[j] = state
        state = kept_ref[j : j + 1, :] * state + got_ref[j]


def weights_of(inside_ref, across_ref, h, transposed=False):
    rows = inside_ref.shape[0]
    first = lax.broadcasted_iota(jnp.int32, (rows, rows), 0)
    second = lax.broadcasted_iota(jnp.int32, (rows, rows), 1)
    if transposed:
        spread = across_ref[h : h + 1, :] - inside_ref[:, h : h + 1]
        return jnp.exp(jnp.where(second >= first, spread, -1e30))
    spread = inside_ref[:, h : h + 1] - across_ref[h : h + 1, :]
    return jnp.exp(jnp.where(first >= second, spread, -1e30))


def mixing_of(
    q_ref, k_ref, v_ref, g_ref, gain_ref, inside_ref, across_ref,
    near_ref, mix_turned_ref, query_ref, query_turned_ref, weights_ref, weights_turned_ref, scaled_ref,
):
    grown = jnp.exp(inside_ref[...])
    for h in range(inside_ref.shape[1]):
        cols = head_cols(h)
        queries, keys = q_ref[:, cols], k_ref[:, cols]
        weights = weights_of(inside_ref, across_ref, h)
        weights_ref[h] = weights
        mixing = (dot(queries, keys, NT) * weights).astype(BF16)
        near_ref[:, cols] = dot(mixing, v_ref[:, cols], NN)
        weights_turned = weights_of(inside_ref, across_ref, h, True)
        weights_turned_ref[h] = weights_turned
        mix_turned_ref[h] = (dot(keys, queries, NT) * weights_turned).astype(BF16)
        decayed = queries.astype(F32) * grown[:, h : h + 1]
        query_ref[:, cols] = decayed.astype(BF16)
        query_turned_ref[h] = decayed.T.astype(BF16)
        scaled_ref[:, cols] = g_ref[:, cols].astype(F32) * gain_ref[:, cols]


def mixing_first_kernel(core_ref, after_ref, *refs):
    @pl.when(core_ref[0] == 0)
    def _():
        mixing_of(*refs)


def enter_kernel(core_ref, half_ref, keep_ref, got_ref, kept_ref, *refs):
    inputs, (own_ref, send_ref, *outputs) = refs[:7], refs[14:]
    core = core_ref[0]
    for i in range(half_ref.shape[0]):
        kept_first, _ = kept_rows(core, kept_ref, got_ref, i)
        first, _ = in_order(core, keep_ref[head_rows(i), :], got_ref[head_rows(i), :])
        state = half_ref[i]
        later = kept_first * state + first
        own_ref[i] = jnp.where(core == 0, state, later)
        send_ref[i] = jnp.where(core == 0, later, state)

    @pl.when(core == 1)
    def _():
        mixing_of(*inputs, *outputs)


def attend_half(base, near_ref, query_ref, half_ref, scaled_ref, att_ref, entering_ref, squares, crossed):
    for i in range(half_ref.shape[0]):
        h = base + i
        cols = pl.ds(pl.multiple_of(h * HEAD, HEAD), HEAD)
        state = half_ref[i].astype(BF16)
        entering_ref[h] = state
        attended = near_ref[:, cols] + dot(query_ref[:, cols], state, NN)
        att_ref[:, cols] = attended
        squares += attended * attended
        crossed += scaled_ref[:, cols] * attended
    return squares, crossed


def attend_own_kernel(
    core_ref, near_ref, query_ref, half_ref, scaled_ref, att_ref, entering_ref, squares_ref, crossed_ref
):
    zero = jnp.zeros(squares_ref.shape, F32)
    squares_ref[...], crossed_ref[...] = attend_half(
        core_ref[0] * half_ref.shape[0], near_ref, query_ref, half_ref, scaled_ref, att_ref, entering_ref, zero, zero
    )


def attend_other_kernel(
    core_ref, near_ref, query_ref, half_ref, scaled_ref, squares_ref, crossed_ref,
    att_in_ref, entering_in_ref, att_ref, entering_ref, sums_ref,
):
    squares, crossed = attend_half(
        (1 - core_ref[0]) * half_ref.shape[0], near_ref, query_ref, half_ref, scaled_ref, att_ref, entering_ref,
        squares_ref[...], crossed_ref[...],
    )
    sums = jnp.concatenate(
        [jnp.sum(squares, axis=1, keepdims=True), jnp.sum(crossed, axis=1, keepdims=True)], axis=1
    ).T
    for peer in range(sums_ref.shape[0]):
        sums_ref[peer] = sums


def norm_columns(sums_ref, rows):
    whole = jnp.sum(sums_ref[...], axis=0)
    first = lax.broadcasted_iota(jnp.int32, (rows, rows), 0)
    second = lax.broadcasted_iota(jnp.int32, (rows, rows), 1)
    same = first == second
    square_sum = jnp.sum(jnp.where(same, whole[0:1, :], 0.0), axis=1, keepdims=True)
    cross_sum = jnp.sum(jnp.where(same, whole[1:2, :], 0.0), axis=1, keepdims=True)
    width = HEAD_COUNT * HEAD
    inverse = lax.rsqrt(square_sum / width + EPSILON)
    return inverse, inverse * inverse * inverse * (cross_sum / width)


def norm_grad_kernel(core_ref, sums_ref, att_ref, scaled_ref, query_turned_ref, send_ref, columns_ref):
    rows, width = att_ref.shape
    inverse, factor = norm_columns(sums_ref, rows)
    columns_ref[...] = jnp.concatenate([inverse, factor], axis=1)

    def state_of(h):
        cols = head_cols(h)
        grad_flat = (inverse * scaled_ref[:, cols] - att_ref[:, cols] * factor).astype(BF16)
        return dot(query_turned_ref[h], grad_flat, NN)

    half_of_heads(core_ref[0], width // HEAD // 2, 1, state_of, send_ref)


def norm_grad_keep_kernel(core_ref, columns_ref, att_ref, scaled_ref, query_turned_ref, keep_ref, gf_ref):
    width = att_ref.shape[1]
    inverse, factor = columns_ref[:, 0:1], columns_ref[:, 1:2]
    for h in range(width // HEAD):
        cols = head_cols(h)
        gf_ref[:, cols] = (inverse * scaled_ref[:, cols] - att_ref[:, cols] * factor).astype(BF16)

    def state_of(h):
        return dot(query_turned_ref[h], gf_ref[:, head_cols(h)], NN)

    half_of_heads(core_ref[0], width // HEAD // 2, 0, state_of, keep_ref)


def send_out(copies, source, target, sems, i, cols):
    copy = pltpu.make_async_copy(source.at[:, cols], target.at[:, cols], sems.at[i])
    copy.start()
    copies.append(copy)


def near_grad(
    columns_ref, att_ref, gain_ref, gf_ref, q_ref, k_ref, v_ref, state_ref, inside_ref, weights_ref,
    weights_turned_ref, mix_turned_ref, normed_hbm, gq_hbm, gk_ref, gv_ref, normed_ref, gq_ref, sems,
):
    rows, heads = inside_ref.shape
    inverse = columns_ref[:, 0:1]
    grown = jnp.exp(inside_ref[...])
    copies = []
    for h in range(heads):
        cols = head_cols(h)
        normed_ref[:, cols] = (att_ref[:, cols] * inverse * gain_ref[:, cols]).astype(BF16)
        grad_flat = gf_ref[:, cols]
        grad_mix = (dot(grad_flat, v_ref[:, cols], NT) * weights_ref[h]).astype(BF16)
        far = dot(grad_flat, state_ref[h], NT)
        gq_ref[:, cols] = (dot(grad_mix, k_ref[:, cols], NN) + grown[:, h : h + 1] * far).astype(BF16)
        if h % 2:
            pair = slice((h - 1) * HEAD, (h + 1) * HEAD)
            send_out(copies, normed_ref, normed_hbm, sems, h - 1, pair)
            send_out(copies, gq_ref, gq_hbm, sems, h, pair)
    for h in range(heads):
        cols = head_cols(h)
        grad_flat = gf_ref[:, cols]
        turned = (dot(v_ref[:, cols], grad_flat, NT) * weights_turned_ref[h]).astype(BF16)
        gk_ref[:, cols] = dot(turned, q_ref[:, cols], NN)
        gv_ref[:, cols] = dot(mix_turned_ref[h], grad_flat, NN)
    for copy in copies:
        copy.wait()


def near_first_kernel(core_ref, *refs):
    @pl.when(core_ref[0] == 0)
    def _():
        near_grad(*refs)


def leave_kernel(core_ref, half_ref, keep_ref, got_ref, kept_ref, got_kept_ref, *refs):
    inputs, (own_ref, send_ref, *outputs) = refs[:12], refs[16:]
    core = core_ref[0]
    for i in range(half_ref.shape[0]):
        _, kept_second = kept_rows(core, kept_ref, got_kept_ref, i)
        _, second = in_order(core, keep_ref[head_rows(i), :], got_ref[head_rows(i), :])
        state = half_ref[i]
        earlier = second + kept_second * state
        own_ref[i] = jnp.where(core == 0, earlier, state)
        send_ref[i] = jnp.where(core == 0, state, earlier)

    @pl.when(core == 1)
    def _():
        near_grad(*inputs, *outputs)


def far_half(
    base, gk_near_ref, gv_near_ref, key_ref, v_ref, half_ref, inside_ref, gk_hbm, gv_hbm, gk_ref, gv_ref, sems
):
    rows, heads = inside_ref.shape
    inside = inside_ref[...]
    shares = jnp.exp(inside[rows - 1 : rows, :] - inside)
    head = lax.broadcasted_iota(jnp.int32, (rows, heads), 1)
    copies = []
    for i in range(half_ref.shape[0]):
        cols = pl.ds(pl.multiple_of((base + i) * HEAD, HEAD), HEAD)
        share = jnp.sum(jnp.where(head == base + i, shares, 0.0), axis=1, keepdims=True)
        arriving = half_ref[i].astype(BF16)
        far = dot(v_ref[:, cols], arriving, NT)
        gk_ref[:, cols] = (gk_near_ref[:, cols] + share * far).astype(BF16)
        gv_ref[:, cols] = (gv_near_ref[:, cols] + dot(key_ref[:, cols], arriving, NN)).astype(BF16)
        if i % 2:
            pair = pl.ds(pl.multiple_of((base + i - 1) * HEAD, 2 * HEAD), 2 * HEAD)
            send_out(copies, gk_ref, gk_hbm, sems, i - 1, pair)
            send_out(copies, gv_ref, gv_hbm, sems, i, pair)
    for copy in copies:
        copy.wait()


def far_own_kernel(core_ref, gk_near_ref, gv_near_ref, key_ref, v_ref, half_ref, inside_ref, *refs):
    base = core_ref[0] * half_ref.shape[0]
    far_half(base, gk_near_ref, gv_near_ref, key_ref, v_ref, half_ref, inside_ref, *refs)


def far_other_kernel(core_ref, gk_near_ref, gv_near_ref, key_ref, v_ref, half_ref, inside_ref, gk_in, gv_in, *refs):
    base = (1 - core_ref[0]) * half_ref.shape[0]
    far_half(base, gk_near_ref, gv_near_ref, key_ref, v_ref, half_ref, inside_ref, *refs)


def body(chips, tp_size, queries, key_vectors, values, decay_log, norm_gain, grad_out):
    rows, width = queries.shape
    heads = decay_log.shape[1]
    half = heads // 2
    slab = half * HEAD // chips
    core = lax.axis_index("core").astype(jnp.int32).reshape(1)
    gain = norm_gain.reshape(1, width)
    wide, tile, half_state = (rows, width), (chips, slab, HEAD), (half, HEAD, HEAD)
    whole, size = rows * width, heads * HEAD * HEAD

    def across_chips(array):
        return lax.all_to_all(array, ("x", "y"), 0, 0)

    def swap(array):
        return lax.ppermute(array, "core", [(0, 1), (1, 0)])

    wide_bf, wide_f32 = ("v", wide, BF16), ("v", wide, F32)
    square, per_token = (heads, rows, rows), ("v", (rows, heads), F32)
    half_rows, half_tile = ("v", (half * HEAD, HEAD), F32), ("v", half_state, F32)
    on_core = ("s", core)

    def vmem(*arrays):
        return [("v", a) for a in arrays]

    def like(outs, arrays):
        return [(m, a) for (m, _, _), a in zip(outs, arrays)]

    inputs = [queries, key_vectors, values, grad_out, decay_log.T, gain]
    send, kept, inside, across, q, k, v, g, gain = call(
        local_kernel,
        [
            ("v", (half * HEAD + heads, HEAD), F32), ("v", (heads, HEAD), F32), per_token,
            ("v", (heads, rows), F32), wide_bf, wide_bf, wide_bf, wide_bf, ("v", (1, width), F32),
        ],
        [on_core] + [("h", a) for a in inputs],
        2 * whole * HEAD, 8 * whole,
        scratch=[pltpu.VMEM((heads, rows), F32), pltpu.SemaphoreType.DMA((6,))],
    )
    got = swap(send)
    keep, key_decayed = call(
        local_keep_kernel, [half_rows, wide_bf], [on_core] + vmem(k, v, inside), whole * HEAD, 4 * whole
    )
    mixing_args = vmem(q, k, v, g, gain, inside, across)
    mixing_outs = [
        wide_f32, ("v", square, BF16), wide_bf, ("v", (heads, HEAD, rows), BF16), ("v", square, F32),
        ("v", square, F32), wide_f32,
    ]
    mixing_done = call(mixing_first_kernel, mixing_outs, [on_core, ("a", got)] + mixing_args, 6 * whole * rows, 12 * whole)
    (pay,) = call(
        forward_join_kernel,
        [("v", (chips * (slab + 1), HEAD), F32)],
        [on_core, ("a", mixing_done[0])] + vmem(keep, got, kept),
        2 * size, 12 * size,
    )
    pay = across_chips(pay.reshape(chips, 1, (slab + 1) * HEAD)).reshape(chips * (slab + 1), HEAD)
    tiles, kept_chips = call(
        forward_scan_kernel,
        [("v", tile, F32), ("v", (chips, HEAD), F32)],
        vmem(pay),
        size, 4 * size,
    )
    half_in = across_chips(tiles).reshape(half_state)
    half_own, half_send, near, mixing_turned, query_decayed, query_turned, weights, weights_turned, scaled = call(
        enter_kernel,
        [half_tile, half_tile] + mixing_outs,
        [on_core] + vmem(half_in, keep, got, kept) + mixing_args + like(mixing_outs, mixing_done),
        6 * whole * rows, 12 * whole, aliases={12 + i: 2 + i for i in range(7)},
    )
    half_other = swap(half_send)
    entering_bf, column = ("v", (heads, HEAD, HEAD), BF16), ("v", (rows, HEAD), F32)
    attended, entering, squares, crossed = call(
        attend_own_kernel,
        [wide_f32, entering_bf, column, column],
        [on_core] + vmem(near, query_decayed, half_own, scaled),
        whole * HEAD, 6 * whole,
    )
    attended, entering, sums = call(
        attend_other_kernel,
        [wide_f32, entering_bf, ("v", (tp_size, 2, rows), F32)],
        [on_core] + vmem(near, query_decayed, half_other, scaled, squares, crossed, attended, entering),
        whole * HEAD, 6 * whole, aliases={7: 0, 8: 1},
    )
    sums = lax.all_to_all(sums, "tp", 0, 0)
    back_send, columns = call(
        norm_grad_kernel,
        [half_rows, ("v", (rows, 2), F32)],
        [on_core] + vmem(sums, attended, scaled, query_turned),
        whole * HEAD, 6 * whole,
    )
    back_got = swap(back_send)
    back_keep, grad_flat = call(
        norm_grad_keep_kernel,
        [half_rows, wide_bf],
        [on_core] + vmem(columns, attended, scaled, query_turned),
        whole * HEAD, 6 * whole,
    )
    near_args = vmem(
        columns, attended, gain, grad_flat, q, k, v, entering, inside, weights, weights_turned, mixing_turned
    )
    near_outs = [("h", wide, BF16), ("h", wide, BF16), wide_f32, wide_f32]
    outputs = [pltpu.VMEM(wide, BF16), pltpu.VMEM(wide, BF16), pltpu.SemaphoreType.DMA((heads,))]
    near_done = call(
        near_first_kernel, near_outs, [on_core] + near_args, 12 * whole * rows, 16 * whole, scratch=outputs
    )
    (pay_back,) = call(
        reverse_join_kernel,
        [half_rows],
        [on_core, ("a", near_done[2])] + vmem(back_keep, back_got, kept, got),
        2 * size, 12 * size,
    )
    (tiles_back,) = call(
        reverse_scan_kernel,
        [("v", tile, F32)],
        vmem(across_chips(pay_back.reshape(tile)), kept_chips),
        size, 4 * size,
    )
    half_back = across_chips(tiles_back).reshape(half_state)
    arriving_own, arriving_send, normed, grad_query, grad_key_near, grad_value_near = call(
        leave_kernel,
        [half_tile, half_tile] + near_outs,
        [on_core] + vmem(half_back, back_keep, back_got, kept, got) + near_args + like(near_outs, near_done),
        12 * whole * rows, 16 * whole, scratch=outputs, aliases={18 + i: 2 + i for i in range(4)},
    )
    arriving_other = swap(arriving_send)
    far_outs = [("h", wide, BF16), ("h", wide, BF16)]
    far_args = vmem(grad_key_near, grad_value_near, key_decayed, v)
    far_done = call(
        far_own_kernel, far_outs, [on_core] + far_args + vmem(arriving_own, inside),
        2 * whole * HEAD, 8 * whole, scratch=outputs,
    )
    grad_key, grad_value = call(
        far_other_kernel, far_outs,
        [on_core] + far_args + vmem(arriving_other, inside) + like(far_outs, far_done),
        2 * whole * HEAD, 8 * whole, scratch=outputs, aliases={7: 0, 8: 1},
    )
    return normed, grad_query, grad_key, grad_value


def solution(mesh):
    seq, tp = mesh.shape["seq"], mesh.shape["tp"]
    fine = Mesh(mesh.devices.reshape(seq // 16, 8, 2, tp), ("x", "y", "core", "tp"))
    spec = P(("x", "y", "core"), "tp")
    return jax.shard_map(
        functools.partial(body, seq // 2, tp),
        mesh=fine,
        in_specs=(spec, spec, spec, spec, P("tp"), spec),
        out_specs=(spec, spec, spec, spec),
        check_vma=False,
    )
```

```python
import functools

import jax
import jax.numpy as jnp
from jax import lax
from jax.experimental import pallas as pl
from jax.experimental.pallas import tpu as pltpu
from jax.sharding import Mesh
from jax.sharding import PartitionSpec as P

HEAD_COUNT = 64
HEAD = 128
EPSILON = 1e-06
HIGH = lax.Precision.HIGHEST
F32 = jnp.float32
BF16 = jnp.bfloat16
VMEM_LIMIT = 20 * 1024 * 1024
NN = (((1,), (0,)), ((), ()))
NT = (((1,), (1,)), ((), ()))
TN = (((0,), (0,)), ((), ()))


def dot(a, b, dims, precision=None):
    return lax.dot_general(a, b, dims, precision=precision, preferred_element_type=F32)


SPACES = {"s": pltpu.SMEM, "h": pltpu.HBM, "v": pltpu.VMEM, "a": pl.ANY}


def call(kernel, outs, args, flops, bytes_accessed, scratch=(), aliases=()):
    return pl.pallas_call(
        kernel,
        out_shape=[SPACES[m](s, d) for m, s, d in outs],
        in_specs=[pl.BlockSpec(memory_space=SPACES[m]) for m, _ in args],
        out_specs=[pl.BlockSpec(memory_space=SPACES[m]) for m, _, _ in outs],
        scratch_shapes=list(scratch),
        input_output_aliases=dict(aliases),
        compiler_params=pltpu.CompilerParams(vmem_limit_bytes=VMEM_LIMIT),
        cost_estimate=pl.CostEstimate(
            flops=flops, bytes_accessed=bytes_accessed, transcendentals=0
        ),
    )(*[pltpu.with_memory_space_constraint(a, SPACES[m]) if m in "hv" else a for m, a in args])


def head_cols(h):
    return slice(h * HEAD, (h + 1) * HEAD)


def head_rows(h):
    return slice(h * HEAD, (h + 1) * HEAD)


def half_of_heads(core, half, sent, state_of, out_ref):
    for place in range(2):

        @pl.when(core == place)
        def _(first=(place ^ sent) * half):
            for i in range(half):
                out_ref[head_rows(i), :] = state_of(first + i)


def local_kernel(
    core_ref, q_hbm, k_hbm, v_hbm, g_hbm, decay_hbm, gain_hbm,
    send_ref, kept_ref, inside_ref, across_ref, q_ref, k_ref, v_ref, g_ref, gain_ref, decay_ref, sems,
):
    heads, rows = decay_ref.shape
    pieces = [
        (decay_hbm, decay_ref), (k_hbm, k_ref), (v_hbm, v_ref), (q_hbm, q_ref), (g_hbm, g_ref), (gain_hbm, gain_ref)
    ]
    copies = [pltpu.make_async_copy(*piece, sems.at[i]) for i, piece in enumerate(pieces)]
    for copy in copies:
        copy.start()
    first = lax.broadcasted_iota(jnp.int32, (rows, rows), 0)
    second = lax.broadcasted_iota(jnp.int32, (rows, rows), 1)
    copies[0].wait()
    decay = decay_ref[...]
    high = decay.astype(BF16)
    rest = decay - high.astype(F32)
    middle = rest.astype(BF16)
    low = (rest - middle.astype(F32)).astype(BF16)
    terms = jnp.concatenate([high, middle, low], axis=0)
    sums = dot(terms, (first <= second).astype(BF16), NN)
    across = sums[:heads] + (sums[heads : 2 * heads] + sums[2 * heads :])
    sums = dot((first >= second).astype(BF16), terms, NT)
    inside = sums[:, :heads] + (sums[:, heads : 2 * heads] + sums[:, 2 * heads :])
    inside_ref[...] = inside
    across_ref[...] = across
    shares = jnp.exp(inside[rows - 1 : rows, :] - inside)
    kept = jnp.broadcast_to(jnp.exp(across[:, rows - 1 : rows]), (heads, HEAD))
    kept_ref[...] = kept
    send_ref[heads // 2 * HEAD :, :] = kept
    copies[1].wait()
    copies[2].wait()

    def state_of(h):
        cols = head_cols(h)
        key_decayed = (k_ref[:, cols].astype(F32) * shares[:, h : h + 1]).astype(BF16)
        return dot(key_decayed, v_ref[:, cols], TN)

    half_of_heads(core_ref[0], heads // 2, 1, state_of, send_ref)
    for copy in copies[3:]:
        copy.wait()


def local_keep_kernel(core_ref, k_ref, v_ref, inside_ref, keep_ref, key_ref):
    rows, heads = inside_ref.shape
    inside = inside_ref[...]
    shares = jnp.exp(inside[rows - 1 : rows, :] - inside)
    for h in range(heads):
        cols = head_cols(h)
        key_ref[:, cols] = (k_ref[:, cols].astype(F32) * shares[:, h : h + 1]).astype(BF16)

    def state_of(h):
        return dot(key_ref[:, head_cols(h)], v_ref[:, head_cols(h)], TN)

    half_of_heads(core_ref[0], heads // 2, 0, state_of, keep_ref)


def kept_rows(core, own_ref, got_ref, i):
    half = got_ref.shape[0] // (HEAD + 2)
    at = got_ref.shape[0] - 2 * half
    own = jnp.where(core == 0, own_ref[i : i + 1, :], own_ref[half + i : half + i + 1, :])
    got = jnp.where(core == 0, got_ref[at + i : at + i + 1, :], got_ref[at + half + i : at + half + i + 1, :])
    return jnp.where(core == 0, own, got), jnp.where(core == 0, got, own)


def in_order(core, own, got):
    return jnp.where(core == 0, own, got), jnp.where(core == 0, got, own)


def forward_join_kernel(core_ref, after_ref, keep_ref, got_ref, kept_ref, pay_ref):
    core = core_ref[0]
    for i in range(keep_ref.shape[0] // HEAD):
        first, second = in_order(core, keep_ref[head_rows(i), :], got_ref[head_rows(i), :])
        kept_first, kept_second = kept_rows(core, kept_ref, got_ref, i)
        joined = kept_second * first + second
        for part in range(8):
            at = 17 * (8 * i + part)
            pay_ref[at : at + 16, :] = joined[16 * part : 16 * part + 16]
            pay_ref[at + 16 : at + 17, :] = kept_first * kept_second


def forward_scan_kernel(got_ref, out_ref, kept_ref):
    count = out_ref.shape[0]
    state = jnp.zeros(out_ref.shape[1:], F32)
    for j in range(count):
        out_ref[j] = state
        kept = got_ref[17 * j + 16 : 17 * j + 17, :]
        kept_ref[j : j + 1, :] = kept
        state = kept * state + got_ref[17 * j : 17 * j + 16, :]


def reverse_join_kernel(core_ref, after_ref, keep_ref, got_ref, kept_ref, got_kept_ref, out_ref):
    core = core_ref[0]
    for i in range(keep_ref.shape[0] // HEAD):
        first, second = in_order(core, keep_ref[head_rows(i), :], got_ref[head_rows(i), :])
        kept_first, _ = kept_rows(core, kept_ref, got_kept_ref, i)
        out_ref[head_rows(i), :] = first + kept_first * second


def reverse_scan_kernel(got_ref, kept_ref, out_ref):
    count = out_ref.shape[0]
    state = jnp.zeros(out_ref.shape[1:], F32)
    for j in reversed(range(count)):
        out_ref[j] = state
        state = kept_ref[j : j + 1, :] * state + got_ref[j]


def weights_of(inside_ref, across_ref, h, transposed=False):
    rows = inside_ref.shape[0]
    first = lax.broadcasted_iota(jnp.int32, (rows, rows), 0)
    second = lax.broadcasted_iota(jnp.int32, (rows, rows), 1)
    if transposed:
        spread = across_ref[h : h + 1, :] - inside_ref[:, h : h + 1]
        return jnp.exp(jnp.where(second >= first, spread, -1e30))
    spread = inside_ref[:, h : h + 1] - across_ref[h : h + 1, :]
    return jnp.exp(jnp.where(first >= second, spread, -1e30))


def mixing_of(
    q_ref, k_ref, v_ref, g_ref, gain_ref, inside_ref, across_ref,
    near_ref, mix_turned_ref, query_ref, query_turned_ref, weights_ref, weights_turned_ref, scaled_ref,
):
    grown = jnp.exp(inside_ref[...])
    for h in range(inside_ref.shape[1]):
        cols = head_cols(h)
        queries, keys = q_ref[:, cols], k_ref[:, cols]
        weights = weights_of(inside_ref, across_ref, h)
        weights_ref[h] = weights
        mixing = (dot(queries, keys, NT) * weights).astype(BF16)
        near_ref[:, cols] = dot(mixing, v_ref[:, cols], NN)
        weights_turned = weights_of(inside_ref, across_ref, h, True)
        weights_turned_ref[h] = weights_turned
        mix_turned_ref[h] = (dot(keys, queries, NT) * weights_turned).astype(BF16)
        decayed = queries.astype(F32) * grown[:, h : h + 1]
        query_ref[:, cols] = decayed.astype(BF16)
        query_turned_ref[h] = decayed.T.astype(BF16)
        scaled_ref[:, cols] = g_ref[:, cols].astype(F32) * gain_ref[:, cols]


def mixing_first_kernel(core_ref, after_ref, *refs):
    @pl.when(core_ref[0] == 0)
    def _():
        mixing_of(*refs)


def enter_kernel(core_ref, half_ref, keep_ref, got_ref, kept_ref, *refs):
    inputs, (own_ref, send_ref, *outputs) = refs[:7], refs[14:]
    core = core_ref[0]
    for i in range(half_ref.shape[0]):
        kept_first, _ = kept_rows(core, kept_ref, got_ref, i)
        first, _ = in_order(core, keep_ref[head_rows(i), :], got_ref[head_rows(i), :])
        state = half_ref[i]
        later = kept_first * state + first
        own_ref[i] = jnp.where(core == 0, state, later)
        send_ref[i] = jnp.where(core == 0, later, state)

    @pl.when(core == 1)
    def _():
        mixing_of(*inputs, *outputs)


def attend_half(base, near_ref, query_ref, half_ref, scaled_ref, att_ref, entering_ref, squares, crossed):
    for i in range(half_ref.shape[0]):
        h = base + i
        cols = pl.ds(pl.multiple_of(h * HEAD, HEAD), HEAD)
        state = half_ref[i].astype(BF16)
        entering_ref[h] = state
        attended = near_ref[:, cols] + dot(query_ref[:, cols], state, NN)
        att_ref[:, cols] = attended
        squares += attended * attended
        crossed += scaled_ref[:, cols] * attended
    return squares, crossed


def attend_own_kernel(
    core_ref, near_ref, query_ref, half_ref, scaled_ref, att_ref, entering_ref, squares_ref, crossed_ref
):
    zero = jnp.zeros(squares_ref.shape, F32)
    squares_ref[...], crossed_ref[...] = attend_half(
        core_ref[0] * half_ref.shape[0], near_ref, query_ref, half_ref, scaled_ref, att_ref, entering_ref, zero, zero
    )


def attend_other_kernel(
    core_ref, near_ref, query_ref, half_ref, scaled_ref, squares_ref, crossed_ref,
    att_in_ref, entering_in_ref, att_ref, entering_ref, sums_ref,
):
    squares, crossed = attend_half(
        (1 - core_ref[0]) * half_ref.shape[0], near_ref, query_ref, half_ref, scaled_ref, att_ref, entering_ref,
        squares_ref[...], crossed_ref[...],
    )
    sums = jnp.concatenate(
        [jnp.sum(squares, axis=1, keepdims=True), jnp.sum(crossed, axis=1, keepdims=True)], axis=1
    ).T
    for peer in range(sums_ref.shape[0]):
        sums_ref[peer] = sums


def norm_columns(sums_ref, rows):
    whole = jnp.sum(sums_ref[...], axis=0)
    first = lax.broadcasted_iota(jnp.int32, (rows, rows), 0)
    second = lax.broadcasted_iota(jnp.int32, (rows, rows), 1)
    same = first == second
    square_sum = jnp.sum(jnp.where(same, whole[0:1, :], 0.0), axis=1, keepdims=True)
    cross_sum = jnp.sum(jnp.where(same, whole[1:2, :], 0.0), axis=1, keepdims=True)
    width = HEAD_COUNT * HEAD
    inverse = lax.rsqrt(square_sum / width + EPSILON)
    return inverse, inverse * inverse * inverse * (cross_sum / width)


def norm_grad_kernel(core_ref, sums_ref, att_ref, scaled_ref, query_turned_ref, send_ref, columns_ref):
    rows, width = att_ref.shape
    inverse, factor = norm_columns(sums_ref, rows)
    columns_ref[...] = jnp.concatenate([inverse, factor], axis=1)

    def state_of(h):
        cols = head_cols(h)
        grad_flat = (inverse * scaled_ref[:, cols] - att_ref[:, cols] * factor).astype(BF16)
        return dot(query_turned_ref[h], grad_flat, NN)

    half_of_heads(core_ref[0], width // HEAD // 2, 1, state_of, send_ref)


def norm_grad_keep_kernel(core_ref, columns_ref, att_ref, scaled_ref, query_turned_ref, keep_ref, gf_ref):
    width = att_ref.shape[1]
    inverse, factor = columns_ref[:, 0:1], columns_ref[:, 1:2]
    for h in range(width // HEAD):
        cols = head_cols(h)
        gf_ref[:, cols] = (inverse * scaled_ref[:, cols] - att_ref[:, cols] * factor).astype(BF16)

    def state_of(h):
        return dot(query_turned_ref[h], gf_ref[:, head_cols(h)], NN)

    half_of_heads(core_ref[0], width // HEAD // 2, 0, state_of, keep_ref)


def send_out(copies, source, target, sems, i, cols):
    copy = pltpu.make_async_copy(source.at[:, cols], target.at[:, cols], sems.at[i])
    copy.start()
    copies.append(copy)


def near_grad(
    columns_ref, att_ref, gain_ref, gf_ref, q_ref, k_ref, v_ref, state_ref, inside_ref, weights_ref,
    weights_turned_ref, mix_turned_ref, normed_hbm, gq_hbm, gk_ref, gv_ref, normed_ref, gq_ref, sems,
):
    rows, heads = inside_ref.shape
    inverse = columns_ref[:, 0:1]
    grown = jnp.exp(inside_ref[...])
    copies = []
    for h in range(heads):
        cols = head_cols(h)
        normed_ref[:, cols] = (att_ref[:, cols] * inverse * gain_ref[:, cols]).astype(BF16)
        grad_flat = gf_ref[:, cols]
        grad_mix = (dot(grad_flat, v_ref[:, cols], NT) * weights_ref[h]).astype(BF16)
        far = dot(grad_flat, state_ref[h], NT)
        gq_ref[:, cols] = (dot(grad_mix, k_ref[:, cols], NN) + grown[:, h : h + 1] * far).astype(BF16)
        if h % 2:
            pair = slice((h - 1) * HEAD, (h + 1) * HEAD)
            send_out(copies, normed_ref, normed_hbm, sems, h - 1, pair)
            send_out(copies, gq_ref, gq_hbm, sems, h, pair)
    for h in range(heads):
        cols = head_cols(h)
        grad_flat = gf_ref[:, cols]
        turned = (dot(v_ref[:, cols], grad_flat, NT) * weights_turned_ref[h]).astype(BF16)
        gk_ref[:, cols] = dot(turned, q_ref[:, cols], NN)
        gv_ref[:, cols] = dot(mix_turned_ref[h], grad_flat, NN)
    for copy in copies:
        copy.wait()


def near_first_kernel(core_ref, *refs):
    @pl.when(core_ref[0] == 0)
    def _():
        near_grad(*refs)


def leave_kernel(core_ref, half_ref, keep_ref, got_ref, kept_ref, got_kept_ref, *refs):
    inputs, (own_ref, send_ref, *outputs) = refs[:12], refs[16:]
    core = core_ref[0]
    for i in range(half_ref.shape[0]):
        _, kept_second = kept_rows(core, kept_ref, got_kept_ref, i)
        _, second = in_order(core, keep_ref[head_rows(i), :], got_ref[head_rows(i), :])
        state = half_ref[i]
        earlier = second + kept_second * state
        own_ref[i] = jnp.where(core == 0, earlier, state)
        send_ref[i] = jnp.where(core == 0, state, earlier)

    @pl.when(core == 1)
    def _():
        near_grad(*inputs, *outputs)


def far_half(
    base, gk_near_ref, gv_near_ref, key_ref, v_ref, half_ref, inside_ref, gk_hbm, gv_hbm, gk_ref, gv_ref, sems
):
    rows, heads = inside_ref.shape
    inside = inside_ref[...]
    shares = jnp.exp(inside[rows - 1 : rows, :] - inside)
    head = lax.broadcasted_iota(jnp.int32, (rows, heads), 1)
    copies = []
    for i in range(half_ref.shape[0]):
        cols = pl.ds(pl.multiple_of((base + i) * HEAD, HEAD), HEAD)
        share = jnp.sum(jnp.where(head == base + i, shares, 0.0), axis=1, keepdims=True)
        arriving = half_ref[i].astype(BF16)
        far = dot(v_ref[:, cols], arriving, NT)
        gk_ref[:, cols] = (gk_near_ref[:, cols] + share * far).astype(BF16)
        gv_ref[:, cols] = (gv_near_ref[:, cols] + dot(key_ref[:, cols], arriving, NN)).astype(BF16)
        if i % 2:
            pair = pl.ds(pl.multiple_of((base + i - 1) * HEAD, 2 * HEAD), 2 * HEAD)
            send_out(copies, gk_ref, gk_hbm, sems, i - 1, pair)
            send_out(copies, gv_ref, gv_hbm, sems, i, pair)
    for copy in copies:
        copy.wait()


def far_own_kernel(core_ref, gk_near_ref, gv_near_ref, key_ref, v_ref, half_ref, inside_ref, *refs):
    base = core_ref[0] * half_ref.shape[0]
    far_half(base, gk_near_ref, gv_near_ref, key_ref, v_ref, half_ref, inside_ref, *refs)


def far_other_kernel(core_ref, gk_near_ref, gv_near_ref, key_ref, v_ref, half_ref, inside_ref, gk_in, gv_in, *refs):
    base = (1 - core_ref[0]) * half_ref.shape[0]
    far_half(base, gk_near_ref, gv_near_ref, key_ref, v_ref, half_ref, inside_ref, *refs)


def body(chips, tp_size, queries, key_vectors, values, decay_log, norm_gain, grad_out):
    rows, width = queries.shape
    heads = decay_log.shape[1]
    half = heads // 2
    slab = half * HEAD // chips
    core = lax.axis_index("core").astype(jnp.int32).reshape(1)
    gain = norm_gain.reshape(1, width)
    wide, tile, half_state = (rows, width), (chips, slab, HEAD), (half, HEAD, HEAD)
    whole, size = rows * width, heads * HEAD * HEAD

    def across_chips(array):
        return lax.all_to_all(array, ("x", "y"), 0, 0)

    def swap(array):
        return lax.ppermute(array, "core", [(0, 1), (1, 0)])

    wide_bf, wide_f32 = ("v", wide, BF16), ("v", wide, F32)
    square, per_token = (heads, rows, rows), ("v", (rows, heads), F32)
    half_rows, half_tile = ("v", (half * HEAD, HEAD), F32), ("v", half_state, F32)
    on_core = ("s", core)

    def vmem(*arrays):
        return [("v", a) for a in arrays]

    def like(outs, arrays):
        return [(m, a) for (m, _, _), a in zip(outs, arrays)]

    inputs = [queries, key_vectors, values, grad_out, decay_log.T, gain]
    send, kept, inside, across, q, k, v, g, gain = call(
        local_kernel,
        [
            ("v", (half * HEAD + heads, HEAD), F32), ("v", (heads, HEAD), F32), per_token,
            ("v", (heads, rows), F32), wide_bf, wide_bf, wide_bf, wide_bf, ("v", (1, width), F32),
        ],
        [on_core] + [("h", a) for a in inputs],
        2 * whole * HEAD, 8 * whole,
        scratch=[pltpu.VMEM((heads, rows), F32), pltpu.SemaphoreType.DMA((6,))],
    )
    got = swap(send)
    keep, key_decayed = call(
        local_keep_kernel, [half_rows, wide_bf], [on_core] + vmem(k, v, inside), whole * HEAD, 4 * whole
    )
    mixing_args = vmem(q, k, v, g, gain, inside, across)
    mixing_outs = [
        wide_f32, ("v", square, BF16), wide_bf, ("v", (heads, HEAD, rows), BF16), ("v", square, F32),
        ("v", square, F32), wide_f32,
    ]
    mixing_done = call(mixing_first_kernel, mixing_outs, [on_core, ("a", keep)] + mixing_args, 6 * whole * rows, 12 * whole)
    (pay,) = call(
        forward_join_kernel,
        [("v", (chips * (slab + 1), HEAD), F32)],
        [on_core, ("a", mixing_done[0])] + vmem(keep, got, kept),
        2 * size, 12 * size,
    )
    pay = across_chips(pay.reshape(chips, 1, (slab + 1) * HEAD)).reshape(chips * (slab + 1), HEAD)
    tiles, kept_chips = call(
        forward_scan_kernel,
        [("v", tile, F32), ("v", (chips, HEAD), F32)],
        vmem(pay),
        size, 4 * size,
    )
    half_in = across_chips(tiles).reshape(half_state)
    half_own, half_send, near, mixing_turned, query_decayed, query_turned, weights, weights_turned, scaled = call(
        enter_kernel,
        [half_tile, half_tile] + mixing_outs,
        [on_core] + vmem(half_in, keep, got, kept) + mixing_args + like(mixing_outs, mixing_done),
        6 * whole * rows, 12 * whole, aliases={12 + i: 2 + i for i in range(7)},
    )
    half_other = swap(half_send)
    entering_bf, column = ("v", (heads, HEAD, HEAD), BF16), ("v", (rows, HEAD), F32)
    attended, entering, squares, crossed = call(
        attend_own_kernel,
        [wide_f32, entering_bf, column, column],
        [on_core] + vmem(near, query_decayed, half_own, scaled),
        whole * HEAD, 6 * whole,
    )
    attended, entering, sums = call(
        attend_other_kernel,
        [wide_f32, entering_bf, ("v", (tp_size, 2, rows), F32)],
        [on_core] + vmem(near, query_decayed, half_other, scaled, squares, crossed, attended, entering),
        whole * HEAD, 6 * whole, aliases={7: 0, 8: 1},
    )
    sums = lax.all_to_all(sums, "tp", 0, 0)
    back_send, columns = call(
        norm_grad_kernel,
        [half_rows, ("v", (rows, 2), F32)],
        [on_core] + vmem(sums, attended, scaled, query_turned),
        whole * HEAD, 6 * whole,
    )
    back_got = swap(back_send)
    back_keep, grad_flat = call(
        norm_grad_keep_kernel,
        [half_rows, wide_bf],
        [on_core] + vmem(columns, attended, scaled, query_turned),
        whole * HEAD, 6 * whole,
    )
    near_args = vmem(
        columns, attended, gain, grad_flat, q, k, v, entering, inside, weights, weights_turned, mixing_turned
    )
    near_outs = [("h", wide, BF16), ("h", wide, BF16), wide_f32, wide_f32]
    outputs = [pltpu.VMEM(wide, BF16), pltpu.VMEM(wide, BF16), pltpu.SemaphoreType.DMA((heads,))]
    near_done = call(
        near_first_kernel, near_outs, [on_core] + near_args, 12 * whole * rows, 16 * whole, scratch=outputs
    )
    (pay_back,) = call(
        reverse_join_kernel,
        [half_rows],
        [on_core, ("a", near_done[2])] + vmem(back_keep, back_got, kept, got),
        2 * size, 12 * size,
    )
    (tiles_back,) = call(
        reverse_scan_kernel,
        [("v", tile, F32)],
        vmem(across_chips(pay_back.reshape(tile)), kept_chips),
        size, 4 * size,
    )
    half_back = across_chips(tiles_back).reshape(half_state)
    arriving_own, arriving_send, normed, grad_query, grad_key_near, grad_value_near = call(
        leave_kernel,
        [half_tile, half_tile] + near_outs,
        [on_core] + vmem(half_back, back_keep, back_got, kept, got) + near_args + like(near_outs, near_done),
        12 * whole * rows, 16 * whole, scratch=outputs, aliases={18 + i: 2 + i for i in range(4)},
    )
    arriving_other = swap(arriving_send)
    far_outs = [("h", wide, BF16), ("h", wide, BF16)]
    far_args = vmem(grad_key_near, grad_value_near, key_decayed, v)
    far_done = call(
        far_own_kernel, far_outs, [on_core] + far_args + vmem(arriving_own, inside),
        2 * whole * HEAD, 8 * whole, scratch=outputs,
    )
    grad_key, grad_value = call(
        far_other_kernel, far_outs,
        [on_core] + far_args + vmem(arriving_other, inside) + like(far_outs, far_done),
        2 * whole * HEAD, 8 * whole, scratch=outputs, aliases={7: 0, 8: 1},
    )
    return normed, grad_query, grad_key, grad_value


def solution(mesh):
    seq, tp = mesh.shape["seq"], mesh.shape["tp"]
    fine = Mesh(mesh.devices.reshape(seq // 16, 8, 2, tp), ("x", "y", "core", "tp"))
    spec = P(("x", "y", "core"), "tp")
    return jax.shard_map(
        functools.partial(body, seq // 2, tp),
        mesh=fine,
        in_specs=(spec, spec, spec, spec, P("tp"), spec),
        out_specs=(spec, spec, spec, spec),
        check_vma=False,
    )
```

```python
import functools

import jax
import jax.numpy as jnp
from jax import lax
from jax.experimental import pallas as pl
from jax.experimental.pallas import tpu as pltpu
from jax.sharding import Mesh
from jax.sharding import PartitionSpec as P

HEAD_COUNT = 64
HEAD = 128
EPSILON = 1e-06
HIGH = lax.Precision.HIGHEST
F32 = jnp.float32
BF16 = jnp.bfloat16
VMEM_LIMIT = 20 * 1024 * 1024
NN = (((1,), (0,)), ((), ()))
NT = (((1,), (1,)), ((), ()))
TN = (((0,), (0,)), ((), ()))


def dot(a, b, dims, precision=None):
    return lax.dot_general(a, b, dims, precision=precision, preferred_element_type=F32)


SPACES = {"s": pltpu.SMEM, "h": pltpu.HBM, "v": pltpu.VMEM, "a": pl.ANY}


def call(kernel, outs, args, flops, bytes_accessed, scratch=(), aliases=()):
    return pl.pallas_call(
        kernel,
        out_shape=[SPACES[m](s, d) for m, s, d in outs],
        in_specs=[pl.BlockSpec(memory_space=SPACES[m]) for m, _ in args],
        out_specs=[pl.BlockSpec(memory_space=SPACES[m]) for m, _, _ in outs],
        scratch_shapes=list(scratch),
        input_output_aliases=dict(aliases),
        compiler_params=pltpu.CompilerParams(vmem_limit_bytes=VMEM_LIMIT),
        cost_estimate=pl.CostEstimate(
            flops=flops, bytes_accessed=bytes_accessed, transcendentals=0
        ),
    )(*[pltpu.with_memory_space_constraint(a, SPACES[m]) if m in "hv" else a for m, a in args])


def head_cols(h):
    return slice(h * HEAD, (h + 1) * HEAD)


def head_rows(h):
    return slice(h * HEAD, (h + 1) * HEAD)


def half_of_heads(core, half, sent, state_of, out_ref):
    for place in range(2):

        @pl.when(core == place)
        def _(first=(place ^ sent) * half):
            for i in range(half):
                out_ref[head_rows(i), :] = state_of(first + i)


def local_kernel(
    core_ref, q_hbm, k_hbm, v_hbm, g_hbm, decay_hbm, gain_hbm,
    send_ref, kept_ref, inside_ref, across_ref, q_ref, k_ref, v_ref, g_ref, gain_ref, decay_ref, sems,
):
    heads, rows = decay_ref.shape
    pieces = [
        (decay_hbm, decay_ref), (k_hbm, k_ref), (v_hbm, v_ref), (q_hbm, q_ref), (g_hbm, g_ref), (gain_hbm, gain_ref)
    ]
    copies = [pltpu.make_async_copy(*piece, sems.at[i]) for i, piece in enumerate(pieces)]
    for copy in copies:
        copy.start()
    first = lax.broadcasted_iota(jnp.int32, (rows, rows), 0)
    second = lax.broadcasted_iota(jnp.int32, (rows, rows), 1)
    copies[0].wait()
    decay = decay_ref[...]
    high = decay.astype(BF16)
    rest = decay - high.astype(F32)
    middle = rest.astype(BF16)
    low = (rest - middle.astype(F32)).astype(BF16)
    terms = jnp.concatenate([high, middle, low], axis=0)
    sums = dot(terms, (first <= second).astype(BF16), NN)
    across = sums[:heads] + (sums[heads : 2 * heads] + sums[2 * heads :])
    sums = dot((first >= second).astype(BF16), terms, NT)
    inside = sums[:, :heads] + (sums[:, heads : 2 * heads] + sums[:, 2 * heads :])
    inside_ref[...] = inside
    across_ref[...] = across
    shares = jnp.exp(inside[rows - 1 : rows, :] - inside)
    kept = jnp.broadcast_to(jnp.exp(across[:, rows - 1 : rows]), (heads, HEAD))
    kept_ref[...] = kept
    send_ref[heads // 2 * HEAD :, :] = kept
    copies[1].wait()
    copies[2].wait()

    def state_of(h):
        cols = head_cols(h)
        key_decayed = (k_ref[:, cols].astype(F32) * shares[:, h : h + 1]).astype(BF16)
        return dot(key_decayed, v_ref[:, cols], TN)

    half_of_heads(core_ref[0], heads // 2, 1, state_of, send_ref)
    for copy in copies[3:]:
        copy.wait()


def local_keep_kernel(core_ref, k_ref, v_ref, inside_ref, keep_ref, key_ref):
    rows, heads = inside_ref.shape
    inside = inside_ref[...]
    shares = jnp.exp(inside[rows - 1 : rows, :] - inside)
    for h in range(heads):
        cols = head_cols(h)
        key_ref[:, cols] = (k_ref[:, cols].astype(F32) * shares[:, h : h + 1]).astype(BF16)

    def state_of(h):
        return dot(key_ref[:, head_cols(h)], v_ref[:, head_cols(h)], TN)

    half_of_heads(core_ref[0], heads // 2, 0, state_of, keep_ref)


def kept_rows(core, own_ref, got_ref, i):
    half = got_ref.shape[0] // (HEAD + 2)
    at = got_ref.shape[0] - 2 * half
    own = jnp.where(core == 0, own_ref[i : i + 1, :], own_ref[half + i : half + i + 1, :])
    got = jnp.where(core == 0, got_ref[at + i : at + i + 1, :], got_ref[at + half + i : at + half + i + 1, :])
    return jnp.where(core == 0, own, got), jnp.where(core == 0, got, own)


def in_order(core, own, got):
    return jnp.where(core == 0, own, got), jnp.where(core == 0, got, own)


def forward_join_kernel(core_ref, after_ref, keep_ref, got_ref, kept_ref, pay_ref):
    core = core_ref[0]
    for i in range(keep_ref.shape[0] // HEAD):
        first, second = in_order(core, keep_ref[head_rows(i), :], got_ref[head_rows(i), :])
        kept_first, kept_second = kept_rows(core, kept_ref, got_ref, i)
        joined = kept_second * first + second
        for part in range(8):
            at = 17 * (8 * i + part)
            pay_ref[at : at + 16, :] = joined[16 * part : 16 * part + 16]
            pay_ref[at + 16 : at + 17, :] = kept_first * kept_second


def chips_in_order(count):
    return [y * (count // 8) + x for x in range(count // 8) for y in range(8)]


def forward_scan_kernel(got_ref, out_ref, kept_ref):
    count = out_ref.shape[0]
    state = jnp.zeros(out_ref.shape[1:], F32)
    for j in chips_in_order(count):
        out_ref[j] = state
        kept = got_ref[17 * j + 16 : 17 * j + 17, :]
        kept_ref[j : j + 1, :] = kept
        state = kept * state + got_ref[17 * j : 17 * j + 16, :]


def reverse_join_kernel(core_ref, after_ref, keep_ref, got_ref, kept_ref, got_kept_ref, out_ref):
    core = core_ref[0]
    for i in range(keep_ref.shape[0] // HEAD):
        first, second = in_order(core, keep_ref[head_rows(i), :], got_ref[head_rows(i), :])
        kept_first, _ = kept_rows(core, kept_ref, got_kept_ref, i)
        out_ref[head_rows(i), :] = first + kept_first * second


def reverse_scan_kernel(got_ref, kept_ref, out_ref):
    count = out_ref.shape[0]
    state = jnp.zeros(out_ref.shape[1:], F32)
    for j in reversed(chips_in_order(count)):
        out_ref[j] = state
        state = kept_ref[j : j + 1, :] * state + got_ref[j]


def weights_of(inside_ref, across_ref, h, transposed=False):
    rows = inside_ref.shape[0]
    first = lax.broadcasted_iota(jnp.int32, (rows, rows), 0)
    second = lax.broadcasted_iota(jnp.int32, (rows, rows), 1)
    if transposed:
        spread = across_ref[h : h + 1, :] - inside_ref[:, h : h + 1]
        return jnp.exp(jnp.where(second >= first, spread, -1e30))
    spread = inside_ref[:, h : h + 1] - across_ref[h : h + 1, :]
    return jnp.exp(jnp.where(first >= second, spread, -1e30))


def mixing_of(
    q_ref, k_ref, v_ref, g_ref, gain_ref, inside_ref, across_ref,
    near_ref, mix_turned_ref, query_ref, query_turned_ref, weights_ref, weights_turned_ref, scaled_ref,
):
    grown = jnp.exp(inside_ref[...])
    for h in range(inside_ref.shape[1]):
        cols = head_cols(h)
        queries, keys = q_ref[:, cols], k_ref[:, cols]
        weights = weights_of(inside_ref, across_ref, h)
        weights_ref[h] = weights
        mixing = (dot(queries, keys, NT) * weights).astype(BF16)
        near_ref[:, cols] = dot(mixing, v_ref[:, cols], NN)
        weights_turned = weights_of(inside_ref, across_ref, h, True)
        weights_turned_ref[h] = weights_turned
        mix_turned_ref[h] = (dot(keys, queries, NT) * weights_turned).astype(BF16)
        decayed = queries.astype(F32) * grown[:, h : h + 1]
        query_ref[:, cols] = decayed.astype(BF16)
        query_turned_ref[h] = decayed.T.astype(BF16)
        scaled_ref[:, cols] = g_ref[:, cols].astype(F32) * gain_ref[:, cols]


def mixing_first_kernel(core_ref, after_ref, *refs):
    @pl.when(core_ref[0] == 0)
    def _():
        mixing_of(*refs)


def enter_kernel(core_ref, half_ref, keep_ref, got_ref, kept_ref, *refs):
    inputs, (own_ref, send_ref, *outputs) = refs[:7], refs[14:]
    core = core_ref[0]
    for i in range(half_ref.shape[0]):
        kept_first, _ = kept_rows(core, kept_ref, got_ref, i)
        first, _ = in_order(core, keep_ref[head_rows(i), :], got_ref[head_rows(i), :])
        state = half_ref[i]
        later = kept_first * state + first
        own_ref[i] = jnp.where(core == 0, state, later)
        send_ref[i] = jnp.where(core == 0, later, state)

    @pl.when(core == 1)
    def _():
        mixing_of(*inputs, *outputs)


def attend_half(base, near_ref, query_ref, half_ref, scaled_ref, att_ref, entering_ref, squares, crossed):
    for i in range(half_ref.shape[0]):
        h = base + i
        cols = pl.ds(pl.multiple_of(h * HEAD, HEAD), HEAD)
        state = half_ref[i].astype(BF16)
        entering_ref[h] = state
        attended = near_ref[:, cols] + dot(query_ref[:, cols], state, NN)
        att_ref[:, cols] = attended
        squares += attended * attended
        crossed += scaled_ref[:, cols] * attended
    return squares, crossed


def attend_own_kernel(
    core_ref, near_ref, query_ref, half_ref, scaled_ref, att_ref, entering_ref, squares_ref, crossed_ref
):
    zero = jnp.zeros(squares_ref.shape, F32)
    squares_ref[...], crossed_ref[...] = attend_half(
        core_ref[0] * half_ref.shape[0], near_ref, query_ref, half_ref, scaled_ref, att_ref, entering_ref, zero, zero
    )


def attend_other_kernel(
    core_ref, near_ref, query_ref, half_ref, scaled_ref, squares_ref, crossed_ref,
    att_in_ref, entering_in_ref, att_ref, entering_ref, sums_ref,
):
    squares, crossed = attend_half(
        (1 - core_ref[0]) * half_ref.shape[0], near_ref, query_ref, half_ref, scaled_ref, att_ref, entering_ref,
        squares_ref[...], crossed_ref[...],
    )
    sums = jnp.concatenate(
        [jnp.sum(squares, axis=1, keepdims=True), jnp.sum(crossed, axis=1, keepdims=True)], axis=1
    ).T
    for peer in range(sums_ref.shape[0]):
        sums_ref[peer] = sums


def norm_columns(sums_ref, rows):
    whole = jnp.sum(sums_ref[...], axis=0)
    first = lax.broadcasted_iota(jnp.int32, (rows, rows), 0)
    second = lax.broadcasted_iota(jnp.int32, (rows, rows), 1)
    same = first == second
    square_sum = jnp.sum(jnp.where(same, whole[0:1, :], 0.0), axis=1, keepdims=True)
    cross_sum = jnp.sum(jnp.where(same, whole[1:2, :], 0.0), axis=1, keepdims=True)
    width = HEAD_COUNT * HEAD
    inverse = lax.rsqrt(square_sum / width + EPSILON)
    return inverse, inverse * inverse * inverse * (cross_sum / width)


def norm_grad_kernel(core_ref, sums_ref, att_ref, scaled_ref, query_turned_ref, send_ref, columns_ref):
    rows, width = att_ref.shape
    inverse, factor = norm_columns(sums_ref, rows)
    columns_ref[...] = jnp.concatenate([inverse, factor], axis=1)

    def state_of(h):
        cols = head_cols(h)
        grad_flat = (inverse * scaled_ref[:, cols] - att_ref[:, cols] * factor).astype(BF16)
        return dot(query_turned_ref[h], grad_flat, NN)

    half_of_heads(core_ref[0], width // HEAD // 2, 1, state_of, send_ref)


def norm_grad_keep_kernel(core_ref, columns_ref, att_ref, scaled_ref, query_turned_ref, keep_ref, gf_ref):
    width = att_ref.shape[1]
    inverse, factor = columns_ref[:, 0:1], columns_ref[:, 1:2]
    for h in range(width // HEAD):
        cols = head_cols(h)
        gf_ref[:, cols] = (inverse * scaled_ref[:, cols] - att_ref[:, cols] * factor).astype(BF16)

    def state_of(h):
        return dot(query_turned_ref[h], gf_ref[:, head_cols(h)], NN)

    half_of_heads(core_ref[0], width // HEAD // 2, 0, state_of, keep_ref)


def send_out(copies, source, target, sems, i, cols):
    copy = pltpu.make_async_copy(source.at[:, cols], target.at[:, cols], sems.at[i])
    copy.start()
    copies.append(copy)


def near_grad(
    columns_ref, att_ref, gain_ref, gf_ref, q_ref, k_ref, v_ref, state_ref, inside_ref, weights_ref,
    weights_turned_ref, mix_turned_ref, normed_hbm, gq_hbm, gk_ref, gv_ref, normed_ref, gq_ref, sems,
):
    rows, heads = inside_ref.shape
    inverse = columns_ref[:, 0:1]
    grown = jnp.exp(inside_ref[...])
    copies = []
    for h in range(heads):
        cols = head_cols(h)
        normed_ref[:, cols] = (att_ref[:, cols] * inverse * gain_ref[:, cols]).astype(BF16)
        grad_flat = gf_ref[:, cols]
        grad_mix = (dot(grad_flat, v_ref[:, cols], NT) * weights_ref[h]).astype(BF16)
        far = dot(grad_flat, state_ref[h], NT)
        gq_ref[:, cols] = (dot(grad_mix, k_ref[:, cols], NN) + grown[:, h : h + 1] * far).astype(BF16)
        if h % 2:
            pair = slice((h - 1) * HEAD, (h + 1) * HEAD)
            send_out(copies, normed_ref, normed_hbm, sems, h - 1, pair)
            send_out(copies, gq_ref, gq_hbm, sems, h, pair)
    for h in range(heads):
        cols = head_cols(h)
        grad_flat = gf_ref[:, cols]
        turned = (dot(v_ref[:, cols], grad_flat, NT) * weights_turned_ref[h]).astype(BF16)
        gk_ref[:, cols] = dot(turned, q_ref[:, cols], NN)
        gv_ref[:, cols] = dot(mix_turned_ref[h], grad_flat, NN)
    for copy in copies:
        copy.wait()


def near_first_kernel(core_ref, *refs):
    @pl.when(core_ref[0] == 0)
    def _():
        near_grad(*refs)


def leave_kernel(core_ref, half_ref, keep_ref, got_ref, kept_ref, got_kept_ref, *refs):
    inputs, (own_ref, send_ref, *outputs) = refs[:12], refs[16:]
    core = core_ref[0]
    for i in range(half_ref.shape[0]):
        _, kept_second = kept_rows(core, kept_ref, got_kept_ref, i)
        _, second = in_order(core, keep_ref[head_rows(i), :], got_ref[head_rows(i), :])
        state = half_ref[i]
        earlier = second + kept_second * state
        own_ref[i] = jnp.where(core == 0, earlier, state)
        send_ref[i] = jnp.where(core == 0, state, earlier)

    @pl.when(core == 1)
    def _():
        near_grad(*inputs, *outputs)


def far_half(
    base, gk_near_ref, gv_near_ref, key_ref, v_ref, half_ref, inside_ref, gk_hbm, gv_hbm, gk_ref, gv_ref, sems
):
    rows, heads = inside_ref.shape
    inside = inside_ref[...]
    shares = jnp.exp(inside[rows - 1 : rows, :] - inside)
    head = lax.broadcasted_iota(jnp.int32, (rows, heads), 1)
    copies = []
    for i in range(half_ref.shape[0]):
        cols = pl.ds(pl.multiple_of((base + i) * HEAD, HEAD), HEAD)
        share = jnp.sum(jnp.where(head == base + i, shares, 0.0), axis=1, keepdims=True)
        arriving = half_ref[i].astype(BF16)
        far = dot(v_ref[:, cols], arriving, NT)
        gk_ref[:, cols] = (gk_near_ref[:, cols] + share * far).astype(BF16)
        gv_ref[:, cols] = (gv_near_ref[:, cols] + dot(key_ref[:, cols], arriving, NN)).astype(BF16)
        if i % 2:
            pair = pl.ds(pl.multiple_of((base + i - 1) * HEAD, 2 * HEAD), 2 * HEAD)
            send_out(copies, gk_ref, gk_hbm, sems, i - 1, pair)
            send_out(copies, gv_ref, gv_hbm, sems, i, pair)
    for copy in copies:
        copy.wait()


def far_own_kernel(core_ref, gk_near_ref, gv_near_ref, key_ref, v_ref, half_ref, inside_ref, *refs):
    base = core_ref[0] * half_ref.shape[0]
    far_half(base, gk_near_ref, gv_near_ref, key_ref, v_ref, half_ref, inside_ref, *refs)


def far_other_kernel(core_ref, gk_near_ref, gv_near_ref, key_ref, v_ref, half_ref, inside_ref, gk_in, gv_in, *refs):
    base = (1 - core_ref[0]) * half_ref.shape[0]
    far_half(base, gk_near_ref, gv_near_ref, key_ref, v_ref, half_ref, inside_ref, *refs)


def body(chips, tp_size, queries, key_vectors, values, decay_log, norm_gain, grad_out):
    rows, width = queries.shape
    heads = decay_log.shape[1]
    half = heads // 2
    slab = half * HEAD // chips
    core = lax.axis_index("core").astype(jnp.int32).reshape(1)
    gain = norm_gain.reshape(1, width)
    wide, tile, half_state = (rows, width), (chips, slab, HEAD), (half, HEAD, HEAD)
    whole, size = rows * width, heads * HEAD * HEAD

    def across_chips(array):
        return lax.all_to_all(array, ("y", "x"), 0, 0)

    def swap(array):
        return lax.ppermute(array, "core", [(0, 1), (1, 0)])

    wide_bf, wide_f32 = ("v", wide, BF16), ("v", wide, F32)
    square, per_token = (heads, rows, rows), ("v", (rows, heads), F32)
    half_rows, half_tile = ("v", (half * HEAD, HEAD), F32), ("v", half_state, F32)
    on_core = ("s", core)

    def vmem(*arrays):
        return [("v", a) for a in arrays]

    def like(outs, arrays):
        return [(m, a) for (m, _, _), a in zip(outs, arrays)]

    inputs = [queries, key_vectors, values, grad_out, decay_log.T, gain]
    send, kept, inside, across, q, k, v, g, gain = call(
        local_kernel,
        [
            ("v", (half * HEAD + heads, HEAD), F32), ("v", (heads, HEAD), F32), per_token,
            ("v", (heads, rows), F32), wide_bf, wide_bf, wide_bf, wide_bf, ("v", (1, width), F32),
        ],
        [on_core] + [("h", a) for a in inputs],
        2 * whole * HEAD, 8 * whole,
        scratch=[pltpu.VMEM((heads, rows), F32), pltpu.SemaphoreType.DMA((6,))],
    )
    got = swap(send)
    keep, key_decayed = call(
        local_keep_kernel, [half_rows, wide_bf], [on_core] + vmem(k, v, inside), whole * HEAD, 4 * whole
    )
    mixing_args = vmem(q, k, v, g, gain, inside, across)
    mixing_outs = [
        wide_f32, ("v", square, BF16), wide_bf, ("v", (heads, HEAD, rows), BF16), ("v", square, F32),
        ("v", square, F32), wide_f32,
    ]
    mixing_done = call(mixing_first_kernel, mixing_outs, [on_core, ("a", got)] + mixing_args, 6 * whole * rows, 12 * whole)
    (pay,) = call(
        forward_join_kernel,
        [("v", (chips * (slab + 1), HEAD), F32)],
        [on_core, ("a", mixing_done[0])] + vmem(keep, got, kept),
        2 * size, 12 * size,
    )
    pay = across_chips(pay.reshape(chips, 1, (slab + 1) * HEAD)).reshape(chips * (slab + 1), HEAD)
    tiles, kept_chips = call(
        forward_scan_kernel,
        [("v", tile, F32), ("v", (chips, HEAD), F32)],
        vmem(pay),
        size, 4 * size,
    )
    half_in = across_chips(tiles).reshape(half_state)
    half_own, half_send, near, mixing_turned, query_decayed, query_turned, weights, weights_turned, scaled = call(
        enter_kernel,
        [half_tile, half_tile] + mixing_outs,
        [on_core] + vmem(half_in, keep, got, kept) + mixing_args + like(mixing_outs, mixing_done),
        6 * whole * rows, 12 * whole, aliases={12 + i: 2 + i for i in range(7)},
    )
    half_other = swap(half_send)
    entering_bf, column = ("v", (heads, HEAD, HEAD), BF16), ("v", (rows, HEAD), F32)
    attended, entering, squares, crossed = call(
        attend_own_kernel,
        [wide_f32, entering_bf, column, column],
        [on_core] + vmem(near, query_decayed, half_own, scaled),
        whole * HEAD, 6 * whole,
    )
    attended, entering, sums = call(
        attend_other_kernel,
        [wide_f32, entering_bf, ("v", (tp_size, 2, rows), F32)],
        [on_core] + vmem(near, query_decayed, half_other, scaled, squares, crossed, attended, entering),
        whole * HEAD, 6 * whole, aliases={7: 0, 8: 1},
    )
    sums = lax.all_to_all(sums, "tp", 0, 0)
    back_send, columns = call(
        norm_grad_kernel,
        [half_rows, ("v", (rows, 2), F32)],
        [on_core] + vmem(sums, attended, scaled, query_turned),
        whole * HEAD, 6 * whole,
    )
    back_got = swap(back_send)
    back_keep, grad_flat = call(
        norm_grad_keep_kernel,
        [half_rows, wide_bf],
        [on_core] + vmem(columns, attended, scaled, query_turned),
        whole * HEAD, 6 * whole,
    )
    near_args = vmem(
        columns, attended, gain, grad_flat, q, k, v, entering, inside, weights, weights_turned, mixing_turned
    )
    near_outs = [("h", wide, BF16), ("h", wide, BF16), wide_f32, wide_f32]
    outputs = [pltpu.VMEM(wide, BF16), pltpu.VMEM(wide, BF16), pltpu.SemaphoreType.DMA((heads,))]
    near_done = call(
        near_first_kernel, near_outs, [on_core] + near_args, 12 * whole * rows, 16 * whole, scratch=outputs
    )
    (pay_back,) = call(
        reverse_join_kernel,
        [half_rows],
        [on_core, ("a", near_done[2])] + vmem(back_keep, back_got, kept, got),
        2 * size, 12 * size,
    )
    (tiles_back,) = call(
        reverse_scan_kernel,
        [("v", tile, F32)],
        vmem(across_chips(pay_back.reshape(tile)), kept_chips),
        size, 4 * size,
    )
    half_back = across_chips(tiles_back).reshape(half_state)
    arriving_own, arriving_send, normed, grad_query, grad_key_near, grad_value_near = call(
        leave_kernel,
        [half_tile, half_tile] + near_outs,
        [on_core] + vmem(half_back, back_keep, back_got, kept, got) + near_args + like(near_outs, near_done),
        12 * whole * rows, 16 * whole, scratch=outputs, aliases={18 + i: 2 + i for i in range(4)},
    )
    arriving_other = swap(arriving_send)
    far_outs = [("h", wide, BF16), ("h", wide, BF16)]
    far_args = vmem(grad_key_near, grad_value_near, key_decayed, v)
    far_done = call(
        far_own_kernel, far_outs, [on_core] + far_args + vmem(arriving_own, inside),
        2 * whole * HEAD, 8 * whole, scratch=outputs,
    )
    grad_key, grad_value = call(
        far_other_kernel, far_outs,
        [on_core] + far_args + vmem(arriving_other, inside) + like(far_outs, far_done),
        2 * whole * HEAD, 8 * whole, scratch=outputs, aliases={7: 0, 8: 1},
    )
    return normed, grad_query, grad_key, grad_value


def solution(mesh):
    seq, tp = mesh.shape["seq"], mesh.shape["tp"]
    fine = Mesh(mesh.devices.reshape(seq // 16, 8, 2, tp), ("x", "y", "core", "tp"))
    spec = P(("x", "y", "core"), "tp")
    return jax.shard_map(
        functools.partial(body, seq // 2, tp),
        mesh=fine,
        in_specs=(spec, spec, spec, spec, P("tp"), spec),
        out_specs=(spec, spec, spec, spec),
        check_vma=False,
    )
```
